512 devices in a mesh: phi: 64 (over y_lo, z, core), layer: 8 (over y_hi, x).
Axes of the slice: x: 4, y: 4 (y_hi: 2, y_lo: 2; y = y_hi * 2 + y_lo), z: 16, core: 2. Of those that a mesh axis runs over, the one named last changes fastest.
Arguments:
- node_feats: bfloat16 [64, 16384], P(None, ('phi', 'layer')), may hold values from -6 to 6
- edge_feats: bfloat16 [64, 1048576], P(None, ('phi', 'layer')), may hold values from -6 to 6
- edge_source: int32 [1048576], P(('phi', 'layer')), may hold values from 0 to 447
- edge_target: int32 [1048576], P(('phi', 'layer')), may hold values from 0 to 255
- edge_counts: int32 [64, 8], P('phi', 'layer'), may hold values from 256 to 2048, as said below
- rim_upper: int32 [64, 96], P('phi'), may hold values from 0 to 255, as said below
- rim_lower: int32 [64, 96], P('phi'), may hold values from 0 to 255, as said below
- edge_first: bfloat16 [64, 192], replicated, may hold values from -0.4375 to 0.4375
- edge_second: bfloat16 [64, 64], replicated, may hold values from -0.75 to 0.75
- node_first: bfloat16 [64, 128], replicated, may hold values from -0.1875 to 0.1875
- node_second: bfloat16 [64, 64], replicated, may hold values from -0.75 to 0.75
- biases: float32 [4, 64], replicated, may hold values from -3 to 3
- node_cot: float32 [64, 16384], P(None, ('phi', 'layer')), may hold values from -0.5 to 0.5
Outputs:
- node_out: bfloat16 [64, 16384], P(None, ('phi', 'layer'))
- edge_out: bfloat16 [64, 1048576], P(None, ('phi', 'layer'))
- node_grad: float32 [64, 16384], P(None, ('phi', 'layer'))
- grad_edge_first: float32 [64, 192], replicated
- grad_edge_second: float32 [64, 64], replicated
- grad_node_first: float32 [64, 128], replicated
- grad_node_second: float32 [64, 64], replicated
- grad_biases: float32 [4, 64], replicated
The draws below stay inside these ranges and needn't reach their ends.
Inputs may be any that keep to these rules, and one draw needn't show every extreme that they name: `edge_source`: columns 0 to 255 are the slab's own hits, the next 96 come from the slab below in phi and the last 96 from the slab above, on a closed loop; slots past the count hold any index. `edge_target`: a hit of the edge's own slab. `edge_counts`: slots of a device at or past this count are padding; some device is full in every draw. `rim_upper`: distinct hits of the slab within each row. `rim_lower`: distinct hits of the slab within each row.
All inputs are finite; a program needn't handle non-finite values.
Results may differ from the reference program's by a relative error of at most 0.02.
Values may be sent and summed in bfloat16 or wider, within the bound.
A program may use at most 64 MiB of HBM per device.

```python
import jax
import jax.numpy as jnp
from jax import lax

F = 64
HID = 64
E_DEV = 2048
ITERS = 2
SLAB = 256
RIM = 96
EXT = 448
NODES = 16384
EDGES = 1048576
N_PHI = 64
N_LAYER = 8


def draw_order(single):
    return jax.random.permutation(single, SLAB).astype(jnp.int32)


def rim_choice(key):
    orders = jax.vmap(draw_order)(jax.random.split(key, N_PHI))
    highest = SLAB - 1
    leading = orders[:, 0:1]
    orders = jnp.where(orders == highest, leading, orders)
    orders = orders.at[:, 0].set(highest)
    second = orders[:, 1:2]
    orders = jnp.where(orders == 0, second, orders)
    orders = orders.at[:, 1].set(0)
    return orders[:, :RIM].astype(jnp.int32)


def draw_rim_upper(key, part):
    key = jax.random.fold_in(key, 21)
    return rim_choice(key)


def draw_rim_lower(key, part):
    key = jax.random.fold_in(key, 22)
    return rim_choice(key)


def draw_edge_counts(key, part):
    key = jax.random.fold_in(key, 11)
    split_one, split_two = jax.random.split(key)
    spread = E_DEV - E_DEV // 8
    drawn = jax.random.randint(split_one, (N_PHI * N_LAYER,), 0, spread + 1)
    counts = E_DEV // 8 + drawn * drawn // spread
    busiest = jax.random.randint(split_two, (), 0, N_PHI * N_LAYER)
    counts = counts.at[busiest].set(E_DEV)
    return counts.reshape(N_PHI, N_LAYER).astype(jnp.int32)


def with_ends(entries, own_key, low, largest):
    index_at = [jax.random.randint(jax.random.fold_in(own_key, axis), (), 0, length) for axis, length in enumerate(entries.shape)]
    main_axis = entries.shape.index(max(entries.shape))
    neighbour = index_at[:main_axis] + [(index_at[main_axis] + 1) % entries.shape[main_axis]] + index_at[main_axis + 1:]
    return entries.at[tuple(index_at)].set(low).at[tuple(neighbour)].set(largest)


def levels(stream_key, dims, pieces, least, high):
    level = 1.0
    for dim, parts in pieces:
        steps = jax.random.uniform(jax.random.fold_in(jax.random.fold_in(stream_key, 6), dim), (parts,), jnp.float32, least / len(pieces), high / len(pieces))
        level = level * jnp.repeat(jnp.exp(steps), dims[dim] // parts).reshape((-1,) + (1,) * (len(dims) - 1 - dim))
    return level


def scatter_about(rng, dims, scale, reach, shards=(), held_as=jnp.bfloat16):
    values = jax.random.normal(rng, dims, jnp.float32) * scale
    if len(shards) > 0:
        values = levels(rng, dims, shards, -0.22, 0.18) * values
    return jnp.clip(values, min=-reach, max=reach).astype(held_as)


def setup_inputs(seed: int = 0) -> dict:
    streams_of = jax.random.split(jax.random.key(seed), 14)
    node_feats = scatter_about(streams_of[0], (F, NODES), 1.0, 6.0, ((1, 512),))
    edge_feats = scatter_about(streams_of[1], (F, EDGES), 1.0, 6.0, ((1, 512),))
    edge_source = with_ends(jax.random.randint(streams_of[2], (EDGES,), 0, EXT), jax.random.fold_in(streams_of[2], 1), 0, EXT - 1).astype(jnp.int32)
    edge_target = with_ends(jax.random.randint(streams_of[3], (EDGES,), 0, SLAB), jax.random.fold_in(streams_of[3], 1), 0, SLAB - 1).astype(jnp.int32)
    edge_counts = draw_edge_counts(jax.random.fold_in(streams_of[13], 71), 0)
    rim_upper = draw_rim_upper(jax.random.fold_in(streams_of[13], 71), 0)
    rim_lower = draw_rim_lower(jax.random.fold_in(streams_of[13], 71), 0)
    edge_first = scatter_about(streams_of[7], (HID, 3 * F), (3 * F) ** -0.5, 0.4375)
    edge_second = scatter_about(streams_of[8], (F, HID), HID ** -0.5, 0.75)
    node_first = scatter_about(streams_of[9], (HID, 2 * F), (16 * F) ** -0.5, 0.1875)
    node_second = scatter_about(streams_of[10], (F, HID), HID ** -0.5, 0.75)
    biases = scatter_about(streams_of[11], (4, HID), 0.5, 3.0, (), jnp.float32)
    node_cot = scatter_about(streams_of[12], (F, NODES), (4 * NODES ** -0.5), 0.5, ((1, 512),), jnp.float32)
    return {"node_feats": node_feats, "edge_feats": edge_feats, "edge_source": edge_source, "edge_target": edge_target, "edge_counts": edge_counts, "rim_upper": rim_upper, "rim_lower": rim_lower, "edge_first": edge_first, "edge_second": edge_second, "node_first": node_first, "node_second": node_second, "biases": biases, "node_cot": node_cot}


def forward_dot(weight, data):
    return jnp.dot(weight, data, preferred_element_type=jnp.float32)


def back_dot(weight, data):
    return lax.dot_general(weight, data, (((0,), (0,)), ((), ())), preferred_element_type=jnp.float32)


def outer_dot(left, right):
    return lax.dot_general(left, right, (((1,), (1,)), ((), ())), preferred_element_type=jnp.float32)


def silu_slope(value):
    logistic = jax.nn.sigmoid(value)
    return logistic * (1.0 + value * (1.0 - logistic))


def pick_columns(table, index):
    return jnp.take(table, index, axis=1)


def place_rims(slab_grad, upper_back, lower_back, upper_index, lower_index):
    return slab_grad.at[:, upper_index].add(upper_back).at[:, lower_index].add(lower_back)


def reference(node_feats, edge_feats, edge_source, edge_target, edge_counts, rim_upper, rim_lower,
              edge_first, edge_second, node_first, node_second, biases, node_cot):
    latent = F
    slab_slots = N_LAYER * E_DEV
    edge_state = edge_feats.reshape(latent, N_PHI, slab_slots).transpose(1, 0, 2)
    source_all = edge_source.reshape(N_PHI, slab_slots)
    target_all = edge_target.reshape(N_PHI, slab_slots)
    position = jnp.arange(slab_slots, dtype=jnp.int32) % E_DEV
    limits = jnp.repeat(edge_counts, E_DEV, axis=1)
    edge_valid = (position[None, :] < limits).astype(jnp.float32)
    bias_edge = biases[0][:, None]
    bias_message = biases[1][:, None]
    bias_node = biases[2][:, None]
    bias_update = biases[3][:, None]

    def extend(node_state):
        slab_nodes = node_state.reshape(latent, N_PHI, SLAB).transpose(1, 0, 2)
        upper_rows = jax.vmap(pick_columns)(slab_nodes, rim_upper)
        lower_rows = jax.vmap(pick_columns)(slab_nodes, rim_lower)
        from_below = jnp.roll(upper_rows, 1, axis=0)
        from_above = jnp.roll(lower_rows, -1, axis=0)
        return slab_nodes, jnp.concatenate([slab_nodes, from_below, from_above], axis=2)

    def edge_inputs(extended, slab_nodes, edges_now, source_p, target_p):
        return jnp.concatenate([jnp.take(extended, source_p, axis=1), jnp.take(slab_nodes, target_p, axis=1),
                                edges_now], axis=0)

    def slab_forward(bundle):
        extended, slab_nodes, edges_now, source_p, target_p, valid_p = bundle
        inputs = edge_inputs(extended, slab_nodes, edges_now, source_p, target_p)
        hidden_pre = forward_dot(edge_first, inputs) + bias_edge
        hidden = jax.nn.silu(hidden_pre).astype(jnp.bfloat16)
        new_edges = (valid_p * (edges_now.astype(jnp.float32) + forward_dot(edge_second, hidden)
                                + bias_message)).astype(jnp.bfloat16)
        messages = jnp.zeros((latent, SLAB), jnp.float32).at[:, target_p].add(new_edges.astype(jnp.float32))
        return new_edges, messages

    node_state = node_feats
    stored = []
    for iteration in range(ITERS):
        slab_nodes, extended = extend(node_state)
        new_edges, messages = lax.map(slab_forward, (extended, slab_nodes, edge_state, source_all, target_all, edge_valid))
        message_cols = messages.transpose(1, 0, 2).reshape(latent, NODES).astype(jnp.bfloat16)
        node_in = jnp.concatenate([node_state, message_cols], axis=0)
        node_pre = forward_dot(node_first, node_in) + bias_node
        node_hidden = jax.nn.silu(node_pre).astype(jnp.bfloat16)
        new_nodes = (node_state.astype(jnp.float32) + forward_dot(node_second, node_hidden)
                     + bias_update).astype(jnp.bfloat16)
        stored.append((slab_nodes, extended, edge_state, node_in, node_pre, node_hidden))
        node_state = new_nodes
        edge_state = new_edges
    node_out = node_state
    edge_out = edge_state.transpose(1, 0, 2).reshape(latent, EDGES)

    def slab_backward(bundle):
        extended, slab_nodes, edges_now, source_p, target_p, valid_p, message_p, grad_edge_p = bundle
        inputs = edge_inputs(extended, slab_nodes, edges_now, source_p, target_p)
        hidden_pre = forward_dot(edge_first, inputs) + bias_edge
        hidden = jax.nn.silu(hidden_pre).astype(jnp.bfloat16)
        edge_grad = valid_p * (grad_edge_p + jnp.take(message_p, target_p, axis=1).astype(jnp.float32))
        edge_low = edge_grad.astype(jnp.bfloat16)
        second_term = outer_dot(edge_low, hidden)
        pre_grad = back_dot(edge_second, edge_low) * silu_slope(hidden_pre)
        pre_low = pre_grad.astype(jnp.bfloat16)
        first_term = outer_dot(pre_low, inputs)
        previous = edge_grad + back_dot(edge_first[:, 2 * latent:], pre_low)
        extended_grad = jnp.zeros((latent, EXT), jnp.float32).at[:, source_p].add(
            back_dot(edge_first[:, :latent], pre_low))
        slab_grad = extended_grad[:, :SLAB].at[:, target_p].add(back_dot(edge_first[:, latent:2 * latent], pre_low))
        return (previous, slab_grad, extended_grad[:, SLAB:SLAB + RIM], extended_grad[:, SLAB + RIM:],
                first_term, second_term, jnp.sum(pre_grad, axis=1), jnp.sum(edge_grad, axis=1))

    grad_nodes = node_cot
    grad_edges = jnp.zeros((N_PHI, latent, slab_slots), jnp.float32)
    sum_first_edge = jnp.zeros(edge_first.shape, jnp.float32)
    sum_second_edge = jnp.zeros(edge_second.shape, jnp.float32)
    sum_first_node = jnp.zeros(node_first.shape, jnp.float32)
    sum_second_node = jnp.zeros(node_second.shape, jnp.float32)
    edge_bias = jnp.zeros((HID,), jnp.float32)
    message_bias = jnp.zeros((F,), jnp.float32)
    node_bias = jnp.zeros((HID,), jnp.float32)
    update_bias = jnp.zeros((F,), jnp.float32)
    for iteration in reversed(range(ITERS)):
        slab_nodes, extended, edges_now, node_in, node_pre, node_hidden = stored[iteration]
        nodes_low = grad_nodes.astype(jnp.bfloat16)
        sum_second_node = sum_second_node + outer_dot(nodes_low, node_hidden)
        update_bias = update_bias + jnp.sum(grad_nodes, axis=1)
        node_pre_grad = back_dot(node_second, nodes_low) * silu_slope(node_pre)
        node_pre_low = node_pre_grad.astype(jnp.bfloat16)
        sum_first_node = sum_first_node + outer_dot(node_pre_low, node_in)
        node_bias = node_bias + jnp.sum(node_pre_grad, axis=1)
        node_in_grad = back_dot(node_first, node_pre_low)
        message_grad = node_in_grad[latent:].astype(jnp.bfloat16)
        message_slabs = message_grad.reshape(latent, N_PHI, SLAB).transpose(1, 0, 2)
        results = lax.map(slab_backward, (extended, slab_nodes, edges_now, source_all, target_all, edge_valid,
                                          message_slabs, grad_edges))
        previous, slab_grad, upper_grad, lower_grad, first_term, second_term, pre_sums, edge_sums = results
        upper_back = jnp.roll(upper_grad, -1, axis=0)
        lower_back = jnp.roll(lower_grad, 1, axis=0)
        slab_grad = jax.vmap(place_rims)(slab_grad, upper_back, lower_back, rim_upper, rim_lower)
        grad_nodes = grad_nodes + node_in_grad[:latent] + slab_grad.transpose(1, 0, 2).reshape(latent, NODES)
        grad_edges = previous
        sum_first_edge = sum_first_edge + jnp.sum(first_term, axis=0)
        sum_second_edge = sum_second_edge + jnp.sum(second_term, axis=0)
        edge_bias = edge_bias + jnp.sum(pre_sums, axis=0)
        message_bias = message_bias + jnp.sum(edge_sums, axis=0)
    grad_biases = jnp.stack([edge_bias, message_bias, node_bias, update_bias])
    return (node_out, edge_out, grad_nodes, sum_first_edge, sum_second_edge, sum_first_node, sum_second_node,
            grad_biases)
```

```python
import functools
import itertools

import jax
import jax.numpy as jnp
from jax import lax
from jax.experimental import pallas as pl
from jax.experimental.pallas import tpu as pltpu
from jax.sharding import PartitionSpec as P

MESH = pl.DeviceIdType.MESH
BF16 = jnp.bfloat16
F32 = jnp.float32
LANES = 128
Y_LO = 2
CORES = 2
CHUNK = 512


def nn(left, right):
    return lax.dot_general(left, right, (((1,), (0,)), ((), ())), preferred_element_type=F32)


def nt(left, right):
    return lax.dot_general(left, right, (((1,), (1,)), ((), ())), preferred_element_type=F32)


def nt_exact(left, right):
    return lax.dot_general(
        left,
        right,
        (((1,), (1,)), ((), ())),
        precision=lax.Precision.HIGHEST,
        preferred_element_type=F32,
    )


def pick(rows, cols, row_shift, col_limit, dtype=BF16):
    row = lax.broadcasted_iota(jnp.int32, (rows, cols), 0)
    col = lax.broadcasted_iota(jnp.int32, (rows, cols), 1)
    return jnp.where((row == col + row_shift) & (col < col_limit), 1.0, 0.0).astype(dtype)


def two_parts(value):
    main = value.astype(BF16)
    return jnp.concatenate([main, (value - main.astype(F32)).astype(BF16)], axis=0)


def logistic(value):
    return 0.5 * jnp.tanh(0.5 * value) + 0.5


def chunks(total, step):
    size = min(CHUNK, total)

    def run(turn, carry):
        step(pl.ds(pl.multiple_of(turn * size, size), size))
        return carry

    lax.fori_loop(0, total // size, run, 0, unroll=True)


def wait_bytes(ref, sem):
    pltpu.make_async_copy(ref, ref, sem).wait()


def far_first(sizes):
    steps = list(itertools.product(*(range(size) for size in sizes)))
    hops = lambda step: sum(min(at, size - at) for at, size in zip(step, sizes))
    return sorted(steps[1:], key=hops, reverse=True)


def kernel(
    n_phi,
    n_layer,
    feats_in,
    edges_in,
    source_in,
    target_in,
    count_in,
    rim_up_in,
    rim_down_in,
    first_in,
    second_in,
    node_first_in,
    node_second_in,
    biases_in,
    cot_in,
    node_out,
    edge_out,
    node_grad,
    grad_first,
    grad_second,
    grad_node_first,
    grad_node_second,
    grad_biases,
    feats,
    edges0,
    source,
    target,
    count,
    rim_up,
    rim_down,
    first,
    second,
    node_first,
    node_second,
    biases,
    cot,
    onehot,
    rim_pick,
    rim_put,
    hidden_in,
    edge_new,
    z_part,
    slopes,
    grad_edge,
    second_grad_edge,
    back_stack,
    node_kept,
    grad_kept,
    own_send,
    slab_land,
    rim_send,
    rim_land,
    message_land,
    swap_land,
    back_send,
    back_land,
    comb_send,
    comb_land,
    grads,
    plane_land,
    z_land,
    grads_sum,
    load_sem,
    send_sem,
    recv_sem,
):
    hits, latent = feats.shape
    slots = edges0.shape[1]
    slab = hits * n_layer
    half = slab // 2
    rim = rim_up.shape[1]
    n_z = n_phi // (Y_LO * CORES)
    n_plane = Y_LO * CORES * n_layer
    n_x = n_layer // 2
    n_y = 2 * Y_LO
    shard = grads.shape[0] // n_plane
    phi = lax.axis_index("phi")
    layer = lax.axis_index("layer")
    core = lax.rem(phi, CORES)
    z_at = lax.rem(lax.div(phi, CORES), n_z)
    y_lo = lax.div(phi, CORES * n_z)
    y_hi = lax.div(layer, n_x)
    x_at = lax.rem(layer, n_x)
    y_at = y_hi * Y_LO + y_lo
    plane_at = (y_lo * CORES + core) * n_layer + layer
    above = lax.rem(phi + 1, n_phi)
    below = lax.rem(phi + n_phi - 1, n_phi)

    x_of = [lax.rem(x_at + step, n_x) for step in range(n_x)]
    y_hi_of = [lax.rem(y_hi + step, 2) * n_x for step in range(2)]
    layer_peers = [
        y_hi_of[dy // Y_LO] + x_of[dx]
        for dy, dx in far_first((n_y, n_x))
        if dy % Y_LO == 0
    ]
    y_of = [lax.rem(y_at + step, n_y) for step in range(n_y)]
    pair_of = [lax.rem(y, Y_LO) * CORES for y in y_of]
    phi_base = [lax.rem(y, Y_LO) * (CORES * n_z) + z_at * CORES for y in y_of]
    layer_base = [lax.div(y, Y_LO) * n_x for y in y_of]
    core_of = [core, 1 - core]
    plane_peers = []
    for dy, dx, dc in far_first((n_y, n_x, CORES)):
        device = (phi_base[dy] + core_of[dc], layer_base[dy] + x_of[dx])
        plane_peers.append((device, (pair_of[dy] + core_of[dc]) * n_layer + device[1]))
    z_peers = [
        (y_lo * (CORES * n_z) + lax.rem(z_at + step, n_z) * CORES + core, layer)
        for (step,) in far_first((n_z,))
    ]

    def send(src, dst, step, device):
        pltpu.make_async_remote_copy(
            src_ref=src,
            dst_ref=dst,
            send_sem=send_sem.at[step],
            recv_sem=recv_sem.at[step],
            device_id=device,
            device_id_type=MESH,
        ).start()

    barrier = pltpu.get_barrier_semaphore()
    greeted = z_peers + [device for device, _ in plane_peers] + [(above, layer), (below, layer)]
    for device in greeted:
        pl.semaphore_signal(barrier, inc=1, device_id=device, device_id_type=MESH)

    loads = [
        pltpu.make_async_copy(src, dst, load_sem.at[at])
        for at, (src, dst) in enumerate(
            (
                (feats_in, feats),
                (cot_in, cot),
                (first_in, first),
                (biases_in, biases),
                (second_in, second),
                (node_first_in, node_first),
                (node_second_in, node_second),
                (count_in, count),
                (source_in, source),
                (target_in, target),
                (rim_up_in, rim_up),
                (rim_down_in, rim_down),
                (edges_in, edges0),
            )
        )
    ]
    for load in loads:
        load.start()

    lane = lax.broadcasted_iota(jnp.int32, (1, LANES), 1)
    low_half = lane < latent
    own_rows = pl.ds(pl.multiple_of(layer * hits, hits), hits)
    swap_rows = pl.ds(pl.multiple_of(layer * half, half), half)

    loads[0].wait()
    loads[1].wait()
    wide_pick = pick(latent, LANES, 0, latent)
    high_pick = pick(latent, LANES, -latent, LANES)
    own_send[...] = (
        nn(feats[...], wide_pick) + nn(cot[...].astype(BF16), high_pick)
    ).astype(BF16)
    pl.semaphore_wait(barrier, len(greeted))
    for peer in layer_peers:
        send(own_send, slab_land.at[own_rows, :], 0, (phi, peer))
    slab_land[own_rows, :] = own_send[...]

    swaps = (message_land, swap_land.at[0], swap_land.at[1])

    def swap(at, value):
        swaps[at][swap_rows, :] = value.astype(swaps[at].dtype)
        mine = swaps[at].at[swap_rows, :]
        for peer in layer_peers:
            send(mine, mine, 3 + at, (phi, peer))

    def swapped_sum(at):
        wait_bytes(swaps[at].at[pl.ds(0, (n_layer - 1) * half), :], recv_sem.at[3 + at])
        total = swaps[at][0:half, :].astype(F32)
        for turn in range(1, n_layer):
            total = total + swaps[at][turn * half : (turn + 1) * half, :].astype(F32)
        return total

    for load in loads[2:7]:
        load.wait()
    edge_first = first[...]
    source_wide = nn(edge_first, pick(3 * latent, LANES, 0, latent)).astype(BF16)
    target_wide = nn(edge_first, pick(3 * latent, LANES, latent, latent)).astype(BF16)
    source_high = nn(edge_first, pick(3 * latent, LANES, -latent, LANES) * (~low_half).astype(BF16)).astype(BF16)
    target_high = nn(edge_first, pick(3 * latent, LANES, 0, LANES) * (~low_half).astype(BF16)).astype(BF16)
    first_self = edge_first[:, 2 * latent :]
    edge_second = second[...]
    square_eye = pick(latent, latent, 0, latent)
    self_back = nt(square_eye, first_self).astype(BF16)
    second_back = nt(square_eye, edge_second).astype(BF16)
    zero_square = jnp.zeros((latent, latent), BF16)
    gm_pick = jnp.concatenate(
        [
            high_pick,
            nt(square_eye, jnp.concatenate([zero_square, edge_second], axis=0)).astype(BF16),
        ],
        axis=0,
    )
    first_back = jnp.concatenate([source_wide, target_wide], axis=0)
    first_back_high = jnp.concatenate([source_high, target_high], axis=0)
    node_first_wide = jnp.concatenate(
        [node_first[...], jnp.zeros((LANES - latent, 2 * latent), BF16)], axis=0
    )
    node_second_low = nn(node_second[...], wide_pick).astype(BF16)
    zero_wide = jnp.zeros((LANES - latent, LANES), BF16)
    node_second_wide = jnp.concatenate([node_second_low, zero_wide], axis=0)
    node_second_under = jnp.concatenate([zero_wide, node_second_low], axis=0)
    bias_rows = lax.dot_general(
        biases[...],
        pick(latent, LANES, 0, latent, F32),
        (((1,), (0,)), ((), ())),
        precision=lax.Precision.HIGHEST,
        preferred_element_type=F32,
    )
    bias_cols = nt_exact(pick(latent, latent, 0, latent, F32), biases[...])
    bias_edge = bias_cols[:, 0:1]
    bias_message = bias_cols[:, 1:2]
    bias_node = bias_rows[2:3, :]
    bias_update = bias_rows[3:4, :]
    for load in loads[7:]:
        load.wait()

    def build(cols):
        width = cols.size
        spot = lax.broadcasted_iota(jnp.int32, (1, width), 1) + cols.start
        here = spot < count[...]
        source_at = jnp.where(here, source[:, cols], -1)
        target_at = jnp.where(here, target[:, cols], -1)
        row = lax.broadcasted_iota(jnp.int32, (slab, width), 0)
        onehot[0:slab, cols] = jnp.where(row == source_at, 1.0, 0.0).astype(BF16)
        onehot[slab : 2 * slab, cols] = jnp.where(row == target_at, 1.0, 0.0).astype(BF16)
        rim_row = lax.broadcasted_iota(jnp.int32, (2 * rim, width), 0) + slab
        onehot[2 * slab : 2 * slab + 2 * rim, cols] = jnp.where(
            rim_row == source_at, 1.0, 0.0
        ).astype(BF16)
        z_part[:, cols] = nn(first_self, edges0[:, cols]) + bias_edge

    chunks(slots, build)
    rim_eye = pick(rim, rim, 0, rim)
    for side, index in enumerate((rim_up, rim_down)):
        put = jnp.where(
            lax.broadcasted_iota(jnp.int32, (slab, rim), 0) == index[...], 1.0, 0.0
        ).astype(BF16)
        rim_put[side] = put
        rim_pick[side * rim : (side + 1) * rim, :] = nt(rim_eye, put).astype(BF16)
    grad_own = lax.dot_general(
        cot[...],
        pick(latent, LANES, 0, latent, F32),
        (((1,), (0,)), ((), ())),
        precision=lax.Precision.HIGHEST,
        preferred_element_type=F32,
    )

    wait_bytes(slab_land.at[pl.ds(0, slab - hits), :], recv_sem.at[0])
    table = jnp.where(low_half, slab_land[...].astype(F32), 0.0).astype(BF16)
    for k in range(2):
        rim_send[k] = nn(rim_pick[...], table).astype(BF16)
        send(rim_send.at[k, 0:rim], rim_land.at[k, 0:rim], 1 + k, (above, layer))
        send(
            rim_send.at[k, rim : 2 * rim],
            rim_land.at[k, rim : 2 * rim],
            1 + k,
            (below, layer),
        )
        own_part = two_parts(
            jnp.concatenate([nt(source_wide, table), nt(target_wide, table)], axis=1)
        )

        def own_terms(cols):
            terms = nn(own_part, onehot[0 : 2 * slab, cols])
            z_part[:, cols] = z_part[:, cols] + (terms[0:latent] + terms[latent:])

        chunks(slots, own_terms)
        wait_bytes(rim_land.at[k], recv_sem.at[1 + k])
        rim_part = two_parts(nt(source_wide, rim_land[k]))

        def edge_mlp(cols):
            width = cols.size
            terms = nn(rim_part, onehot[2 * slab : 2 * slab + 2 * rim, cols])
            pre = z_part[:, cols] + (terms[0:latent] + terms[latent:])
            gate = logistic(pre)
            hidden = (pre * gate).astype(BF16)
            hidden_in[k, 3 * latent : 4 * latent, cols] = hidden
            slopes[k, :, cols] = gate * (1.0 + pre * (1.0 - gate))
            old = edges0[:, cols] if k == 0 else edge_new[0, 0:latent, cols]
            here = lax.broadcasted_iota(jnp.int32, (1, width), 1) + cols.start < count[...]
            fresh = jnp.where(
                here, old.astype(F32) + nn(edge_second, hidden) + bias_message, 0.0
            ).astype(BF16)
            edge_new[k, 0:latent, cols] = fresh
            edge_new[k, latent : 2 * latent, cols] = fresh

        chunks(slots, edge_mlp)
        both_halves = nt(onehot[slab : 2 * slab, :], edge_new[k])
        swap(k, jnp.where(low_half, both_halves[0:half], both_halves[half:]))

        raw_own = nt(wide_pick, table).astype(BF16)
        raw_rim = nt(wide_pick, rim_land[k]).astype(BF16)

        def inputs(cols):
            hidden_in[k, 0:latent, cols] = (
                nn(raw_own, onehot[0:slab, cols])
                + nn(raw_rim, onehot[2 * slab : 2 * slab + 2 * rim, cols])
            ).astype(BF16)
            hidden_in[k, latent : 2 * latent, cols] = nn(
                raw_own, onehot[slab : 2 * slab, cols]
            ).astype(BF16)
            if k == 0:
                old = edges0[:, cols]
                z_part[:, cols] = nn(first_self, edge_new[0, 0:latent, cols]) + bias_edge
            else:
                old = edge_new[0, 0:latent, cols]
                edge_out[:, cols] = edge_new[1, 0:latent, cols]
            hidden_in[k, 2 * latent : 3 * latent, cols] = old

        chunks(slots, inputs)
        packed = swapped_sum(k)
        turned = pltpu.roll(packed, latent, 1)
        table_wide = table.astype(F32)
        node_in = jnp.concatenate(
            [
                jnp.where(low_half, table_wide[0:half], turned),
                jnp.where(low_half, table_wide[half:], packed),
            ],
            axis=0,
        ).astype(BF16)
        node_pre = nt(node_in, node_first_wide) + bias_node
        node_gate = logistic(node_pre)
        node_hidden = (node_pre * node_gate).astype(BF16)
        node_slope = node_gate * (1.0 + node_pre * (1.0 - node_gate))
        node_kept[k, 0] = node_in
        node_kept[k, 1] = node_hidden
        if k == 0:
            first_slope = node_slope
        table = (table_wide + nt(node_hidden, node_second_wide) + bias_update).astype(BF16)

    for k in (1, 0):
        if k == 1:
            pre_back = nn(slab_land[...], node_second_under) * node_slope
        else:
            grad_low = grad_now.astype(BF16)
            pre_back = nn(grad_low, node_second_wide) * first_slope
        pre_low = pre_back.astype(BF16)
        in_back = nn(pre_low, node_first_wide)
        gm_part = nt(gm_pick, in_back.astype(BF16))
        gm_part = jnp.concatenate([gm_part[0:latent].astype(BF16), two_parts(gm_part[latent:])], axis=0)

        def edge_back(cols):
            both = nn(gm_part, onehot[slab : 2 * slab, cols])
            edge_grad = both[0:latent]
            hidden_grad = both[latent : 2 * latent] + both[2 * latent :]
            if k == 0:
                edge_grad = edge_grad + grad_edge[:, cols]
                hidden_grad = hidden_grad + second_grad_edge[:, cols]
            else:
                grad_edge[:, cols] = edge_grad
            pre_grad = (hidden_grad * slopes[k, :, cols]).astype(BF16)
            back_stack[0:latent, cols] = pre_grad
            back_stack[latent : 2 * latent, cols] = pre_grad
            back_stack[2 * latent : 3 * latent, cols] = edge_grad.astype(BF16)

        chunks(slots, edge_back)

        def weight_terms():
            outer = nt(back_stack[latent : 3 * latent, :], hidden_in[k])
            upper = outer[0:latent, 0:LANES]
            lower = jnp.where(low_half, outer[0:latent, LANES:], outer[latent:, LANES:])
            ones = jnp.ones((8, slots), BF16)
            pre_sums = nt(ones, back_stack[0 : 2 * latent, :])
            edge_sums = nt(ones, back_stack[latent : 3 * latent, :])
            row = lax.broadcasted_iota(jnp.int32, (8, LANES), 0)
            bias_terms = jnp.where(
                low_half,
                0.0,
                jnp.where(row == 0, pre_sums, jnp.where(row == 1, edge_sums, 0.0)),
            )
            return upper, lower, bias_terms

        if k == 0:
            upper, lower, bias_terms = weight_terms()
            grads[0:latent, :] = grads[0:latent, :] + upper
            grads[latent : 2 * latent, :] = grads[latent : 2 * latent, :] + lower

        def node_terms():
            grad_kept[0] = pre_back
            grad_kept[1] = in_back
            if k == 0:
                grad_kept[2] = gained
                grad_mine = grad_own + grad_kept[2, own_rows, :]
            else:
                grad_mine = grad_own
            pre_mine = grad_kept[0, own_rows, :]
            row = lax.broadcasted_iota(jnp.int32, (8, LANES), 0)
            shifted = jnp.where(
                row == 2,
                jnp.sum(pre_mine, axis=0, keepdims=True),
                jnp.where(row == 3, jnp.sum(grad_mine, axis=0, keepdims=True), 0.0),
            )
            return (
                nn(nt(wide_pick, pre_mine.astype(BF16)).astype(BF16), node_kept[k, 0, own_rows, :]),
                nn(nt(wide_pick, grad_mine.astype(BF16)).astype(BF16), node_kept[k, 1, own_rows, :]),
                pltpu.roll(shifted, latent, 1),
                grad_mine + jnp.where(low_half, grad_kept[1, own_rows, :], 0.0),
            )

        if k == 0:
            first_terms, second_terms, node_bias, grad_own = node_terms()
            grads[2 * latent : 3 * latent, :] = grads[2 * latent : 3 * latent, :] + first_terms
            grads[3 * latent : 4 * latent, :] = grads[3 * latent : 4 * latent, :] + second_terms
            bias_at = slice(3 * latent, 3 * latent + 8)
            grads[bias_at, :] = grads[bias_at, :] + bias_terms + node_bias
            for at, (device, spot) in enumerate(plane_peers):
                send(
                    grads.at[pl.ds(pl.multiple_of(spot * shard, shard), shard), :],
                    plane_land.at[pl.ds(at * shard, shard), :],
                    6,
                    device,
                )

        back_send[k] = nt(
            onehot[2 * slab : 2 * slab + 2 * rim, :], back_stack[0 : 2 * latent, :]
        ).astype(BF16)
        send(back_send.at[k, 0:rim], back_land.at[k, 0:rim], 7 + k, (below, layer))
        send(
            back_send.at[k, rim : 2 * rim],
            back_land.at[k, rim : 2 * rim],
            7 + k,
            (above, layer),
        )
        from_source = nt(onehot[0:slab, :], back_stack[0 : 2 * latent, :])
        from_target = nt(onehot[slab : 2 * slab, :], back_stack[0 : 2 * latent, :])
        if k == 0:
            wait_bytes(plane_land, recv_sem.at[6])
            shard_rows = pl.ds(pl.multiple_of(plane_at * shard, shard), shard)
            total = grads[shard_rows, :]
            for turn in range(n_plane - 1):
                total = total + plane_land[turn * shard : (turn + 1) * shard, :]
            z_rows = pl.ds(pl.multiple_of(z_at * shard, shard), shard)
            z_land[z_rows, :] = total
            for peer in z_peers:
                send(z_land.at[z_rows, :], z_land.at[z_rows, :], 9, peer)
        wait_bytes(back_land.at[k], recv_sem.at[7 + k])
        from_source = (
            from_source
            + nn(rim_put[0], back_land[k, 0:rim])
            + nn(rim_put[1], back_land[k, rim : 2 * rim])
        )
        comb = jnp.where(low_half, from_source, from_target).astype(BF16)
        packed = nn(comb[0:half], first_back) + nn(comb[half:], first_back_high)
        if k == 1:
            swap(2, packed)
            upper, lower, bias_terms = weight_terms()
            first_terms, second_terms, node_bias, grad_own = node_terms()
            grads[0:latent, :] = upper
            grads[latent : 2 * latent, :] = lower
            grads[2 * latent : 3 * latent, :] = first_terms
            grads[3 * latent : 4 * latent, :] = second_terms
            bias_at = slice(3 * latent, 3 * latent + 8)
            grads[bias_at, :] = grads[bias_at, :] + bias_terms + node_bias
            node_kept[1, 0] = table
            node_out[...] = node_kept[1, 0, own_rows, 0:latent]

            def carried(cols):
                old = grad_edge[:, cols] + nn(self_back, back_stack[0:latent, cols])
                grad_edge[:, cols] = old
                second_grad_edge[:, cols] = nn(second_back, old.astype(BF16))

            chunks(slots, carried)
            cot_slab = pltpu.roll(slab_land[...].astype(F32), latent, 1)
            grad_before = jnp.where(low_half, cot_slab + in_back, 0.0)
            packed = swapped_sum(2)
            gained = jnp.concatenate(
                [
                    jnp.where(low_half, packed, 0.0),
                    jnp.where(low_half, pltpu.roll(packed, latent, 1), 0.0),
                ],
                axis=0,
            )
            grad_now = grad_before + gained
        else:
            comb_send[...] = packed.astype(BF16)

            def rows_of(device):
                return pl.ds(pl.multiple_of(lax.rem(device, n_layer // 2) * hits, hits), hits)

            for at, peer in enumerate(layer_peers):
                send(
                    comb_send.at[rows_of(peer), :],
                    comb_land.at[pl.ds(at * hits, hits), :],
                    10,
                    (phi, peer),
                )
            wait_bytes(z_land.at[pl.ds(0, (n_z - 1) * shard), :], recv_sem.at[9])
            total = z_land[0:shard, :]
            for turn in range(1, n_z):
                total = total + z_land[turn * shard : (turn + 1) * shard, :]
            grads_sum[shard_rows, :] = total
            for device, _ in plane_peers:
                send(grads_sum.at[shard_rows, :], grads_sum.at[shard_rows, :], 11, device)
            wait_bytes(comb_land, recv_sem.at[10])
            total = comb_send[rows_of(layer), :].astype(F32)
            for turn in range(n_layer - 1):
                total = total + comb_land[turn * hits : (turn + 1) * hits, :].astype(F32)
            total = jnp.where(layer < n_layer // 2, total, pltpu.roll(total, latent, 1))
            node_grad[...] = (grad_own + total)[:, 0:latent]

    wait_bytes(grads_sum.at[pl.ds(0, (n_plane - 1) * shard), :], recv_sem.at[11])
    grad_first[:, 0:LANES] = grads_sum[0:latent, :]
    grad_first[:, LANES:] = grads_sum[latent : 2 * latent, 0:latent]
    grad_second[...] = pltpu.roll(grads_sum[latent : 2 * latent, :], latent, 1)[:, 0:latent]
    grad_node_first[...] = grads_sum[2 * latent : 3 * latent, :]
    grad_node_second[...] = grads_sum[3 * latent : 4 * latent, 0:latent]
    grad_biases[...] = pltpu.roll(grads_sum[3 * latent : 3 * latent + 8, :], latent, 1)[
        0:4, 0:latent
    ]

    wait_bytes(slab_land.at[pl.ds(0, slab - hits), :], send_sem.at[0])
    for k in range(2):
        wait_bytes(rim_send.at[k], send_sem.at[1 + k])
        wait_bytes(back_send.at[k], send_sem.at[7 + k])
    for at in range(3):
        wait_bytes(swaps[at].at[pl.ds(0, (n_layer - 1) * half), :], send_sem.at[3 + at])
    wait_bytes(plane_land, send_sem.at[6])
    wait_bytes(z_land.at[pl.ds(0, (n_z - 1) * shard), :], send_sem.at[9])
    wait_bytes(comb_land, send_sem.at[10])
    wait_bytes(grads_sum.at[pl.ds(0, (n_plane - 1) * shard), :], send_sem.at[11])


def deliver(*refs):
    many = len(refs) // 2
    sems = refs[-1]
    copies = [
        pltpu.make_async_copy(refs[at], refs[many + at], sems.at[at]) for at in range(many)
    ]
    for copy in copies:
        copy.start()
    for copy in copies:
        copy.wait()


def body(n_phi, n_layer, *arrays):
    node_feats, edge_feats, edge_source, edge_target, *others, node_cot = arrays
    latent, hits = node_feats.shape
    slots = edge_feats.shape[1]
    slab = hits * n_layer
    rim = others[1].shape[1]
    n_plane = Y_LO * CORES * n_layer
    n_z = n_phi // (Y_LO * CORES)
    grad_rows = 4 * latent
    shard = grad_rows // n_plane
    vmem = pl.BlockSpec(memory_space=pltpu.VMEM)
    hbm = pl.BlockSpec(memory_space=pltpu.HBM)
    operands = (
        node_feats.T,
        edge_feats,
        edge_source.reshape(1, slots),
        edge_target.reshape(1, slots),
        *others,
        node_cot.T,
    )
    outs = [
        jax.ShapeDtypeStruct(*out)
        for out in (
            ((hits, latent), BF16),
            ((latent, slots), BF16),
            ((hits, latent), F32),
            ((latent, 3 * latent), F32),
            ((latent, latent), F32),
            ((latent, 2 * latent), F32),
            ((latent, latent), F32),
            ((4, latent), F32),
        )
    ]
    results = pl.pallas_call(
        functools.partial(kernel, n_phi, n_layer),
        out_shape=outs,
        in_specs=[hbm] * len(operands),
        out_specs=[vmem] * len(outs),
        scratch_shapes=[pltpu.VMEM(array.shape, array.dtype) for array in operands]
        + [
            pltpu.VMEM((2 * slab + 2 * rim, slots), BF16),
            pltpu.VMEM((2 * rim, slab), BF16),
            pltpu.VMEM((2, slab, rim), BF16),
            pltpu.VMEM((2, 4 * latent, slots), BF16),
            pltpu.VMEM((2, 2 * latent, slots), BF16),
            pltpu.VMEM((latent, slots), F32),
            pltpu.VMEM((2, latent, slots), F32),
            pltpu.VMEM((latent, slots), F32),
            pltpu.VMEM((latent, slots), F32),
            pltpu.VMEM((3 * latent, slots), BF16),
            pltpu.VMEM((2, 2, slab, LANES), BF16),
            pltpu.VMEM((3, slab, LANES), F32),
            pltpu.VMEM((hits, LANES), BF16),
            pltpu.VMEM((slab, LANES), BF16),
            pltpu.VMEM((2, 2 * rim, LANES), BF16),
            pltpu.VMEM((2, 2 * rim, LANES), BF16),
            pltpu.VMEM((n_layer * slab // 2, LANES), F32),
            pltpu.VMEM((2, n_layer * slab // 2, LANES), BF16),
            pltpu.VMEM((2, 2 * rim, LANES), BF16),
            pltpu.VMEM((2, 2 * rim, LANES), BF16),
            pltpu.VMEM((slab // 2, LANES), BF16),
            pltpu.VMEM(((n_layer - 1) * hits, LANES), BF16),
            pltpu.VMEM((grad_rows, LANES), F32),
            pltpu.VMEM(((n_plane - 1) * shard, LANES), F32),
            pltpu.VMEM((n_z * shard, LANES), F32),
            pltpu.VMEM((grad_rows, LANES), F32),
            pltpu.SemaphoreType.DMA((len(operands),)),
            pltpu.SemaphoreType.DMA((12,)),
            pltpu.SemaphoreType.DMA((12,)),
        ],
        compiler_params=pltpu.CompilerParams(
            collective_id=0, has_side_effects=True, vmem_limit_bytes=40 * 1024 * 1024
        ),
    )(*operands)
    node_out, edge_out, node_grad, *totals = pl.pallas_call(
        deliver,
        out_shape=outs,
        in_specs=[vmem] * len(outs),
        out_specs=[hbm] * len(outs),
        scratch_shapes=[pltpu.SemaphoreType.DMA((len(outs),))],
    )(*results)
    return node_out.T, edge_out, node_grad.T, *totals


def solution(mesh):
    split = P(None, ("phi", "layer"))
    return jax.shard_map(
        functools.partial(body, mesh.shape["phi"], mesh.shape["layer"]),
        mesh=mesh,
        in_specs=(
            split,
            split,
            P(("phi", "layer")),
            P(("phi", "layer")),
            P("phi", "layer"),
            P("phi", None),
            P("phi", None),
            P(),
            P(),
            P(),
            P(),
            P(),
            split,
        ),
        out_specs=(split, split, split, P(), P(), P(), P(), P()),
        check_vma=False,
    )
```

```python
import functools
import itertools

import jax
import jax.numpy as jnp
from jax import lax
from jax.experimental import pallas as pl
from jax.experimental.pallas import tpu as pltpu
from jax.sharding import PartitionSpec as P

MESH = pl.DeviceIdType.MESH
BF16 = jnp.bfloat16
F32 = jnp.float32
LANES = 128
Y_LO = 2
CORES = 2
CHUNK = 512
VMEM_BYTES = 64 * 1024 * 1024


def nn(left, right):
    return lax.dot_general(left, right, (((1,), (0,)), ((), ())), preferred_element_type=F32)


def nt(left, right):
    return lax.dot_general(left, right, (((1,), (1,)), ((), ())), preferred_element_type=F32)


def nt_exact(left, right):
    return lax.dot_general(
        left,
        right,
        (((1,), (1,)), ((), ())),
        precision=lax.Precision.HIGHEST,
        preferred_element_type=F32,
    )


def pick(rows, cols, row_shift, col_limit, dtype=BF16):
    row = lax.broadcasted_iota(jnp.int32, (rows, cols), 0)
    col = lax.broadcasted_iota(jnp.int32, (rows, cols), 1)
    return jnp.where((row == col + row_shift) & (col < col_limit), 1.0, 0.0).astype(dtype)


def two_parts(value):
    main = value.astype(BF16)
    return jnp.concatenate([main, (value - main.astype(F32)).astype(BF16)], axis=0)


def logistic(value):
    return 0.5 * jnp.tanh(0.5 * value) + 0.5


def chunks(total, step):
    size = min(CHUNK, total)

    def run(turn, carry):
        step(pl.ds(pl.multiple_of(turn * size, size), size))
        return carry

    lax.fori_loop(0, total // size, run, 0, unroll=True)


def wait_bytes(ref, sem):
    pltpu.make_async_copy(ref, ref, sem).wait()


def far_first(sizes):
    steps = list(itertools.product(*(range(size) for size in sizes)))
    hops = lambda step: sum(min(at, size - at) for at, size in zip(step, sizes))
    return sorted(steps[1:], key=hops, reverse=True)


def kernel(
    n_phi,
    n_layer,
    feats_in,
    edges_in,
    source_in,
    target_in,
    count_in,
    rim_up_in,
    rim_down_in,
    first_in,
    second_in,
    node_first_in,
    node_second_in,
    biases_in,
    cot_in,
    node_out_to,
    edge_out_to,
    node_grad_to,
    grad_first_to,
    grad_second_to,
    grad_node_first_to,
    grad_node_second_to,
    grad_biases_to,
    feats,
    edges0,
    source,
    target,
    count,
    rim_up,
    rim_down,
    first,
    second,
    node_first,
    node_second,
    biases,
    cot,
    node_out,
    edge_out,
    node_grad,
    grad_first,
    grad_second,
    grad_node_first,
    grad_node_second,
    grad_biases,
    onehot,
    rim_pick,
    rim_put,
    hidden_in,
    edge_new,
    z_part,
    slopes,
    grad_edge,
    second_grad_edge,
    back_stack,
    node_kept,
    grad_kept,
    own_send,
    slab_land,
    rim_send,
    rim_land,
    message_land,
    swap_land,
    back_send,
    back_land,
    comb_send,
    comb_land,
    grads,
    plane_land,
    z_land,
    grads_sum,
    load_sem,
    store_sem,
    chain_sem,
    send_sem,
    recv_sem,
):
    hits, latent = feats.shape
    slots = edges0.shape[1]
    slab = hits * n_layer
    half = slab // 2
    rim = rim_up.shape[1]
    n_z = n_phi // (Y_LO * CORES)
    n_plane = Y_LO * CORES * n_layer
    n_x = n_layer // 2
    n_y = 2 * Y_LO
    shard = grads.shape[0] // n_plane
    phi = lax.axis_index("phi")
    layer = lax.axis_index("layer")
    core = lax.rem(phi, CORES)
    z_at = lax.rem(lax.div(phi, CORES), n_z)
    y_lo = lax.div(phi, CORES * n_z)
    y_hi = lax.div(layer, n_x)
    x_at = lax.rem(layer, n_x)
    y_at = y_hi * Y_LO + y_lo
    plane_at = (y_lo * CORES + core) * n_layer + layer
    above = lax.rem(phi + 1, n_phi)
    below = lax.rem(phi + n_phi - 1, n_phi)

    x_of = [lax.rem(x_at + step, n_x) for step in range(n_x)]
    y_hi_of = [lax.rem(y_hi + step, 2) * n_x for step in range(2)]
    layer_peers = [
        y_hi_of[dy // Y_LO] + x_of[dx]
        for dy, dx in far_first((n_y, n_x))
        if dy % Y_LO == 0
    ]
    y_of = [lax.rem(y_at + step, n_y) for step in range(n_y)]
    pair_of = [lax.rem(y, Y_LO) * CORES for y in y_of]
    phi_base = [lax.rem(y, Y_LO) * (CORES * n_z) + z_at * CORES for y in y_of]
    layer_base = [lax.div(y, Y_LO) * n_x for y in y_of]
    core_of = [core, 1 - core]
    plane_peers = []
    for dy, dx, dc in far_first((n_y, n_x, CORES)):
        device = (phi_base[dy] + core_of[dc], layer_base[dy] + x_of[dx])
        plane_peers.append((device, (pair_of[dy] + core_of[dc]) * n_layer + device[1]))
    z_peers = [
        (y_lo * (CORES * n_z) + lax.rem(z_at + step, n_z) * CORES + core, layer)
        for (step,) in far_first((n_z,))
    ]

    def send(src, dst, step, device):
        pltpu.make_async_remote_copy(
            src_ref=src,
            dst_ref=dst,
            send_sem=send_sem.at[step],
            recv_sem=recv_sem.at[step],
            device_id=device,
            device_id_type=MESH,
        ).start()

    barrier = pltpu.get_barrier_semaphore()

    def along_z(step):
        return y_lo * (CORES * n_z) + lax.rem(z_at + step + n_z, n_z) * CORES + core, layer

    def greet(sem, devices):
        for device in devices:
            pl.semaphore_signal(sem, inc=1, device_id=device, device_id_type=MESH)

    greeted = [(phi, peer) for peer in layer_peers] + [
        (phi_base[0] + 1 - core, layer),
        (phi_base[0] + (1 - 2 * y_lo) * (CORES * n_z) + core, layer),
        (phi_base[0] + (1 - 2 * y_lo) * (CORES * n_z) + 1 - core, layer),
        (above, layer),
        (below, layer),
        along_z(1),
        along_z(-1),
    ]
    greet(barrier, greeted)

    loads = [
        pltpu.make_async_copy(src, dst, load_sem.at[at])
        for at, (src, dst) in enumerate(
            (
                (feats_in, feats),
                (cot_in, cot),
                (first_in, first),
                (biases_in, biases),
                (second_in, second),
                (node_first_in, node_first),
                (node_second_in, node_second),
                (count_in, count),
                (source_in, source),
                (target_in, target),
                (rim_up_in, rim_up),
                (rim_down_in, rim_down),
                (edges_in, edges0),
            )
        )
    ]
    for load in loads:
        load.start()

    lane = lax.broadcasted_iota(jnp.int32, (1, LANES), 1)
    low_half = lane < latent
    own_rows = pl.ds(pl.multiple_of(layer * hits, hits), hits)
    swap_rows = pl.ds(pl.multiple_of(layer * half, half), half)

    loads[0].wait()
    loads[1].wait()
    wide_pick = pick(latent, LANES, 0, latent)
    high_pick = pick(latent, LANES, -latent, LANES)
    own_send[...] = (
        nn(feats[...], wide_pick) + nn(cot[...].astype(BF16), high_pick)
    ).astype(BF16)
    pl.semaphore_wait(barrier, len(greeted))
    known = [step for step in (1, 2, 4) if step < n_z // 2]

    def tell(at):
        if at < len(known):
            greet(chain_sem.at[at], [along_z(known[at]), along_z(-known[at])])

    def told(at):
        if at < len(known):
            pl.semaphore_wait(chain_sem.at[at], 2)

    tell(0)
    for peer in layer_peers:
        send(own_send, slab_land.at[own_rows, :], 0, (phi, peer))
    slab_land[own_rows, :] = own_send[...]

    stores = [
        pltpu.make_async_copy(src, dst, store_sem.at[at])
        for at, (src, dst) in enumerate(
            (
                (node_out, node_out_to),
                (edge_out, edge_out_to),
                (node_grad, node_grad_to),
                (grad_first, grad_first_to),
                (grad_second, grad_second_to),
                (grad_node_first, grad_node_first_to),
                (grad_node_second, grad_node_second_to),
                (grad_biases, grad_biases_to),
            )
        )
    ]
    swaps = (message_land, swap_land.at[0], swap_land.at[1])

    def swap(at, value):
        swaps[at][swap_rows, :] = value.astype(swaps[at].dtype)
        mine = swaps[at].at[swap_rows, :]
        for peer in layer_peers:
            send(mine, mine, 3 + at, (phi, peer))

    def swapped_sum(at):
        wait_bytes(swaps[at].at[pl.ds(0, (n_layer - 1) * half), :], recv_sem.at[3 + at])
        total = swaps[at][0:half, :].astype(F32)
        for turn in range(1, n_layer):
            total = total + swaps[at][turn * half : (turn + 1) * half, :].astype(F32)
        return total

    for load in loads[2:7]:
        load.wait()
    edge_first = first[...]
    source_wide = nn(edge_first, pick(3 * latent, LANES, 0, latent)).astype(BF16)
    target_wide = nn(edge_first, pick(3 * latent, LANES, latent, latent)).astype(BF16)
    source_high = nn(edge_first, pick(3 * latent, LANES, -latent, LANES) * (~low_half).astype(BF16)).astype(BF16)
    target_high = nn(edge_first, pick(3 * latent, LANES, 0, LANES) * (~low_half).astype(BF16)).astype(BF16)
    first_self = edge_first[:, 2 * latent :]
    edge_second = second[...]
    square_eye = pick(latent, latent, 0, latent)
    self_back = nt(square_eye, first_self).astype(BF16)
    second_back = nt(square_eye, edge_second).astype(BF16)
    zero_square = jnp.zeros((latent, latent), BF16)
    gm_pick = jnp.concatenate(
        [
            high_pick,
            nt(square_eye, jnp.concatenate([zero_square, edge_second], axis=0)).astype(BF16),
        ],
        axis=0,
    )
    first_back = jnp.concatenate([source_wide, target_wide], axis=0)
    first_back_high = jnp.concatenate([source_high, target_high], axis=0)
    node_first_wide = jnp.concatenate(
        [node_first[...], jnp.zeros((LANES - latent, 2 * latent), BF16)], axis=0
    )
    node_second_low = nn(node_second[...], wide_pick).astype(BF16)
    zero_wide = jnp.zeros((LANES - latent, LANES), BF16)
    node_second_wide = jnp.concatenate([node_second_low, zero_wide], axis=0)
    node_second_under = jnp.concatenate([zero_wide, node_second_low], axis=0)
    bias_rows = lax.dot_general(
        biases[...],
        pick(latent, LANES, 0, latent, F32),
        (((1,), (0,)), ((), ())),
        precision=lax.Precision.HIGHEST,
        preferred_element_type=F32,
    )
    bias_cols = nt_exact(pick(latent, latent, 0, latent, F32), biases[...])
    bias_edge = bias_cols[:, 0:1]
    bias_message = bias_cols[:, 1:2]
    bias_node = bias_rows[2:3, :]
    bias_update = bias_rows[3:4, :]
    for load in loads[7:]:
        load.wait()

    def build(cols):
        width = cols.size
        spot = lax.broadcasted_iota(jnp.int32, (1, width), 1) + cols.start
        here = spot < count[...]
        source_at = jnp.where(here, source[:, cols], -1)
        target_at = jnp.where(here, target[:, cols], -1)
        row = lax.broadcasted_iota(jnp.int32, (slab, width), 0)
        onehot[0:slab, cols] = jnp.where(row == source_at, 1.0, 0.0).astype(BF16)
        onehot[slab : 2 * slab, cols] = jnp.where(row == target_at, 1.0, 0.0).astype(BF16)
        rim_row = lax.broadcasted_iota(jnp.int32, (2 * rim, width), 0) + slab
        onehot[2 * slab : 2 * slab + 2 * rim, cols] = jnp.where(
            rim_row == source_at, 1.0, 0.0
        ).astype(BF16)
        z_part[:, cols] = nn(first_self, edges0[:, cols]) + bias_edge

    chunks(slots, build)
    rim_eye = pick(rim, rim, 0, rim)
    for side, index in enumerate((rim_up, rim_down)):
        put = jnp.where(
            lax.broadcasted_iota(jnp.int32, (slab, rim), 0) == index[...], 1.0, 0.0
        ).astype(BF16)
        rim_put[side] = put
        rim_pick[side * rim : (side + 1) * rim, :] = nt(rim_eye, put).astype(BF16)
    grad_own = lax.dot_general(
        cot[...],
        pick(latent, LANES, 0, latent, F32),
        (((1,), (0,)), ((), ())),
        precision=lax.Precision.HIGHEST,
        preferred_element_type=F32,
    )

    wait_bytes(slab_land.at[pl.ds(0, slab - hits), :], recv_sem.at[0])
    told(0)
    tell(1)
    table = jnp.where(low_half, slab_land[...].astype(F32), 0.0).astype(BF16)
    for k in range(2):
        rim_send[k] = nn(rim_pick[...], table).astype(BF16)
        send(rim_send.at[k, 0:rim], rim_land.at[k, 0:rim], 1 + k, (above, layer))
        send(
            rim_send.at[k, rim : 2 * rim],
            rim_land.at[k, rim : 2 * rim],
            1 + k,
            (below, layer),
        )
        own_part = two_parts(
            jnp.concatenate([nt(source_wide, table), nt(target_wide, table)], axis=1)
        )

        def own_terms(cols):
            terms = nn(own_part, onehot[0 : 2 * slab, cols])
            z_part[:, cols] = z_part[:, cols] + (terms[0:latent] + terms[latent:])

        chunks(slots, own_terms)
        wait_bytes(rim_land.at[k], recv_sem.at[1 + k])
        rim_part = two_parts(nt(source_wide, rim_land[k]))

        def edge_mlp(cols):
            width = cols.size
            terms = nn(rim_part, onehot[2 * slab : 2 * slab + 2 * rim, cols])
            pre = z_part[:, cols] + (terms[0:latent] + terms[latent:])
            gate = logistic(pre)
            hidden = (pre * gate).astype(BF16)
            hidden_in[k, 3 * latent : 4 * latent, cols] = hidden
            slopes[k, :, cols] = gate * (1.0 + pre * (1.0 - gate))
            old = edges0[:, cols] if k == 0 else edge_new[0, 0:latent, cols]
            here = lax.broadcasted_iota(jnp.int32, (1, width), 1) + cols.start < count[...]
            fresh = jnp.where(
                here, old.astype(F32) + nn(edge_second, hidden) + bias_message, 0.0
            ).astype(BF16)
            edge_new[k, 0:latent, cols] = fresh
            edge_new[k, latent : 2 * latent, cols] = fresh

        chunks(slots, edge_mlp)
        both_halves = nt(onehot[slab : 2 * slab, :], edge_new[k])
        swap(k, jnp.where(low_half, both_halves[0:half], both_halves[half:]))

        raw_own = nt(wide_pick, table).astype(BF16)
        raw_rim = nt(wide_pick, rim_land[k]).astype(BF16)

        def inputs(cols):
            hidden_in[k, 0:latent, cols] = (
                nn(raw_own, onehot[0:slab, cols])
                + nn(raw_rim, onehot[2 * slab : 2 * slab + 2 * rim, cols])
            ).astype(BF16)
            hidden_in[k, latent : 2 * latent, cols] = nn(
                raw_own, onehot[slab : 2 * slab, cols]
            ).astype(BF16)
            if k == 0:
                old = edges0[:, cols]
                z_part[:, cols] = nn(first_self, edge_new[0, 0:latent, cols]) + bias_edge
            else:
                old = edge_new[0, 0:latent, cols]
                edge_out[:, cols] = edge_new[1, 0:latent, cols]
            hidden_in[k, 2 * latent : 3 * latent, cols] = old

        chunks(slots, inputs)
        packed = swapped_sum(k)
        told(1 + k)
        if k == 0:
            tell(2)
        turned = pltpu.roll(packed, latent, 1)
        table_wide = table.astype(F32)
        node_in = jnp.concatenate(
            [
                jnp.where(low_half, table_wide[0:half], turned),
                jnp.where(low_half, table_wide[half:], packed),
            ],
            axis=0,
        ).astype(BF16)
        node_pre = nt(node_in, node_first_wide) + bias_node
        node_gate = logistic(node_pre)
        node_hidden = (node_pre * node_gate).astype(BF16)
        node_slope = node_gate * (1.0 + node_pre * (1.0 - node_gate))
        node_kept[k, 0] = node_in
        node_kept[k, 1] = node_hidden
        if k == 0:
            first_slope = node_slope
        else:
            stores[1].start()
        table = (table_wide + nt(node_hidden, node_second_wide) + bias_update).astype(BF16)

    for k in (1, 0):
        if k == 1:
            pre_back = nn(slab_land[...], node_second_under) * node_slope
        else:
            grad_low = grad_now.astype(BF16)
            pre_back = nn(grad_low, node_second_wide) * first_slope
        pre_low = pre_back.astype(BF16)
        in_back = nn(pre_low, node_first_wide)
        gm_part = nt(gm_pick, in_back.astype(BF16))
        gm_part = jnp.concatenate([gm_part[0:latent].astype(BF16), two_parts(gm_part[latent:])], axis=0)

        def edge_back(cols):
            both = nn(gm_part, onehot[slab : 2 * slab, cols])
            edge_grad = both[0:latent]
            hidden_grad = both[latent : 2 * latent] + both[2 * latent :]
            if k == 0:
                edge_grad = edge_grad + grad_edge[:, cols]
                hidden_grad = hidden_grad + second_grad_edge[:, cols]
            else:
                grad_edge[:, cols] = edge_grad
            pre_grad = (hidden_grad * slopes[k, :, cols]).astype(BF16)
            back_stack[0:latent, cols] = pre_grad
            back_stack[latent : 2 * latent, cols] = pre_grad
            back_stack[2 * latent : 3 * latent, cols] = edge_grad.astype(BF16)

        chunks(slots, edge_back)

        def weight_terms():
            outer = nt(back_stack[latent : 3 * latent, :], hidden_in[k])
            upper = outer[0:latent, 0:LANES]
            lower = jnp.where(low_half, outer[0:latent, LANES:], outer[latent:, LANES:])
            ones = jnp.ones((8, slots), BF16)
            pre_sums = nt(ones, back_stack[0 : 2 * latent, :])
            edge_sums = nt(ones, back_stack[latent : 3 * latent, :])
            row = lax.broadcasted_iota(jnp.int32, (8, LANES), 0)
            bias_terms = jnp.where(
                low_half,
                0.0,
                jnp.where(row == 0, pre_sums, jnp.where(row == 1, edge_sums, 0.0)),
            )
            return upper, lower, bias_terms

        if k == 0:
            upper, lower, bias_terms = weight_terms()
            grads[0:latent, :] = grads[0:latent, :] + upper
            grads[latent : 2 * latent, :] = grads[latent : 2 * latent, :] + lower

        def node_terms():
            grad_kept[0] = pre_back
            grad_kept[1] = in_back
            if k == 0:
                grad_kept[2] = gained
                grad_mine = grad_own + grad_kept[2, own_rows, :]
            else:
                grad_mine = grad_own
            pre_mine = grad_kept[0, own_rows, :]
            row = lax.broadcasted_iota(jnp.int32, (8, LANES), 0)
            shifted = jnp.where(
                row == 2,
                jnp.sum(pre_mine, axis=0, keepdims=True),
                jnp.where(row == 3, jnp.sum(grad_mine, axis=0, keepdims=True), 0.0),
            )
            return (
                nn(nt(wide_pick, pre_mine.astype(BF16)).astype(BF16), node_kept[k, 0, own_rows, :]),
                nn(nt(wide_pick, grad_mine.astype(BF16)).astype(BF16), node_kept[k, 1, own_rows, :]),
                pltpu.roll(shifted, latent, 1),
                grad_mine + jnp.where(low_half, grad_kept[1, own_rows, :], 0.0),
            )

        if k == 0:
            first_terms, second_terms, node_bias, grad_own = node_terms()
            grads[2 * latent : 3 * latent, :] = grads[2 * latent : 3 * latent, :] + first_terms
            grads[3 * latent : 4 * latent, :] = grads[3 * latent : 4 * latent, :] + second_terms
            bias_at = slice(3 * latent, 3 * latent + 8)
            grads[bias_at, :] = grads[bias_at, :] + bias_terms + node_bias
            for at, (device, spot) in enumerate(plane_peers):
                send(
                    grads.at[pl.ds(pl.multiple_of(spot * shard, shard), shard), :],
                    plane_land.at[pl.ds(at * shard, shard), :],
                    6,
                    device,
                )

        back_send[k] = nt(
            onehot[2 * slab : 2 * slab + 2 * rim, :], back_stack[0 : 2 * latent, :]
        ).astype(BF16)
        send(back_send.at[k, 0:rim], back_land.at[k, 0:rim], 7 + k, (below, layer))
        send(
            back_send.at[k, rim : 2 * rim],
            back_land.at[k, rim : 2 * rim],
            7 + k,
            (above, layer),
        )
        from_source = nt(onehot[0:slab, :], back_stack[0 : 2 * latent, :])
        from_target = nt(onehot[slab : 2 * slab, :], back_stack[0 : 2 * latent, :])
        if k == 0:
            wait_bytes(plane_land, recv_sem.at[6])
            shard_rows = pl.ds(pl.multiple_of(plane_at * shard, shard), shard)
            total = grads[shard_rows, :]
            for turn in range(n_plane - 1):
                total = total + plane_land[turn * shard : (turn + 1) * shard, :]
            z_rows = pl.ds(pl.multiple_of(z_at * shard, shard), shard)
            z_land[z_rows, :] = total
            for peer in z_peers:
                send(z_land.at[z_rows, :], z_land.at[z_rows, :], 9, peer)
        wait_bytes(back_land.at[k], recv_sem.at[7 + k])
        from_source = (
            from_source
            + nn(rim_put[0], back_land[k, 0:rim])
            + nn(rim_put[1], back_land[k, rim : 2 * rim])
        )
        comb = jnp.where(low_half, from_source, from_target).astype(BF16)
        packed = nn(comb[0:half], first_back) + nn(comb[half:], first_back_high)
        if k == 1:
            swap(2, packed)
            upper, lower, bias_terms = weight_terms()
            first_terms, second_terms, node_bias, grad_own = node_terms()
            grads[0:latent, :] = upper
            grads[latent : 2 * latent, :] = lower
            grads[2 * latent : 3 * latent, :] = first_terms
            grads[3 * latent : 4 * latent, :] = second_terms
            bias_at = slice(3 * latent, 3 * latent + 8)
            grads[bias_at, :] = grads[bias_at, :] + bias_terms + node_bias
            node_kept[1, 0] = table
            node_out[...] = node_kept[1, 0, own_rows, 0:latent]
            stores[0].start()

            def carried(cols):
                old = grad_edge[:, cols] + nn(self_back, back_stack[0:latent, cols])
                grad_edge[:, cols] = old
                second_grad_edge[:, cols] = nn(second_back, old.astype(BF16))

            chunks(slots, carried)
            cot_slab = pltpu.roll(slab_land[...].astype(F32), latent, 1)
            grad_before = jnp.where(low_half, cot_slab + in_back, 0.0)
            packed = swapped_sum(2)
            gained = jnp.concatenate(
                [
                    jnp.where(low_half, packed, 0.0),
                    jnp.where(low_half, pltpu.roll(packed, latent, 1), 0.0),
                ],
                axis=0,
            )
            grad_now = grad_before + gained
        else:
            comb_send[...] = packed.astype(BF16)

            def rows_of(device):
                return pl.ds(pl.multiple_of(lax.rem(device, n_layer // 2) * hits, hits), hits)

            for at, peer in enumerate(layer_peers):
                send(
                    comb_send.at[rows_of(peer), :],
                    comb_land.at[pl.ds(at * hits, hits), :],
                    10,
                    (phi, peer),
                )
            wait_bytes(z_land.at[pl.ds(0, (n_z - 1) * shard), :], recv_sem.at[9])
            total = z_land[0:shard, :]
            for turn in range(1, n_z):
                total = total + z_land[turn * shard : (turn + 1) * shard, :]
            grads_sum[shard_rows, :] = total
            for device, _ in plane_peers:
                send(grads_sum.at[shard_rows, :], grads_sum.at[shard_rows, :], 11, device)
            wait_bytes(comb_land, recv_sem.at[10])
            total = comb_send[rows_of(layer), :].astype(F32)
            for turn in range(n_layer - 1):
                total = total + comb_land[turn * hits : (turn + 1) * hits, :].astype(F32)
            total = jnp.where(layer < n_layer // 2, total, pltpu.roll(total, latent, 1))
            node_grad[...] = (grad_own + total)[:, 0:latent]
            stores[2].start()

    wait_bytes(grads_sum.at[pl.ds(0, (n_plane - 1) * shard), :], recv_sem.at[11])
    grad_first[:, 0:LANES] = grads_sum[0:latent, :]
    grad_first[:, LANES:] = grads_sum[latent : 2 * latent, 0:latent]
    grad_second[...] = pltpu.roll(grads_sum[latent : 2 * latent, :], latent, 1)[:, 0:latent]
    grad_node_first[...] = grads_sum[2 * latent : 3 * latent, :]
    grad_node_second[...] = grads_sum[3 * latent : 4 * latent, 0:latent]
    grad_biases[...] = pltpu.roll(grads_sum[3 * latent : 3 * latent + 8, :], latent, 1)[
        0:4, 0:latent
    ]
    for store in stores[3:]:
        store.start()

    wait_bytes(slab_land.at[pl.ds(0, slab - hits), :], send_sem.at[0])
    for k in range(2):
        wait_bytes(rim_send.at[k], send_sem.at[1 + k])
        wait_bytes(back_send.at[k], send_sem.at[7 + k])
    for at in range(3):
        wait_bytes(swaps[at].at[pl.ds(0, (n_layer - 1) * half), :], send_sem.at[3 + at])
    wait_bytes(plane_land, send_sem.at[6])
    wait_bytes(z_land.at[pl.ds(0, (n_z - 1) * shard), :], send_sem.at[9])
    wait_bytes(comb_land, send_sem.at[10])
    wait_bytes(grads_sum.at[pl.ds(0, (n_plane - 1) * shard), :], send_sem.at[11])
    for store in stores:
        store.wait()


def deliver(many, *refs):
    sources, targets, held = refs[:many], refs[many : 2 * many], refs[2 * many : 3 * many]
    in_sem, out_sem = refs[3 * many :]
    loads = [
        pltpu.make_async_copy(sources[at], held[at], in_sem.at[at]) for at in range(many)
    ]
    stores = [
        pltpu.make_async_copy(held[at], targets[at], out_sem.at[at]) for at in range(many)
    ]
    for load in loads:
        load.start()
    for load, store in zip(loads, stores):
        load.wait()
        store.start()
    for store in stores:
        store.wait()


def body(n_phi, n_layer, *arrays):
    node_feats, edge_feats, edge_source, edge_target, *others, node_cot = arrays
    latent, hits = node_feats.shape
    slots = edge_feats.shape[1]
    slab = hits * n_layer
    rim = others[1].shape[1]
    n_plane = Y_LO * CORES * n_layer
    n_z = n_phi // (Y_LO * CORES)
    grad_rows = 4 * latent
    shard = grad_rows // n_plane
    hbm = pl.BlockSpec(memory_space=pltpu.HBM)
    operands = (
        node_feats.T,
        edge_feats,
        edge_source.reshape(1, slots),
        edge_target.reshape(1, slots),
        *others,
        node_cot.T,
    )
    outs = [
        jax.ShapeDtypeStruct(*out)
        for out in (
            ((hits, latent), BF16),
            ((latent, slots), BF16),
            ((hits, latent), F32),
            ((latent, 3 * latent), F32),
            ((latent, latent), F32),
            ((latent, 2 * latent), F32),
            ((latent, latent), F32),
            ((4, latent), F32),
        )
    ]
    results = pl.pallas_call(
        functools.partial(kernel, n_phi, n_layer),
        out_shape=outs,
        in_specs=[hbm] * len(operands),
        out_specs=[hbm] * len(outs),
        scratch_shapes=[pltpu.VMEM(array.shape, array.dtype) for array in (*operands, *outs)]
        + [
            pltpu.VMEM((2 * slab + 2 * rim, slots), BF16),
            pltpu.VMEM((2 * rim, slab), BF16),
            pltpu.VMEM((2, slab, rim), BF16),
            pltpu.VMEM((2, 4 * latent, slots), BF16),
            pltpu.VMEM((2, 2 * latent, slots), BF16),
            pltpu.VMEM((latent, slots), F32),
            pltpu.VMEM((2, latent, slots), F32),
            pltpu.VMEM((latent, slots), F32),
            pltpu.VMEM((latent, slots), F32),
            pltpu.VMEM((3 * latent, slots), BF16),
            pltpu.VMEM((2, 2, slab, LANES), BF16),
            pltpu.VMEM((3, slab, LANES), F32),
            pltpu.VMEM((hits, LANES), BF16),
            pltpu.VMEM((slab, LANES), BF16),
            pltpu.VMEM((2, 2 * rim, LANES), BF16),
            pltpu.VMEM((2, 2 * rim, LANES), BF16),
            pltpu.VMEM((n_layer * slab // 2, LANES), F32),
            pltpu.VMEM((2, n_layer * slab // 2, LANES), BF16),
            pltpu.VMEM((2, 2 * rim, LANES), BF16),
            pltpu.VMEM((2, 2 * rim, LANES), BF16),
            pltpu.VMEM((slab // 2, LANES), BF16),
            pltpu.VMEM(((n_layer - 1) * hits, LANES), BF16),
            pltpu.VMEM((grad_rows, LANES), F32),
            pltpu.VMEM(((n_plane - 1) * shard, LANES), F32),
            pltpu.VMEM((n_z * shard, LANES), F32),
            pltpu.VMEM((grad_rows, LANES), F32),
            pltpu.SemaphoreType.DMA((len(operands),)),
            pltpu.SemaphoreType.DMA((len(outs),)),
            pltpu.SemaphoreType.REGULAR((3,)),
            pltpu.SemaphoreType.DMA((12,)),
            pltpu.SemaphoreType.DMA((12,)),
        ],
        compiler_params=pltpu.CompilerParams(
            collective_id=0, has_side_effects=True, vmem_limit_bytes=VMEM_BYTES
        ),
    )(*operands)
    node_out, edge_out, node_grad, *totals = pl.pallas_call(
        functools.partial(deliver, len(outs)),
        out_shape=outs,
        in_specs=[hbm] * len(outs),
        out_specs=[hbm] * len(outs),
        scratch_shapes=[pltpu.VMEM(out.shape, out.dtype) for out in outs]
        + [pltpu.SemaphoreType.DMA((len(outs),))] * 2,
        compiler_params=pltpu.CompilerParams(vmem_limit_bytes=VMEM_BYTES),
    )(*results)
    return node_out.T, edge_out, node_grad.T, *totals


def solution(mesh):
    split = P(None, ("phi", "layer"))
    return jax.shard_map(
        functools.partial(body, mesh.shape["phi"], mesh.shape["layer"]),
        mesh=mesh,
        in_specs=(
            split,
            split,
            P(("phi", "layer")),
            P(("phi", "layer")),
            P("phi", "layer"),
            P("phi", None),
            P("phi", None),
            P(),
            P(),
            P(),
            P(),
            P(),
            split,
        ),
        out_specs=(split, split, split, P(), P(), P(), P(), P()),
        check_vma=False,
    )
```

```python
import functools
import itertools

import jax
import jax.numpy as jnp
from jax import lax
from jax.experimental import pallas as pl
from jax.experimental.pallas import tpu as pltpu
from jax.sharding import PartitionSpec as P

MESH = pl.DeviceIdType.MESH
BF16 = jnp.bfloat16
F32 = jnp.float32
LANES = 128
Y_LO = 2
CORES = 2
CHUNK = 512
VMEM_BYTES = 64 * 1024 * 1024


def nn(left, right):
    return lax.dot_general(left, right, (((1,), (0,)), ((), ())), preferred_element_type=F32)


def nt(left, right):
    return lax.dot_general(left, right, (((1,), (1,)), ((), ())), preferred_element_type=F32)


def nt_exact(left, right):
    return lax.dot_general(
        left,
        right,
        (((1,), (1,)), ((), ())),
        precision=lax.Precision.HIGHEST,
        preferred_element_type=F32,
    )


def pick(rows, cols, row_shift, col_limit, dtype=BF16):
    row = lax.broadcasted_iota(jnp.int32, (rows, cols), 0)
    col = lax.broadcasted_iota(jnp.int32, (rows, cols), 1)
    return jnp.where((row == col + row_shift) & (col < col_limit), 1.0, 0.0).astype(dtype)


def two_parts(value):
    main = value.astype(BF16)
    return jnp.concatenate([main, (value - main.astype(F32)).astype(BF16)], axis=0)


def logistic(value):
    return 0.5 * jnp.tanh(0.5 * value) + 0.5


def chunks(total, step):
    size = min(CHUNK, total)

    def run(turn, carry):
        step(pl.ds(pl.multiple_of(turn * size, size), size))
        return carry

    lax.fori_loop(0, total // size, run, 0, unroll=True)


def wait_bytes(ref, sem):
    pltpu.make_async_copy(ref, ref, sem).wait()


def far_first(sizes):
    steps = list(itertools.product(*(range(size) for size in sizes)))
    hops = lambda step: sum(min(at, size - at) for at, size in zip(step, sizes))
    return sorted(steps[1:], key=hops, reverse=True)


def kernel(
    n_phi,
    n_layer,
    feats_in,
    edges_in,
    source_in,
    target_in,
    count_in,
    rim_up_in,
    rim_down_in,
    first_in,
    second_in,
    node_first_in,
    node_second_in,
    biases_in,
    cot_in,
    node_out_to,
    edge_out_to,
    node_grad_to,
    grad_first_to,
    grad_second_to,
    grad_node_first_to,
    grad_node_second_to,
    grad_biases_to,
    feats,
    edges0,
    source,
    target,
    count,
    rim_up,
    rim_down,
    first,
    second,
    node_first,
    node_second,
    biases,
    cot,
    node_out,
    edge_out,
    node_grad,
    grad_first,
    grad_second,
    grad_node_first,
    grad_node_second,
    grad_biases,
    onehot,
    rim_pick,
    rim_put,
    hidden_in,
    edge_new,
    z_part,
    slopes,
    grad_edge,
    second_grad_edge,
    back_stack,
    bias_sums,
    node_kept,
    grad_kept,
    own_send,
    slab_land,
    table_kept,
    rim_near,
    near_pick,
    near_land,
    pairs_land,
    rim_send,
    rim_land,
    message_send,
    message_land,
    swap_land,
    back_send,
    back_land,
    comb_send,
    comb_land,
    grads,
    plane_land,
    z_land,
    grads_sum,
    load_sem,
    store_sem,
    chain_sem,
    send_sem,
    recv_sem,
):
    hits, latent = feats.shape
    slots = edges0.shape[1]
    slab = hits * n_layer
    half = slab // 2
    rim = rim_up.shape[1]
    n_z = n_phi // (Y_LO * CORES)
    n_plane = Y_LO * CORES * n_layer
    n_x = n_layer // 2
    n_y = 2 * Y_LO
    shard = grads.shape[0] // n_plane
    phi = lax.axis_index("phi")
    layer = lax.axis_index("layer")
    core = lax.rem(phi, CORES)
    z_at = lax.rem(lax.div(phi, CORES), n_z)
    y_lo = lax.div(phi, CORES * n_z)
    y_hi = lax.div(layer, n_x)
    x_at = lax.rem(layer, n_x)
    y_at = y_hi * Y_LO + y_lo
    plane_at = (y_lo * CORES + core) * n_layer + layer
    above = lax.rem(phi + 1, n_phi)
    below = lax.rem(phi + n_phi - 1, n_phi)

    x_of = [lax.rem(x_at + step, n_x) for step in range(n_x)]
    y_hi_of = [lax.rem(y_hi + step, 2) * n_x for step in range(2)]
    layer_peers = [
        y_hi_of[dy // Y_LO] + x_of[dx]
        for dy, dx in far_first((n_y, n_x))
        if dy % Y_LO == 0
    ]
    y_of = [lax.rem(y_at + step, n_y) for step in range(n_y)]
    pair_of = [lax.rem(y, Y_LO) * CORES for y in y_of]
    phi_base = [lax.rem(y, Y_LO) * (CORES * n_z) + z_at * CORES for y in y_of]
    layer_base = [lax.div(y, Y_LO) * n_x for y in y_of]
    core_of = [core, 1 - core]
    plane_peers = []
    for dy, dx, dc in far_first((n_y, n_x, CORES)):
        device = (phi_base[dy] + core_of[dc], layer_base[dy] + x_of[dx])
        plane_peers.append((device, (pair_of[dy] + core_of[dc]) * n_layer + device[1]))
    z_peers = [
        (y_lo * (CORES * n_z) + lax.rem(z_at + step, n_z) * CORES + core, layer)
        for (step,) in far_first((n_z,))
    ]

    def send(src, dst, step, device):
        pltpu.make_async_remote_copy(
            src_ref=src,
            dst_ref=dst,
            send_sem=send_sem.at[step],
            recv_sem=recv_sem.at[step],
            device_id=device,
            device_id_type=MESH,
        ).start()

    barrier = pltpu.get_barrier_semaphore()

    def along_z(step):
        return y_lo * (CORES * n_z) + lax.rem(z_at + step + n_z, n_z) * CORES + core, layer

    def greet(sem, devices):
        for device in devices:
            pl.semaphore_signal(sem, inc=1, device_id=device, device_id_type=MESH)

    greeted = [(phi, peer) for peer in layer_peers] + [
        (phi_base[0] + 1 - core, layer),
        (phi_base[0] + (1 - 2 * y_lo) * (CORES * n_z) + core, layer),
        (phi_base[0] + (1 - 2 * y_lo) * (CORES * n_z) + 1 - core, layer),
        (above, layer),
        (below, layer),
        along_z(1),
        along_z(-1),
    ]
    loads = [
        pltpu.make_async_copy(src, dst, load_sem.at[at])
        for at, (src, dst) in enumerate(
            (
                (feats_in, feats),
                (cot_in, cot),
                (first_in, first),
                (biases_in, biases),
                (second_in, second),
                (node_first_in, node_first),
                (node_second_in, node_second),
                (count_in, count),
                (source_in, source),
                (target_in, target),
                (rim_up_in, rim_up),
                (rim_down_in, rim_down),
                (edges_in, edges0),
            )
        )
    ]
    for load in loads[:2]:
        load.start()
    greet(barrier, greeted)
    for load in loads[2:]:
        load.start()

    lane = lax.broadcasted_iota(jnp.int32, (1, LANES), 1)
    low_half = lane < latent
    own_rows = pl.ds(pl.multiple_of(layer * hits, hits), hits)
    swap_rows = pl.ds(pl.multiple_of(layer * half, half), half)

    loads[0].wait()
    loads[1].wait()
    wide_pick = pick(latent, LANES, 0, latent)
    high_pick = pick(latent, LANES, -latent, LANES)
    own_send[...] = (
        nn(feats[...], wide_pick) + nn(cot[...].astype(BF16), high_pick)
    ).astype(BF16)
    pl.semaphore_wait(barrier, len(greeted))
    known = [step for step in (1, 2, 4) if step < n_z // 2]

    def tell(at):
        if at < len(known):
            greet(chain_sem.at[at], [along_z(known[at]), along_z(-known[at])])

    def told(at):
        if at < len(known):
            pl.semaphore_wait(chain_sem.at[at], 2)

    tell(0)
    for peer in layer_peers:
        send(own_send, slab_land.at[own_rows, :], 0, (phi, peer))
    slab_land[own_rows, :] = own_send[...]
    send(rim_up_in, rim_near.at[0], 2, (above, layer))
    send(rim_down_in, rim_near.at[1], 2, (below, layer))

    stores = [
        pltpu.make_async_copy(src, dst, store_sem.at[at])
        for at, (src, dst) in enumerate(
            (
                (node_out, node_out_to),
                (edge_out, edge_out_to),
                (node_grad, node_grad_to),
                (grad_first, grad_first_to),
                (grad_second, grad_second_to),
                (grad_node_first, grad_node_first_to),
                (grad_node_second, grad_node_second_to),
                (grad_biases, grad_biases_to),
            )
        )
    ]
    swaps = (None, swap_land.at[0], swap_land.at[1])
    x_rows = pl.ds(pl.multiple_of(x_at * hits, hits), hits)
    lower_x_rows = pl.ds(pl.multiple_of(half + x_at * hits, hits), hits)
    pair_rows = pl.ds(pl.multiple_of(x_at * 2 * hits, 2 * hits), 2 * hits)

    def in_order(pairs):
        parts = [
            pairs[(2 * x + side) * hits : (2 * x + side + 1) * hits]
            for side in range(2)
            for x in range(n_x)
        ]
        return jnp.concatenate(parts, axis=0)

    def swap(at, value):
        swaps[at][swap_rows, :] = value.astype(swaps[at].dtype)
        mine = swaps[at].at[swap_rows, :]
        for peer in layer_peers:
            send(mine, mine, 3 + at, (phi, peer))

    def swapped_sum(at):
        wait_bytes(swaps[at].at[pl.ds(0, (n_layer - 1) * half), :], recv_sem.at[3 + at])
        total = swaps[at][0:half, :].astype(F32)
        for turn in range(1, n_layer):
            total = total + swaps[at][turn * half : (turn + 1) * half, :].astype(F32)
        return total

    for load in loads[2:7]:
        load.wait()
    edge_first = first[...]
    source_wide = nn(edge_first, pick(3 * latent, LANES, 0, latent)).astype(BF16)
    target_wide = nn(edge_first, pick(3 * latent, LANES, latent, latent)).astype(BF16)
    source_high = nn(edge_first, pick(3 * latent, LANES, -latent, LANES) * (~low_half).astype(BF16)).astype(BF16)
    target_high = nn(edge_first, pick(3 * latent, LANES, 0, LANES) * (~low_half).astype(BF16)).astype(BF16)
    first_self = edge_first[:, 2 * latent :]
    edge_second = second[...]
    square_eye = pick(latent, latent, 0, latent)
    self_back = nt(square_eye, first_self).astype(BF16)
    second_back = nt(square_eye, edge_second).astype(BF16)
    zero_square = jnp.zeros((latent, latent), BF16)
    gm_pick = jnp.concatenate(
        [
            high_pick,
            nt(square_eye, jnp.concatenate([zero_square, edge_second], axis=0)).astype(BF16),
        ],
        axis=0,
    )
    first_back = jnp.concatenate([source_wide, target_wide], axis=0)
    first_back_high = jnp.concatenate([source_high, target_high], axis=0)
    node_first_wide = jnp.concatenate(
        [node_first[...], jnp.zeros((LANES - latent, 2 * latent), BF16)], axis=0
    )
    gm_back = nt(gm_pick, node_first_wide)
    gm_back = jnp.concatenate([gm_back[0:latent].astype(BF16), two_parts(gm_back[latent:])], axis=0)
    node_second_low = nn(node_second[...], wide_pick).astype(BF16)
    zero_wide = jnp.zeros((LANES - latent, LANES), BF16)
    node_second_wide = jnp.concatenate([node_second_low, zero_wide], axis=0)
    node_second_under = jnp.concatenate([zero_wide, node_second_low], axis=0)
    bias_rows = lax.dot_general(
        biases[...],
        pick(latent, LANES, 0, latent, F32),
        (((1,), (0,)), ((), ())),
        precision=lax.Precision.HIGHEST,
        preferred_element_type=F32,
    )
    bias_cols = nt_exact(pick(latent, latent, 0, latent, F32), biases[...])
    bias_edge = bias_cols[:, 0:1]
    bias_message = bias_cols[:, 1:2]
    bias_node = bias_rows[2:3, :]
    bias_update = bias_rows[3:4, :]
    for load in loads[7:]:
        load.wait()

    def build(cols):
        width = cols.size
        spot = lax.broadcasted_iota(jnp.int32, (1, width), 1) + cols.start
        here = spot < count[...]
        source_at = jnp.where(here, source[:, cols], -1)
        target_at = jnp.where(here, target[:, cols], -1)
        row = lax.broadcasted_iota(jnp.int32, (slab, width), 0)
        onehot[0:slab, cols] = jnp.where(row == source_at, 1.0, 0.0).astype(BF16)
        onehot[slab : 2 * slab, cols] = jnp.where(row == target_at, 1.0, 0.0).astype(BF16)
        rim_row = lax.broadcasted_iota(jnp.int32, (2 * rim, width), 0) + slab
        onehot[2 * slab : 2 * slab + 2 * rim, cols] = jnp.where(
            rim_row == source_at, 1.0, 0.0
        ).astype(BF16)
        z_part[:, cols] = nn(first_self, edges0[:, cols]) + bias_edge

    chunks(slots, build)
    rim_eye = pick(rim, rim, 0, rim)
    for side, index in enumerate((rim_up, rim_down)):
        put = jnp.where(
            lax.broadcasted_iota(jnp.int32, (slab, rim), 0) == index[...], 1.0, 0.0
        ).astype(BF16)
        rim_put[side] = put
        rim_pick[side * rim : (side + 1) * rim, :] = nt(rim_eye, put).astype(BF16)
    grad_own = lax.dot_general(
        cot[...],
        pick(latent, LANES, 0, latent, F32),
        (((1,), (0,)), ((), ())),
        precision=lax.Precision.HIGHEST,
        preferred_element_type=F32,
    )

    wait_bytes(slab_land.at[pl.ds(0, slab - hits), :], recv_sem.at[0])
    told(0)
    tell(1)
    table = jnp.where(low_half, slab_land[...].astype(F32), 0.0).astype(BF16)
    rim_send[...] = nn(rim_pick[...], table).astype(BF16)
    send(rim_send.at[0:rim], rim_land.at[0, 0:rim], 1, (above, layer))
    send(rim_send.at[rim : 2 * rim], rim_land.at[0, rim : 2 * rim], 1, (below, layer))
    table_kept[...] = table
    for k in range(2):
        own_part = two_parts(
            jnp.concatenate([nt(source_wide, table), nt(target_wide, table)], axis=1)
        )

        def own_terms(cols):
            terms = nn(own_part, onehot[0 : 2 * slab, cols])
            z_part[:, cols] = z_part[:, cols] + (terms[0:latent] + terms[latent:])

        chunks(slots, own_terms)
        if k == 0:
            wait_bytes(rim_land.at[0], recv_sem.at[1])
        else:
            wait_bytes(near_land, recv_sem.at[13])
            for side in range(2):
                rim_land[1, side * rim : (side + 1) * rim, :] = nn(
                    near_pick[side * rim : (side + 1) * rim, :], near_land[side]
                ).astype(BF16)
        rim_part = two_parts(nt(source_wide, rim_land[k]))

        def edge_mlp(cols):
            width = cols.size
            terms = nn(rim_part, onehot[2 * slab : 2 * slab + 2 * rim, cols])
            pre = z_part[:, cols] + (terms[0:latent] + terms[latent:])
            gate = logistic(pre)
            hidden = (pre * gate).astype(BF16)
            hidden_in[k, 3 * latent : 4 * latent, cols] = hidden
            slopes[k, :, cols] = gate * (1.0 + pre * (1.0 - gate))
            old = edges0[:, cols] if k == 0 else edge_new[0, 0:latent, cols]
            here = lax.broadcasted_iota(jnp.int32, (1, width), 1) + cols.start < count[...]
            fresh = jnp.where(
                here, old.astype(F32) + nn(edge_second, hidden) + bias_message, 0.0
            ).astype(BF16)
            edge_new[k, 0:latent, cols] = fresh
            edge_new[k, latent : 2 * latent, cols] = fresh

        chunks(slots, edge_mlp)
        both_halves = nt(onehot[slab : 2 * slab, :], edge_new[k])
        packed = jnp.where(low_half, both_halves[0:half], both_halves[half:])
        if k == 0:
            message_send[...] = packed
            for peer in layer_peers:
                spot = pl.ds(pl.multiple_of(lax.rem(peer, n_x) * hits, hits), hits)
                send(message_send.at[spot, :], message_land.at[own_rows, :], 3, (phi, peer))
            message_land[own_rows, :] = message_send[x_rows, :]
            wait_bytes(rim_near, recv_sem.at[2])
            row = lax.broadcasted_iota(jnp.int32, (slab, rim), 0)
            pair_row = lax.rem(row, 2 * hits)
            hit = (
                lax.div(row, 2 * hits) * hits
                + lax.rem(pair_row, hits)
                + lax.div(pair_row, hits) * half
            )
            for side in range(2):
                put = jnp.where(hit == rim_near[side], 1.0, 0.0).astype(BF16)
                near_pick[side * rim : (side + 1) * rim, :] = nt(rim_eye, put).astype(BF16)
        else:
            swap(k, packed)

        raw_own = nt(wide_pick, table).astype(BF16)
        raw_rim = nt(wide_pick, rim_land[k]).astype(BF16)

        def inputs(cols):
            hidden_in[k, 0:latent, cols] = (
                nn(raw_own, onehot[0:slab, cols])
                + nn(raw_rim, onehot[2 * slab : 2 * slab + 2 * rim, cols])
            ).astype(BF16)
            hidden_in[k, latent : 2 * latent, cols] = nn(
                raw_own, onehot[slab : 2 * slab, cols]
            ).astype(BF16)
            if k == 0:
                old = edges0[:, cols]
                z_part[:, cols] = nn(first_self, edge_new[0, 0:latent, cols]) + bias_edge
            else:
                old = edge_new[0, 0:latent, cols]
                edge_out[:, cols] = edge_new[1, 0:latent, cols]
            hidden_in[k, 2 * latent : 3 * latent, cols] = old

        chunks(slots, inputs)
        if k == 0:
            wait_bytes(message_land.at[pl.ds(0, (n_layer - 1) * hits), :], recv_sem.at[3])
            packed = message_land[0:hits, :]
            for turn in range(1, n_layer):
                packed = packed + message_land[turn * hits : (turn + 1) * hits, :]
            upper_old = table_kept[x_rows, :].astype(F32)
            lower_old = table_kept[lower_x_rows, :].astype(F32)
        else:
            packed = swapped_sum(k)
            table_wide = table.astype(F32)
            upper_old, lower_old = table_wide[0:half], table_wide[half:]
        told(1 + k)
        if k == 0:
            tell(2)
        node_old = jnp.concatenate([upper_old, lower_old], axis=0)
        node_in = jnp.concatenate(
            [
                jnp.where(low_half, upper_old, pltpu.roll(packed, latent, 1)),
                jnp.where(low_half, lower_old, packed),
            ],
            axis=0,
        ).astype(BF16)
        node_pre = nt(node_in, node_first_wide) + bias_node
        node_gate = logistic(node_pre)
        node_hidden = (node_pre * node_gate).astype(BF16)
        node_slope = node_gate * (1.0 + node_pre * (1.0 - node_gate))
        table = (node_old + nt(node_hidden, node_second_wide) + bias_update).astype(BF16)
        if k == 0:
            turned = pltpu.roll(node_slope, latent, 1)
            pairs_land[pair_rows, :] = jnp.where(low_half, table.astype(F32), turned).astype(BF16)
            mine = pairs_land.at[pair_rows, :]
            for side, slab_at in enumerate((above, below)):
                for x in x_of:
                    send(mine, near_land.at[side, pair_rows, :], 13, (slab_at, y_hi * n_x + x))
            for (step,) in far_first((n_x,)):
                send(mine, mine, 12, (phi, y_hi * n_x + x_of[step]))
            node_kept[0, 0, 0 : 2 * hits] = node_in
            node_kept[0, 1, 0 : 2 * hits] = node_hidden
            if n_x > 1:
                wait_bytes(pairs_land.at[pl.ds(0, (n_x - 1) * 2 * hits), :], recv_sem.at[12])
            gathered = in_order(pairs_land[...].astype(F32))
            table = jnp.where(low_half, gathered, 0.0).astype(BF16)
            first_slope = pltpu.roll(gathered, latent, 1)
        else:
            node_kept[1, 0] = node_in
            node_kept[1, 1] = node_hidden
            stores[1].start()

    for k in (1, 0):
        if k == 1:
            pre_back = nn(slab_land[...], node_second_under) * node_slope
        else:
            grad_low = grad_now.astype(BF16)
            pre_back = nn(grad_low, node_second_wide) * first_slope
        pre_low = pre_back.astype(BF16)
        in_back = nn(pre_low, node_first_wide)
        gm_part = nt(gm_back, pre_low)
        gm_part = jnp.concatenate(
            [
                gm_part[0:latent].astype(BF16),
                two_parts(gm_part[latent : 2 * latent] + gm_part[2 * latent :]),
            ],
            axis=0,
        )

        if k == 1:
            bias_sums[...] = jnp.zeros_like(bias_sums)

        def folded(value):
            pieces = [
                value[:, at : at + LANES] for at in range(0, value.shape[1], LANES)
            ]
            return functools.reduce(lambda one, other: one + other, pieces)

        def edge_back(cols):
            both = nn(gm_part, onehot[slab : 2 * slab, cols])
            edge_grad = both[0:latent]
            hidden_grad = both[latent : 2 * latent] + both[2 * latent :]
            if k == 0:
                edge_grad = edge_grad + grad_edge[:, cols]
                hidden_grad = hidden_grad + second_grad_edge[:, cols]
            else:
                grad_edge[:, cols] = edge_grad
            pre_grad = hidden_grad * slopes[k, :, cols]
            bias_sums[0] = bias_sums[0] + folded(pre_grad)
            bias_sums[1] = bias_sums[1] + folded(edge_grad)
            pre_grad = pre_grad.astype(BF16)
            back_stack[0:latent, cols] = pre_grad
            back_stack[latent : 2 * latent, cols] = pre_grad
            back_stack[2 * latent : 3 * latent, cols] = edge_grad.astype(BF16)

        chunks(slots, edge_back)

        def weight_terms():
            outer = nt(back_stack[latent : 3 * latent, :], hidden_in[k])
            upper = outer[0:latent, 0:LANES]
            lower = jnp.where(low_half, outer[0:latent, LANES:], outer[latent:, LANES:])
            return upper, lower

        def column_at(at, sums):
            return jnp.where(lane == latent + at, jnp.sum(sums, axis=1, keepdims=True), 0.0)

        if k == 0:
            upper, lower = weight_terms()
            grads[0:latent, :] = grads[0:latent, :] + upper
            grads[latent : 2 * latent, :] = grads[latent : 2 * latent, :] + lower

        def node_terms():
            kept_rows = (
                pl.ds(pl.multiple_of(y_hi * hits, hits), hits) if k == 0 else own_rows
            )
            grad_kept[0] = pre_back
            grad_kept[1] = in_back
            if k == 0:
                grad_kept[2] = gained
                grad_mine = grad_own + grad_kept[2, own_rows, :]
            else:
                grad_mine = grad_own
            pre_mine = grad_kept[0, own_rows, :]
            pre_turned = nt(wide_pick, pre_mine.astype(BF16))
            grad_turned = nt(wide_pick, grad_mine.astype(BF16))
            return (
                nn(pre_turned.astype(BF16), node_kept[k, 0, kept_rows, :]),
                nn(grad_turned.astype(BF16), node_kept[k, 1, kept_rows, :])
                + column_at(2, pre_turned)
                + column_at(3, grad_turned),
                grad_mine + jnp.where(low_half, grad_kept[1, own_rows, :], 0.0),
            )

        if k == 0:
            first_terms, second_terms, grad_own = node_terms()
            grads[2 * latent : 3 * latent, :] = grads[2 * latent : 3 * latent, :] + first_terms
            grads[3 * latent : 4 * latent, :] = (
                grads[3 * latent : 4 * latent, :]
                + second_terms
                + column_at(0, bias_sums[0])
                + column_at(1, bias_sums[1])
            )
            for at, (device, spot) in enumerate(plane_peers):
                send(
                    grads.at[pl.ds(pl.multiple_of(spot * shard, shard), shard), :],
                    plane_land.at[pl.ds(at * shard, shard), :],
                    6,
                    device,
                )

        back_send[k] = nt(
            onehot[2 * slab : 2 * slab + 2 * rim, :], back_stack[0 : 2 * latent, :]
        ).astype(BF16)
        send(back_send.at[k, 0:rim], back_land.at[k, 0:rim], 7 + k, (below, layer))
        send(
            back_send.at[k, rim : 2 * rim],
            back_land.at[k, rim : 2 * rim],
            7 + k,
            (above, layer),
        )
        from_source = nt(onehot[0:slab, :], back_stack[0 : 2 * latent, :])
        from_target = nt(onehot[slab : 2 * slab, :], back_stack[0 : 2 * latent, :])
        if k == 0:
            wait_bytes(plane_land, recv_sem.at[6])
            shard_rows = pl.ds(pl.multiple_of(plane_at * shard, shard), shard)
            total = grads[shard_rows, :]
            for turn in range(n_plane - 1):
                total = total + plane_land[turn * shard : (turn + 1) * shard, :]
            z_rows = pl.ds(pl.multiple_of(z_at * shard, shard), shard)
            z_land[z_rows, :] = total
            for peer in z_peers:
                send(z_land.at[z_rows, :], z_land.at[z_rows, :], 9, peer)
        wait_bytes(back_land.at[k], recv_sem.at[7 + k])
        from_source = (
            from_source
            + nn(rim_put[0], back_land[k, 0:rim])
            + nn(rim_put[1], back_land[k, rim : 2 * rim])
        )
        comb = jnp.where(low_half, from_source, from_target).astype(BF16)
        packed = nn(comb[0:half], first_back) + nn(comb[half:], first_back_high)
        if k == 1:
            swap(2, packed)
            upper, lower = weight_terms()
            first_terms, second_terms, grad_own = node_terms()
            grads[0:latent, :] = upper
            grads[latent : 2 * latent, :] = lower
            grads[2 * latent : 3 * latent, :] = first_terms
            grads[3 * latent : 4 * latent, :] = second_terms
            node_kept[1, 0] = table
            node_out[...] = node_kept[1, 0, own_rows, 0:latent]
            stores[0].start()

            def carried(cols):
                old = grad_edge[:, cols] + nn(self_back, back_stack[0:latent, cols])
                grad_edge[:, cols] = old
                second_grad_edge[:, cols] = nn(second_back, old.astype(BF16))

            chunks(slots, carried)
            cot_slab = pltpu.roll(slab_land[...].astype(F32), latent, 1)
            grad_before = jnp.where(low_half, cot_slab + in_back, 0.0)
            packed = swapped_sum(2)
            gained = jnp.concatenate(
                [
                    jnp.where(low_half, packed, 0.0),
                    jnp.where(low_half, pltpu.roll(packed, latent, 1), 0.0),
                ],
                axis=0,
            )
            grad_now = grad_before + gained
        else:
            comb_send[...] = packed.astype(BF16)

            def rows_of(device):
                return pl.ds(pl.multiple_of(lax.rem(device, n_layer // 2) * hits, hits), hits)

            for at, peer in enumerate(layer_peers):
                send(
                    comb_send.at[rows_of(peer), :],
                    comb_land.at[pl.ds(at * hits, hits), :],
                    10,
                    (phi, peer),
                )
            wait_bytes(z_land.at[pl.ds(0, (n_z - 1) * shard), :], recv_sem.at[9])
            total = z_land[0:shard, :]
            for turn in range(1, n_z):
                total = total + z_land[turn * shard : (turn + 1) * shard, :]
            grads_sum[shard_rows, :] = total
            for device, _ in plane_peers:
                send(grads_sum.at[shard_rows, :], grads_sum.at[shard_rows, :], 11, device)
            wait_bytes(comb_land, recv_sem.at[10])
            total = comb_send[rows_of(layer), :].astype(F32)
            for turn in range(n_layer - 1):
                total = total + comb_land[turn * hits : (turn + 1) * hits, :].astype(F32)
            total = jnp.where(layer < n_layer // 2, total, pltpu.roll(total, latent, 1))
            node_grad[...] = (grad_own + total)[:, 0:latent]
            stores[2].start()

    wait_bytes(grads_sum.at[pl.ds(0, (n_plane - 1) * shard), :], recv_sem.at[11])
    grad_first[:, 0:LANES] = grads_sum[0:latent, :]
    grad_first[:, LANES:] = grads_sum[latent : 2 * latent, 0:latent]
    grad_second[...] = pltpu.roll(grads_sum[latent : 2 * latent, :], latent, 1)[:, 0:latent]
    grad_node_first[...] = grads_sum[2 * latent : 3 * latent, :]
    grad_node_second[...] = grads_sum[3 * latent : 4 * latent, 0:latent]
    grad_biases[...] = grads_sum[3 * latent : 4 * latent, :].T[latent : latent + 4, :]
    for store in stores[3:]:
        store.start()

    wait_bytes(slab_land.at[pl.ds(0, slab - hits), :], send_sem.at[0])
    wait_bytes(rim_send, send_sem.at[1])
    wait_bytes(rim_near, send_sem.at[2])
    wait_bytes(message_land.at[pl.ds(0, (n_layer - 1) * hits), :], send_sem.at[3])
    if n_x > 1:
        wait_bytes(pairs_land.at[pl.ds(0, (n_x - 1) * 2 * hits), :], send_sem.at[12])
    wait_bytes(near_land, send_sem.at[13])
    for k in range(2):
        wait_bytes(back_send.at[k], send_sem.at[7 + k])
    for at in range(1, 3):
        wait_bytes(swaps[at].at[pl.ds(0, (n_layer - 1) * half), :], send_sem.at[3 + at])
    wait_bytes(plane_land, send_sem.at[6])
    wait_bytes(z_land.at[pl.ds(0, (n_z - 1) * shard), :], send_sem.at[9])
    wait_bytes(comb_land, send_sem.at[10])
    wait_bytes(grads_sum.at[pl.ds(0, (n_plane - 1) * shard), :], send_sem.at[11])
    for store in stores:
        store.wait()


def deliver(many, *refs):
    sources, targets, held = refs[:many], refs[many : 2 * many], refs[2 * many : 3 * many]
    in_sem, out_sem = refs[3 * many :]
    loads = [
        pltpu.make_async_copy(sources[at], held[at], in_sem.at[at]) for at in range(many)
    ]
    stores = [
        pltpu.make_async_copy(held[at], targets[at], out_sem.at[at]) for at in range(many)
    ]
    for load in loads:
        load.start()
    for load, store in zip(loads, stores):
        load.wait()
        store.start()
    for store in stores:
        store.wait()


def body(n_phi, n_layer, *arrays):
    node_feats, edge_feats, edge_source, edge_target, *others, node_cot = arrays
    latent, hits = node_feats.shape
    slots = edge_feats.shape[1]
    slab = hits * n_layer
    rim = others[1].shape[1]
    n_plane = Y_LO * CORES * n_layer
    n_z = n_phi // (Y_LO * CORES)
    grad_rows = 4 * latent
    shard = grad_rows // n_plane
    hbm = pl.BlockSpec(memory_space=pltpu.HBM)
    operands = (
        node_feats.T,
        edge_feats,
        edge_source.reshape(1, slots),
        edge_target.reshape(1, slots),
        *others,
        node_cot.T,
    )
    outs = [
        jax.ShapeDtypeStruct(*out)
        for out in (
            ((hits, latent), BF16),
            ((latent, slots), BF16),
            ((hits, latent), F32),
            ((latent, 3 * latent), F32),
            ((latent, latent), F32),
            ((latent, 2 * latent), F32),
            ((latent, latent), F32),
            ((4, latent), F32),
        )
    ]
    results = pl.pallas_call(
        functools.partial(kernel, n_phi, n_layer),
        out_shape=outs,
        in_specs=[hbm] * len(operands),
        out_specs=[hbm] * len(outs),
        scratch_shapes=[pltpu.VMEM(array.shape, array.dtype) for array in (*operands, *outs)]
        + [
            pltpu.VMEM((2 * slab + 2 * rim, slots), BF16),
            pltpu.VMEM((2 * rim, slab), BF16),
            pltpu.VMEM((2, slab, rim), BF16),
            pltpu.VMEM((2, 4 * latent, slots), BF16),
            pltpu.VMEM((2, 2 * latent, slots), BF16),
            pltpu.VMEM((latent, slots), F32),
            pltpu.VMEM((2, latent, slots), F32),
            pltpu.VMEM((latent, slots), F32),
            pltpu.VMEM((latent, slots), F32),
            pltpu.VMEM((3 * latent, slots), BF16),
            pltpu.VMEM((2, latent, LANES), F32),
            pltpu.VMEM((2, 2, slab, LANES), BF16),
            pltpu.VMEM((3, slab, LANES), F32),
            pltpu.VMEM((hits, LANES), BF16),
            pltpu.VMEM((slab, LANES), BF16),
            pltpu.VMEM((slab, LANES), BF16),
            pltpu.VMEM((2, 1, rim), jnp.int32),
            pltpu.VMEM((2 * rim, slab), BF16),
            pltpu.VMEM((2, slab, LANES), BF16),
            pltpu.VMEM((slab, LANES), BF16),
            pltpu.VMEM((2 * rim, LANES), BF16),
            pltpu.VMEM((2, 2 * rim, LANES), BF16),
            pltpu.VMEM((slab // 2, LANES), F32),
            pltpu.VMEM((slab, LANES), F32),
            pltpu.VMEM((2, n_layer * slab // 2, LANES), BF16),
            pltpu.VMEM((2, 2 * rim, LANES), BF16),
            pltpu.VMEM((2, 2 * rim, LANES), BF16),
            pltpu.VMEM((slab // 2, LANES), BF16),
            pltpu.VMEM(((n_layer - 1) * hits, LANES), BF16),
            pltpu.VMEM((grad_rows, LANES), F32),
            pltpu.VMEM(((n_plane - 1) * shard, LANES), F32),
            pltpu.VMEM((n_z * shard, LANES), F32),
            pltpu.VMEM((grad_rows, LANES), F32),
            pltpu.SemaphoreType.DMA((len(operands),)),
            pltpu.SemaphoreType.DMA((len(outs),)),
            pltpu.SemaphoreType.REGULAR((3,)),
            pltpu.SemaphoreType.DMA((14,)),
            pltpu.SemaphoreType.DMA((14,)),
        ],
        compiler_params=pltpu.CompilerParams(
            collective_id=0, has_side_effects=True, vmem_limit_bytes=VMEM_BYTES
        ),
    )(*operands)
    node_out, edge_out, node_grad, *totals = pl.pallas_call(
        functools.partial(deliver, len(outs)),
        out_shape=outs,
        in_specs=[hbm] * len(outs),
        out_specs=[hbm] * len(outs),
        scratch_shapes=[pltpu.VMEM(out.shape, out.dtype) for out in outs]
        + [pltpu.SemaphoreType.DMA((len(outs),))] * 2,
        compiler_params=pltpu.CompilerParams(vmem_limit_bytes=VMEM_BYTES),
    )(*results)
    return node_out.T, edge_out, node_grad.T, *totals


def solution(mesh):
    split = P(None, ("phi", "layer"))
    return jax.shard_map(
        functools.partial(body, mesh.shape["phi"], mesh.shape["layer"]),
        mesh=mesh,
        in_specs=(
            split,
            split,
            P(("phi", "layer")),
            P(("phi", "layer")),
            P("phi", "layer"),
            P("phi", None),
            P("phi", None),
            P(),
            P(),
            P(),
            P(),
            P(),
            split,
        ),
        out_specs=(split, split, split, P(), P(), P(), P(), P()),
        check_vma=False,
    )
```

```python
import functools
import itertools

import jax
import jax.numpy as jnp
from jax import lax
from jax.experimental import pallas as pl
from jax.experimental.pallas import tpu as pltpu
from jax.sharding import PartitionSpec as P

MESH = pl.DeviceIdType.MESH
BF16 = jnp.bfloat16
F32 = jnp.float32
LANES = 128
Y_LO = 2
CORES = 2
CHUNK = 1024
VMEM_BYTES = 64 * 1024 * 1024


def nn(left, right):
    return lax.dot_general(left, right, (((1,), (0,)), ((), ())), preferred_element_type=F32)


def nt(left, right):
    return lax.dot_general(left, right, (((1,), (1,)), ((), ())), preferred_element_type=F32)


def nt_exact(left, right):
    return lax.dot_general(
        left,
        right,
        (((1,), (1,)), ((), ())),
        precision=lax.Precision.HIGHEST,
        preferred_element_type=F32,
    )


def pick(rows, cols, row_shift, col_limit, dtype=BF16):
    row = lax.broadcasted_iota(jnp.int32, (rows, cols), 0)
    col = lax.broadcasted_iota(jnp.int32, (rows, cols), 1)
    return jnp.where((row == col + row_shift) & (col < col_limit), 1.0, 0.0).astype(dtype)


def two_parts(value):
    main = value.astype(BF16)
    return jnp.concatenate([main, (value - main.astype(F32)).astype(BF16)], axis=0)


def logistic(value):
    return 0.5 * jnp.tanh(0.5 * value) + 0.5


def chunks(total, step):
    size = min(CHUNK, total)

    def run(turn, carry):
        step(pl.ds(pl.multiple_of(turn * size, size), size))
        return carry

    lax.fori_loop(0, total // size, run, 0, unroll=True)


def wait_bytes(ref, sem):
    pltpu.make_async_copy(ref, ref, sem).wait()


def far_first(sizes):
    steps = list(itertools.product(*(range(size) for size in sizes)))
    hops = lambda step: sum(min(at, size - at) for at, size in zip(step, sizes))
    return sorted(steps[1:], key=hops, reverse=True)


def kernel(
    n_phi,
    n_layer,
    feats_in,
    edges_in,
    source_in,
    target_in,
    count_in,
    rim_up_in,
    rim_down_in,
    first_in,
    second_in,
    node_first_in,
    node_second_in,
    biases_in,
    cot_in,
    node_out_to,
    edge_out_to,
    node_grad_to,
    sums_to,
    feats,
    edges0,
    source,
    target,
    count,
    rim_up,
    rim_down,
    first,
    second,
    node_first,
    node_second,
    biases,
    cot,
    node_out,
    edge_out,
    node_grad,
    onehot,
    rim_pick,
    rim_put,
    hidden_in,
    edge_new,
    z_part,
    slopes,
    grad_edge,
    second_grad_edge,
    back_stack,
    bias_sums,
    node_kept,
    grad_kept,
    own_send,
    slab_land,
    table_kept,
    rim_near,
    near_pick,
    near_land,
    pairs_land,
    rim_send,
    rim_land,
    message_send,
    message_land,
    swap_land,
    back_send,
    back_land,
    comb_send,
    comb_land,
    grads,
    plane_land,
    z_land,
    shard_sum,
    load_sem,
    store_sem,
    chain_sem,
    send_sem,
    recv_sem,
):
    hits, latent = feats.shape
    slots = edges0.shape[1]
    slab = hits * n_layer
    half = slab // 2
    rim = rim_up.shape[1]
    n_z = n_phi // (Y_LO * CORES)
    n_plane = Y_LO * CORES * n_layer
    n_x = n_layer // 2
    n_y = 2 * Y_LO
    shard = grads.shape[0] // n_plane
    phi = lax.axis_index("phi")
    layer = lax.axis_index("layer")
    core = lax.rem(phi, CORES)
    z_at = lax.rem(lax.div(phi, CORES), n_z)
    y_lo = lax.div(phi, CORES * n_z)
    y_hi = lax.div(layer, n_x)
    x_at = lax.rem(layer, n_x)
    y_at = y_hi * Y_LO + y_lo
    plane_at = (y_lo * CORES + core) * n_layer + layer
    above = lax.rem(phi + 1, n_phi)
    below = lax.rem(phi + n_phi - 1, n_phi)

    x_of = [lax.rem(x_at + step, n_x) for step in range(n_x)]
    y_hi_of = [lax.rem(y_hi + step, 2) * n_x for step in range(2)]
    layer_peers = [
        y_hi_of[dy // Y_LO] + x_of[dx]
        for dy, dx in far_first((n_y, n_x))
        if dy % Y_LO == 0
    ]
    y_of = [lax.rem(y_at + step, n_y) for step in range(n_y)]
    pair_of = [lax.rem(y, Y_LO) * CORES for y in y_of]
    phi_base = [lax.rem(y, Y_LO) * (CORES * n_z) + z_at * CORES for y in y_of]
    layer_base = [lax.div(y, Y_LO) * n_x for y in y_of]
    core_of = [core, 1 - core]
    plane_peers = []
    for dy, dx, dc in far_first((n_y, n_x, CORES)):
        device = (phi_base[dy] + core_of[dc], layer_base[dy] + x_of[dx])
        plane_peers.append((device, (pair_of[dy] + core_of[dc]) * n_layer + device[1]))
    z_peers = [
        (y_lo * (CORES * n_z) + lax.rem(z_at + step, n_z) * CORES + core, layer)
        for (step,) in far_first((n_z,))
    ]

    def send(src, dst, step, device):
        pltpu.make_async_remote_copy(
            src_ref=src,
            dst_ref=dst,
            send_sem=send_sem.at[step],
            recv_sem=recv_sem.at[step],
            device_id=device,
            device_id_type=MESH,
        ).start()

    barrier = pltpu.get_barrier_semaphore()

    def along_z(step):
        return y_lo * (CORES * n_z) + lax.rem(z_at + step + n_z, n_z) * CORES + core, layer

    def greet(sem, devices):
        for device in devices:
            pl.semaphore_signal(sem, inc=1, device_id=device, device_id_type=MESH)

    greeted = [(phi, peer) for peer in layer_peers] + [
        (phi_base[0] + 1 - core, layer),
        (phi_base[0] + (1 - 2 * y_lo) * (CORES * n_z) + core, layer),
        (phi_base[0] + (1 - 2 * y_lo) * (CORES * n_z) + 1 - core, layer),
        (above, layer),
        (below, layer),
        along_z(1),
        along_z(-1),
    ]
    loads = [
        pltpu.make_async_copy(src, dst, load_sem.at[at])
        for at, (src, dst) in enumerate(
            (
                (feats_in, feats),
                (cot_in, cot),
                (first_in, first),
                (biases_in, biases),
                (second_in, second),
                (node_first_in, node_first),
                (node_second_in, node_second),
                (count_in, count),
                (source_in, source),
                (target_in, target),
                (rim_up_in, rim_up),
                (rim_down_in, rim_down),
                (edges_in, edges0),
            )
        )
    ]
    for load in loads[:2]:
        load.start()
    greet(barrier, greeted)
    for load in loads[2:]:
        load.start()

    lane = lax.broadcasted_iota(jnp.int32, (1, LANES), 1)
    low_half = lane < latent
    own_rows = pl.ds(pl.multiple_of(layer * hits, hits), hits)
    swap_rows = pl.ds(pl.multiple_of(layer * half, half), half)

    loads[0].wait()
    loads[1].wait()
    wide_pick = pick(latent, LANES, 0, latent)
    high_pick = pick(latent, LANES, -latent, LANES)
    own_send[...] = (
        nn(feats[...], wide_pick) + nn(cot[...].astype(BF16), high_pick)
    ).astype(BF16)
    pl.semaphore_wait(barrier, len(greeted))
    known = [step for step in (1, 2, 4) if step < n_z // 2]

    def tell(at):
        if at < len(known):
            greet(chain_sem.at[at], [along_z(known[at]), along_z(-known[at])])

    def told(at):
        if at < len(known):
            pl.semaphore_wait(chain_sem.at[at], 2)

    tell(0)
    for peer in layer_peers:
        send(own_send, slab_land.at[own_rows, :], 0, (phi, peer))
    slab_land[own_rows, :] = own_send[...]
    send(rim_up_in, rim_near.at[0], 2, (above, layer))
    send(rim_down_in, rim_near.at[1], 2, (below, layer))

    shard_rows = pl.ds(pl.multiple_of(plane_at * shard, shard), shard)
    stores = [
        pltpu.make_async_copy(src, dst, store_sem.at[at])
        for at, (src, dst) in enumerate(
            (
                (node_out, node_out_to),
                (edge_out, edge_out_to),
                (node_grad, node_grad_to),
                (shard_sum, sums_to.at[shard_rows, :]),
            )
        )
    ]
    swaps = (None, swap_land.at[0], swap_land.at[1])
    x_rows = pl.ds(pl.multiple_of(x_at * hits, hits), hits)
    lower_x_rows = pl.ds(pl.multiple_of(half + x_at * hits, hits), hits)
    pair_rows = pl.ds(pl.multiple_of(x_at * 2 * hits, 2 * hits), 2 * hits)

    def in_order(pairs):
        parts = [
            pairs[(2 * x + side) * hits : (2 * x + side + 1) * hits]
            for side in range(2)
            for x in range(n_x)
        ]
        return jnp.concatenate(parts, axis=0)

    def swap(at, value):
        swaps[at][swap_rows, :] = value.astype(swaps[at].dtype)
        mine = swaps[at].at[swap_rows, :]
        for peer in layer_peers:
            send(mine, mine, 3 + at, (phi, peer))

    def swapped_sum(at):
        wait_bytes(swaps[at].at[pl.ds(0, (n_layer - 1) * half), :], recv_sem.at[3 + at])
        total = swaps[at][0:half, :].astype(F32)
        for turn in range(1, n_layer):
            total = total + swaps[at][turn * half : (turn + 1) * half, :].astype(F32)
        return total

    for load in loads[2:7]:
        load.wait()
    edge_first = first[...]
    source_wide = nn(edge_first, pick(3 * latent, LANES, 0, latent)).astype(BF16)
    target_wide = nn(edge_first, pick(3 * latent, LANES, latent, latent)).astype(BF16)
    source_high = nn(edge_first, pick(3 * latent, LANES, -latent, LANES) * (~low_half).astype(BF16)).astype(BF16)
    target_high = nn(edge_first, pick(3 * latent, LANES, 0, LANES) * (~low_half).astype(BF16)).astype(BF16)
    first_self = edge_first[:, 2 * latent :]
    edge_second = second[...]
    square_eye = pick(latent, latent, 0, latent)
    self_back = nt(square_eye, first_self).astype(BF16)
    second_back = nt(square_eye, edge_second).astype(BF16)
    zero_square = jnp.zeros((latent, latent), BF16)
    gm_pick = jnp.concatenate(
        [
            high_pick,
            nt(square_eye, jnp.concatenate([zero_square, edge_second], axis=0)).astype(BF16),
        ],
        axis=0,
    )
    first_back = jnp.concatenate([source_wide, target_wide], axis=0)
    first_back_high = jnp.concatenate([source_high, target_high], axis=0)
    node_first_wide = jnp.concatenate(
        [node_first[...], jnp.zeros((LANES - latent, 2 * latent), BF16)], axis=0
    )
    gm_back = nt(gm_pick, node_first_wide)
    gm_back = jnp.concatenate([gm_back[0:latent].astype(BF16), two_parts(gm_back[latent:])], axis=0)
    node_second_low = nn(node_second[...], wide_pick).astype(BF16)
    zero_wide = jnp.zeros((LANES - latent, LANES), BF16)
    node_second_wide = jnp.concatenate([node_second_low, zero_wide], axis=0)
    node_second_under = jnp.concatenate([zero_wide, node_second_low], axis=0)
    bias_rows = lax.dot_general(
        biases[...],
        pick(latent, LANES, 0, latent, F32),
        (((1,), (0,)), ((), ())),
        precision=lax.Precision.HIGHEST,
        preferred_element_type=F32,
    )
    bias_cols = nt_exact(pick(latent, latent, 0, latent, F32), biases[...])
    bias_edge = bias_cols[:, 0:1]
    bias_message = bias_cols[:, 1:2]
    bias_node = bias_rows[2:3, :]
    bias_update = bias_rows[3:4, :]
    for load in loads[7:]:
        load.wait()

    def build(cols):
        width = cols.size
        spot = lax.broadcasted_iota(jnp.int32, (1, width), 1) + cols.start
        here = spot < count[...]
        source_at = jnp.where(here, source[:, cols], -1)
        target_at = jnp.where(here, target[:, cols], -1)
        row = lax.broadcasted_iota(jnp.int32, (slab, width), 0)
        onehot[0:slab, cols] = jnp.where(row == source_at, 1.0, 0.0).astype(BF16)
        onehot[slab : 2 * slab, cols] = jnp.where(row == target_at, 1.0, 0.0).astype(BF16)
        rim_row = lax.broadcasted_iota(jnp.int32, (2 * rim, width), 0) + slab
        onehot[2 * slab : 2 * slab + 2 * rim, cols] = jnp.where(
            rim_row == source_at, 1.0, 0.0
        ).astype(BF16)
        z_part[:, cols] = nn(first_self, edges0[:, cols]) + bias_edge

    chunks(slots, build)
    rim_eye = pick(rim, rim, 0, rim)
    for side, index in enumerate((rim_up, rim_down)):
        put = jnp.where(
            lax.broadcasted_iota(jnp.int32, (slab, rim), 0) == index[...], 1.0, 0.0
        ).astype(BF16)
        rim_put[side] = put
        rim_pick[side * rim : (side + 1) * rim, :] = nt(rim_eye, put).astype(BF16)
    grad_own = lax.dot_general(
        cot[...],
        pick(latent, LANES, 0, latent, F32),
        (((1,), (0,)), ((), ())),
        precision=lax.Precision.HIGHEST,
        preferred_element_type=F32,
    )

    wait_bytes(slab_land.at[pl.ds(0, slab - hits), :], recv_sem.at[0])
    told(0)
    tell(1)
    rim_send[...] = nn(rim_pick[...], slab_land[...]).astype(BF16)
    send(rim_send.at[0:rim], rim_land.at[0, 0:rim], 1, (above, layer))
    send(rim_send.at[rim : 2 * rim], rim_land.at[0, rim : 2 * rim], 1, (below, layer))
    table = jnp.where(low_half, slab_land[...].astype(F32), 0.0).astype(BF16)
    table_kept[...] = table
    for k in range(2):
        own_part = two_parts(
            jnp.concatenate([nt(source_wide, table), nt(target_wide, table)], axis=1)
        )

        def own_terms(cols):
            terms = nn(own_part, onehot[0 : 2 * slab, cols])
            z_part[:, cols] = z_part[:, cols] + (terms[0:latent] + terms[latent:])

        chunks(slots, own_terms)
        if k == 0:
            wait_bytes(rim_land.at[0], recv_sem.at[1])
        else:
            wait_bytes(near_land, recv_sem.at[13])
            for side in range(2):
                rim_land[1, side * rim : (side + 1) * rim, :] = nn(
                    near_pick[side * rim : (side + 1) * rim, :], near_land[side]
                ).astype(BF16)
        rim_part = two_parts(nt(source_wide, rim_land[k]))

        def edge_mlp(cols):
            width = cols.size
            terms = nn(rim_part, onehot[2 * slab : 2 * slab + 2 * rim, cols])
            pre = z_part[:, cols] + (terms[0:latent] + terms[latent:])
            gate = logistic(pre)
            hidden = (pre * gate).astype(BF16)
            hidden_in[k, 3 * latent : 4 * latent, cols] = hidden
            slopes[k, :, cols] = gate * (1.0 + pre * (1.0 - gate))
            old = edges0[:, cols] if k == 0 else edge_new[0, 0:latent, cols]
            here = lax.broadcasted_iota(jnp.int32, (1, width), 1) + cols.start < count[...]
            fresh = jnp.where(
                here, old.astype(F32) + nn(edge_second, hidden) + bias_message, 0.0
            ).astype(BF16)
            edge_new[k, 0:latent, cols] = fresh

        chunks(slots, edge_mlp)
        both_halves = nt(onehot[slab : 2 * slab, :], edge_new[k])
        packed = jnp.concatenate([both_halves[0:half], both_halves[half:]], axis=1)
        if k == 0:
            message_send[...] = packed
            for peer in layer_peers:
                spot = pl.ds(pl.multiple_of(lax.rem(peer, n_x) * hits, hits), hits)
                send(message_send.at[spot, :], message_land.at[own_rows, :], 3, (phi, peer))
            message_land[own_rows, :] = message_send[x_rows, :]
            wait_bytes(rim_near, recv_sem.at[2])
            row = lax.broadcasted_iota(jnp.int32, (slab, rim), 0)
            pair_row = lax.rem(row, 2 * hits)
            hit = (
                lax.div(row, 2 * hits) * hits
                + lax.rem(pair_row, hits)
                + lax.div(pair_row, hits) * half
            )
            for side in range(2):
                put = jnp.where(hit == rim_near[side], 1.0, 0.0).astype(BF16)
                near_pick[side * rim : (side + 1) * rim, :] = nt(rim_eye, put).astype(BF16)
        else:
            swap(k, packed)

        raw_own = nt(wide_pick, table).astype(BF16)
        raw_rim = nt(wide_pick, rim_land[k]).astype(BF16)

        def inputs(cols):
            hidden_in[k, 0:latent, cols] = (
                nn(raw_own, onehot[0:slab, cols])
                + nn(raw_rim, onehot[2 * slab : 2 * slab + 2 * rim, cols])
            ).astype(BF16)
            hidden_in[k, latent : 2 * latent, cols] = nn(
                raw_own, onehot[slab : 2 * slab, cols]
            ).astype(BF16)
            if k == 0:
                old = edges0[:, cols]
                z_part[:, cols] = nn(first_self, edge_new[0, 0:latent, cols]) + bias_edge
            else:
                old = edge_new[0, 0:latent, cols]
                edge_out[:, cols] = edge_new[1, 0:latent, cols]
            hidden_in[k, 2 * latent : 3 * latent, cols] = old

        chunks(slots, inputs)
        if k == 0:
            wait_bytes(message_land.at[pl.ds(0, (n_layer - 1) * hits), :], recv_sem.at[3])
            packed = message_land[0:hits, :]
            for turn in range(1, n_layer):
                packed = packed + message_land[turn * hits : (turn + 1) * hits, :]
            upper_old = table_kept[x_rows, :].astype(F32)
            lower_old = table_kept[lower_x_rows, :].astype(F32)
        else:
            packed = swapped_sum(k)
            table_wide = table.astype(F32)
            upper_old, lower_old = table_wide[0:half], table_wide[half:]
        told(1 + k)
        if k == 0:
            tell(2)
        node_old = jnp.concatenate([upper_old, lower_old], axis=0)
        node_in = jnp.concatenate(
            [
                jnp.where(low_half, upper_old, pltpu.roll(packed, latent, 1)),
                jnp.where(low_half, lower_old, packed),
            ],
            axis=0,
        ).astype(BF16)
        node_pre = nt(node_in, node_first_wide) + bias_node
        node_gate = logistic(node_pre)
        node_hidden = (node_pre * node_gate).astype(BF16)
        node_slope = node_gate * (1.0 + node_pre * (1.0 - node_gate))
        table = (node_old + nt(node_hidden, node_second_wide) + bias_update).astype(BF16)
        if k == 0:
            turned = pltpu.roll(node_slope, latent, 1)
            pairs_land[pair_rows, :] = jnp.where(low_half, table.astype(F32), turned).astype(BF16)
            mine = pairs_land.at[pair_rows, :]
            for side, slab_at in enumerate((above, below)):
                for x in x_of:
                    send(mine, near_land.at[side, pair_rows, :], 13, (slab_at, y_hi * n_x + x))
            for (step,) in far_first((n_x,)):
                send(mine, mine, 12, (phi, y_hi * n_x + x_of[step]))
            node_kept[0, 0, 0 : 2 * hits] = node_in
            node_kept[0, 1, 0 : 2 * hits] = node_hidden
            if n_x > 1:
                wait_bytes(pairs_land.at[pl.ds(0, (n_x - 1) * 2 * hits), :], recv_sem.at[12])
            gathered = in_order(pairs_land[...].astype(F32))
            table = jnp.where(low_half, gathered, 0.0).astype(BF16)
            first_slope = pltpu.roll(gathered, latent, 1)
        else:
            node_kept[1, 0] = node_in
            node_kept[1, 1] = node_hidden
            stores[1].start()

    for k in (1, 0):
        if k == 1:
            pre_back = nn(slab_land[...], node_second_under) * node_slope
        else:
            grad_low = grad_now.astype(BF16)
            pre_back = nn(grad_low, node_second_wide) * first_slope
        pre_low = pre_back.astype(BF16)
        in_back = nn(pre_low, node_first_wide)
        gm_part = nt(gm_back, pre_low)
        gm_part = jnp.concatenate(
            [
                gm_part[0:latent].astype(BF16),
                two_parts(gm_part[latent : 2 * latent] + gm_part[2 * latent :]),
            ],
            axis=0,
        )

        if k == 1:
            bias_sums[...] = jnp.zeros_like(bias_sums)

        def folded(value):
            pieces = [
                value[:, at : at + LANES] for at in range(0, value.shape[1], LANES)
            ]
            return functools.reduce(lambda one, other: one + other, pieces)

        def edge_back(cols):
            both = nn(gm_part, onehot[slab : 2 * slab, cols])
            edge_grad = both[0:latent]
            hidden_grad = both[latent : 2 * latent] + both[2 * latent :]
            if k == 0:
                edge_grad = edge_grad + grad_edge[:, cols]
                hidden_grad = hidden_grad + second_grad_edge[:, cols]
            else:
                grad_edge[:, cols] = edge_grad
            pre_grad = hidden_grad * slopes[k, :, cols]
            bias_sums[0] = bias_sums[0] + folded(pre_grad)
            bias_sums[1] = bias_sums[1] + folded(edge_grad)
            pre_grad = pre_grad.astype(BF16)
            back_stack[0:latent, cols] = pre_grad
            back_stack[latent : 2 * latent, cols] = pre_grad
            back_stack[2 * latent : 3 * latent, cols] = edge_grad.astype(BF16)

        chunks(slots, edge_back)

        def weight_terms():
            outer = nt(back_stack[latent : 3 * latent, :], hidden_in[k])
            upper = outer[0:latent, 0:LANES]
            lower = jnp.where(low_half, outer[0:latent, LANES:], outer[latent:, LANES:])
            return upper, lower

        def column_at(at, sums):
            return jnp.where(lane == latent + at, jnp.sum(sums, axis=1, keepdims=True), 0.0)

        if k == 0:
            upper, lower = weight_terms()
            grads[0:latent, :] = grads[0:latent, :] + upper
            grads[latent : 2 * latent, :] = grads[latent : 2 * latent, :] + lower

        def node_terms():
            kept_rows = (
                pl.ds(pl.multiple_of(y_hi * hits, hits), hits) if k == 0 else own_rows
            )
            grad_kept[0] = pre_back
            grad_kept[1] = in_back
            if k == 0:
                grad_kept[2] = gained
                grad_mine = grad_own + grad_kept[2, own_rows, :]
            else:
                grad_mine = grad_own
            pre_mine = grad_kept[0, own_rows, :]
            pre_turned = nt(wide_pick, pre_mine.astype(BF16))
            grad_turned = nt(wide_pick, grad_mine.astype(BF16))
            return (
                nn(pre_turned.astype(BF16), node_kept[k, 0, kept_rows, :]),
                nn(grad_turned.astype(BF16), node_kept[k, 1, kept_rows, :])
                + column_at(2, pre_turned)
                + column_at(3, grad_turned),
                grad_mine + jnp.where(low_half, grad_kept[1, own_rows, :], 0.0),
            )

        if k == 0:
            first_terms, second_terms, grad_own = node_terms()
            grads[2 * latent : 3 * latent, :] = grads[2 * latent : 3 * latent, :] + first_terms
            grads[3 * latent : 4 * latent, :] = (
                grads[3 * latent : 4 * latent, :]
                + second_terms
                + column_at(0, bias_sums[0])
                + column_at(1, bias_sums[1])
            )
            for at, (device, spot) in enumerate(plane_peers):
                send(
                    grads.at[pl.ds(pl.multiple_of(spot * shard, shard), shard), :],
                    plane_land.at[pl.ds(at * shard, shard), :],
                    6,
                    device,
                )

        back_send[k] = nt(
            onehot[2 * slab : 2 * slab + 2 * rim, :], back_stack[0 : 2 * latent, :]
        ).astype(BF16)
        send(back_send.at[k, 0:rim], back_land.at[k, 0:rim], 7 + k, (below, layer))
        send(
            back_send.at[k, rim : 2 * rim],
            back_land.at[k, rim : 2 * rim],
            7 + k,
            (above, layer),
        )
        from_source = nt(onehot[0:slab, :], back_stack[0 : 2 * latent, :])
        from_target = nt(onehot[slab : 2 * slab, :], back_stack[0 : 2 * latent, :])
        if k == 0:
            wait_bytes(plane_land, recv_sem.at[6])
            total = grads[shard_rows, :]
            for turn in range(n_plane - 1):
                total = total + plane_land[turn * shard : (turn + 1) * shard, :]
            z_rows = pl.ds(pl.multiple_of(z_at * shard, shard), shard)
            z_land[z_rows, :] = total
            for peer in z_peers:
                send(z_land.at[z_rows, :], z_land.at[z_rows, :], 9, peer)
        wait_bytes(back_land.at[k], recv_sem.at[7 + k])
        from_source = (
            from_source
            + nn(rim_put[0], back_land[k, 0:rim])
            + nn(rim_put[1], back_land[k, rim : 2 * rim])
        )
        comb = jnp.where(low_half, from_source, from_target).astype(BF16)
        packed = nn(comb[0:half], first_back) + nn(comb[half:], first_back_high)
        if k == 1:
            swap(2, packed)
            upper, lower = weight_terms()
            first_terms, second_terms, grad_own = node_terms()
            grads[0:latent, :] = upper
            grads[latent : 2 * latent, :] = lower
            grads[2 * latent : 3 * latent, :] = first_terms
            grads[3 * latent : 4 * latent, :] = second_terms
            node_kept[1, 0] = table
            node_out[...] = node_kept[1, 0, own_rows, 0:latent]
            stores[0].start()

            def carried(cols):
                old = grad_edge[:, cols] + nn(self_back, back_stack[0:latent, cols])
                grad_edge[:, cols] = old
                second_grad_edge[:, cols] = nn(second_back, old.astype(BF16))

            chunks(slots, carried)
            cot_slab = pltpu.roll(slab_land[...].astype(F32), latent, 1)
            grad_before = jnp.where(low_half, cot_slab + in_back, 0.0)
            packed = swapped_sum(2)
            gained = jnp.concatenate(
                [
                    jnp.where(low_half, packed, 0.0),
                    jnp.where(low_half, pltpu.roll(packed, latent, 1), 0.0),
                ],
                axis=0,
            )
            grad_now = grad_before + gained
        else:
            comb_send[...] = packed.astype(BF16)

            def rows_of(device):
                return pl.ds(pl.multiple_of(lax.rem(device, n_layer // 2) * hits, hits), hits)

            for at, peer in enumerate(layer_peers):
                send(
                    comb_send.at[rows_of(peer), :],
                    comb_land.at[pl.ds(at * hits, hits), :],
                    10,
                    (phi, peer),
                )
            wait_bytes(z_land.at[pl.ds(0, (n_z - 1) * shard), :], recv_sem.at[9])
            total = z_land[0:shard, :]
            for turn in range(1, n_z):
                total = total + z_land[turn * shard : (turn + 1) * shard, :]
            shard_sum[...] = total
            for device, _ in plane_peers:
                send(shard_sum, sums_to.at[shard_rows, :], 11, device)
            stores[3].start()
            wait_bytes(comb_land, recv_sem.at[10])
            total = comb_send[rows_of(layer), :].astype(F32)
            for turn in range(n_layer - 1):
                total = total + comb_land[turn * hits : (turn + 1) * hits, :].astype(F32)
            total = jnp.where(layer < n_layer // 2, total, pltpu.roll(total, latent, 1))
            node_grad[...] = (grad_own + total)[:, 0:latent]
            stores[2].start()

    wait_bytes(sums_to.at[pl.ds(0, (n_plane - 1) * shard), :], recv_sem.at[11])
    wait_bytes(slab_land.at[pl.ds(0, slab - hits), :], send_sem.at[0])
    wait_bytes(rim_send, send_sem.at[1])
    wait_bytes(rim_near, send_sem.at[2])
    wait_bytes(message_land.at[pl.ds(0, (n_layer - 1) * hits), :], send_sem.at[3])
    if n_x > 1:
        wait_bytes(pairs_land.at[pl.ds(0, (n_x - 1) * 2 * hits), :], send_sem.at[12])
    wait_bytes(near_land, send_sem.at[13])
    for k in range(2):
        wait_bytes(back_send.at[k], send_sem.at[7 + k])
    for at in range(1, 3):
        wait_bytes(swaps[at].at[pl.ds(0, (n_layer - 1) * half), :], send_sem.at[3 + at])
    wait_bytes(plane_land, send_sem.at[6])
    wait_bytes(z_land.at[pl.ds(0, (n_z - 1) * shard), :], send_sem.at[9])
    wait_bytes(comb_land, send_sem.at[10])
    wait_bytes(plane_land, send_sem.at[11])
    for store in stores:
        store.wait()


def deliver(*refs):
    sources, targets, held, sums = refs[:4], refs[4:12], refs[12:20], refs[20]
    in_sem, out_sem = refs[21:]
    first, second, node_first, node_second, biases = held[3:]
    latent = second.shape[0]
    loads = [
        pltpu.make_async_copy(sources[at], dst, in_sem.at[at])
        for at, dst in enumerate((*held[:3], sums))
    ]
    stores = [
        pltpu.make_async_copy(held[at], targets[at], out_sem.at[at]) for at in range(8)
    ]
    for load in loads:
        load.start()
    loads[3].wait()
    first[:, 0:LANES] = sums[0:latent, :]
    first[:, LANES:] = sums[latent : 2 * latent, 0:latent]
    second[...] = pltpu.roll(sums[latent : 2 * latent, :], latent, 1)[:, 0:latent]
    node_first[...] = sums[2 * latent : 3 * latent, :]
    node_second[...] = sums[3 * latent : 4 * latent, 0:latent]
    biases[...] = sums[3 * latent : 4 * latent, :].T[latent : latent + 4, :]
    for store in stores[3:]:
        store.start()
    for load, store in zip(loads[:3], stores):
        load.wait()
        store.start()
    for store in stores:
        store.wait()


def body(n_phi, n_layer, *arrays):
    node_feats, edge_feats, edge_source, edge_target, *others, node_cot = arrays
    latent, hits = node_feats.shape
    slots = edge_feats.shape[1]
    slab = hits * n_layer
    rim = others[1].shape[1]
    n_plane = Y_LO * CORES * n_layer
    n_z = n_phi // (Y_LO * CORES)
    grad_rows = 4 * latent
    shard = grad_rows // n_plane
    hbm = pl.BlockSpec(memory_space=pltpu.HBM)
    operands = (
        node_feats.T,
        edge_feats,
        edge_source.reshape(1, slots),
        edge_target.reshape(1, slots),
        *others,
        node_cot.T,
    )
    outs = [
        jax.ShapeDtypeStruct(*out)
        for out in (
            ((hits, latent), BF16),
            ((latent, slots), BF16),
            ((hits, latent), F32),
            ((latent, 3 * latent), F32),
            ((latent, latent), F32),
            ((latent, 2 * latent), F32),
            ((latent, latent), F32),
            ((4, latent), F32),
        )
    ]
    results = pl.pallas_call(
        functools.partial(kernel, n_phi, n_layer),
        out_shape=[*outs[:3], jax.ShapeDtypeStruct((grad_rows, LANES), F32)],
        in_specs=[hbm] * len(operands),
        out_specs=[hbm] * 4,
        scratch_shapes=[pltpu.VMEM(array.shape, array.dtype) for array in (*operands, *outs[:3])]
        + [
            pltpu.VMEM((2 * slab + 2 * rim, slots), BF16),
            pltpu.VMEM((2 * rim, slab), BF16),
            pltpu.VMEM((2, slab, rim), BF16),
            pltpu.VMEM((2, 4 * latent, slots), BF16),
            pltpu.VMEM((2, latent, slots), BF16),
            pltpu.VMEM((latent, slots), F32),
            pltpu.VMEM((2, latent, slots), F32),
            pltpu.VMEM((latent, slots), F32),
            pltpu.VMEM((latent, slots), F32),
            pltpu.VMEM((3 * latent, slots), BF16),
            pltpu.VMEM((2, latent, LANES), F32),
            pltpu.VMEM((2, 2, slab, LANES), BF16),
            pltpu.VMEM((3, slab, LANES), F32),
            pltpu.VMEM((hits, LANES), BF16),
            pltpu.VMEM((slab, LANES), BF16),
            pltpu.VMEM((slab, LANES), BF16),
            pltpu.VMEM((2, 1, rim), jnp.int32),
            pltpu.VMEM((2 * rim, slab), BF16),
            pltpu.VMEM((2, slab, LANES), BF16),
            pltpu.VMEM((slab, LANES), BF16),
            pltpu.VMEM((2 * rim, LANES), BF16),
            pltpu.VMEM((2, 2 * rim, LANES), BF16),
            pltpu.VMEM((slab // 2, LANES), F32),
            pltpu.VMEM((slab, LANES), F32),
            pltpu.VMEM((2, n_layer * slab // 2, LANES), BF16),
            pltpu.VMEM((2, 2 * rim, LANES), BF16),
            pltpu.VMEM((2, 2 * rim, LANES), BF16),
            pltpu.VMEM((slab // 2, LANES), BF16),
            pltpu.VMEM(((n_layer - 1) * hits, LANES), BF16),
            pltpu.VMEM((grad_rows, LANES), F32),
            pltpu.VMEM(((n_plane - 1) * shard, LANES), F32),
            pltpu.VMEM((n_z * shard, LANES), F32),
            pltpu.VMEM((shard, LANES), F32),
            pltpu.SemaphoreType.DMA((len(operands),)),
            pltpu.SemaphoreType.DMA((4,)),
            pltpu.SemaphoreType.REGULAR((3,)),
            pltpu.SemaphoreType.DMA((14,)),
            pltpu.SemaphoreType.DMA((14,)),
        ],
        compiler_params=pltpu.CompilerParams(
            collective_id=0, has_side_effects=True, vmem_limit_bytes=VMEM_BYTES
        ),
    )(*operands)
    node_out, edge_out, node_grad, *totals = pl.pallas_call(
        deliver,
        out_shape=outs,
        in_specs=[hbm] * 4,
        out_specs=[hbm] * len(outs),
        scratch_shapes=[pltpu.VMEM(out.shape, out.dtype) for out in outs]
        + [
            pltpu.VMEM((grad_rows, LANES), F32),
            pltpu.SemaphoreType.DMA((4,)),
            pltpu.SemaphoreType.DMA((len(outs),)),
        ],
        compiler_params=pltpu.CompilerParams(vmem_limit_bytes=VMEM_BYTES),
    )(*results)
    return node_out.T, edge_out, node_grad.T, *totals


def solution(mesh):
    split = P(None, ("phi", "layer"))
    return jax.shard_map(
        functools.partial(body, mesh.shape["phi"], mesh.shape["layer"]),
        mesh=mesh,
        in_specs=(
            split,
            split,
            P(("phi", "layer")),
            P(("phi", "layer")),
            P("phi", "layer"),
            P("phi", None),
            P("phi", None),
            P(),
            P(),
            P(),
            P(),
            P(),
            split,
        ),
        out_specs=(split, split, split, P(), P(), P(), P(), P()),
        check_vma=False,
    )
```

```python
import functools
import itertools

import jax
import jax.numpy as jnp
from jax import lax
from jax.experimental import pallas as pl
from jax.experimental.pallas import tpu as pltpu
from jax.sharding import PartitionSpec as P

MESH = pl.DeviceIdType.MESH
BF16 = jnp.bfloat16
F32 = jnp.float32
LANES = 128
Y_LO = 2
CORES = 2
CHUNK = 1024
VMEM_BYTES = 64 * 1024 * 1024


def nn(left, right):
    return lax.dot_general(left, right, (((1,), (0,)), ((), ())), preferred_element_type=F32)


def nt(left, right):
    return lax.dot_general(left, right, (((1,), (1,)), ((), ())), preferred_element_type=F32)


def nt_exact(left, right):
    return lax.dot_general(
        left,
        right,
        (((1,), (1,)), ((), ())),
        precision=lax.Precision.HIGHEST,
        preferred_element_type=F32,
    )


def pick(rows, cols, row_shift, col_limit, dtype=BF16):
    row = lax.broadcasted_iota(jnp.int32, (rows, cols), 0)
    col = lax.broadcasted_iota(jnp.int32, (rows, cols), 1)
    return jnp.where((row == col + row_shift) & (col < col_limit), 1.0, 0.0).astype(dtype)


def two_parts(value):
    main = value.astype(BF16)
    return jnp.concatenate([main, (value - main.astype(F32)).astype(BF16)], axis=0)


def logistic(value):
    return 0.5 * jnp.tanh(0.5 * value) + 0.5


def chunks(total, step):
    size = min(CHUNK, total)

    def run(turn, carry):
        step(pl.ds(pl.multiple_of(turn * size, size), size))
        return carry

    lax.fori_loop(0, total // size, run, 0, unroll=True)


def wait_bytes(ref, sem):
    pltpu.make_async_copy(ref, ref, sem).wait()


def far_first(sizes):
    steps = list(itertools.product(*(range(size) for size in sizes)))
    hops = lambda step: sum(min(at, size - at) for at, size in zip(step, sizes))
    return sorted(steps[1:], key=hops, reverse=True)


def kernel(
    n_phi,
    n_layer,
    feats_in,
    edges_in,
    source_in,
    target_in,
    count_in,
    rim_up_in,
    rim_down_in,
    first_in,
    second_in,
    node_first_in,
    node_second_in,
    biases_in,
    cot_in,
    node_out_to,
    edge_out_to,
    node_grad_to,
    sums_to,
    feats,
    edges0,
    source,
    target,
    count,
    rim_up,
    rim_down,
    first,
    second,
    node_first,
    node_second,
    biases,
    cot,
    node_out,
    edge_out,
    node_grad,
    onehot,
    rim_pick,
    rim_put,
    hidden_in,
    edge_new,
    z_part,
    slopes,
    grad_edge,
    second_grad_edge,
    back_stack,
    bias_sums,
    node_kept,
    grad_kept,
    own_send,
    slab_land,
    table_kept,
    rim_near,
    near_pick,
    near_land,
    pairs_land,
    rim_send,
    rim_land,
    message_send,
    message_land,
    swap_land,
    back_send,
    back_land,
    comb_send,
    comb_land,
    grads,
    plane_land,
    z_land,
    shard_sum,
    load_sem,
    store_sem,
    chain_sem,
    send_sem,
    recv_sem,
):
    hits, latent = feats.shape
    slots = edges0.shape[1]
    slab = hits * n_layer
    half = slab // 2
    rim = rim_up.shape[1]
    n_z = n_phi // (Y_LO * CORES)
    n_plane = Y_LO * CORES * n_layer
    n_x = n_layer // 2
    n_y = 2 * Y_LO
    shard = grads.shape[0] // n_plane
    phi = lax.axis_index("phi")
    layer = lax.axis_index("layer")
    core = lax.rem(phi, CORES)
    z_at = lax.rem(lax.div(phi, CORES), n_z)
    y_lo = lax.div(phi, CORES * n_z)
    y_hi = lax.div(layer, n_x)
    x_at = lax.rem(layer, n_x)
    y_at = y_hi * Y_LO + y_lo
    plane_at = (y_lo * CORES + core) * n_layer + layer
    above = lax.rem(phi + 1, n_phi)
    below = lax.rem(phi + n_phi - 1, n_phi)

    x_of = [lax.rem(x_at + step, n_x) for step in range(n_x)]
    y_hi_of = [lax.rem(y_hi + step, 2) * n_x for step in range(2)]
    layer_peers = [
        y_hi_of[dy // Y_LO] + x_of[dx]
        for dy, dx in far_first((n_y, n_x))
        if dy % Y_LO == 0
    ]
    y_of = [lax.rem(y_at + step, n_y) for step in range(n_y)]
    pair_of = [lax.rem(y, Y_LO) * CORES for y in y_of]
    phi_base = [lax.rem(y, Y_LO) * (CORES * n_z) + z_at * CORES for y in y_of]
    layer_base = [lax.div(y, Y_LO) * n_x for y in y_of]
    core_of = [core, 1 - core]
    plane_peers = []
    for dy, dx, dc in far_first((n_y, n_x, CORES)):
        device = (phi_base[dy] + core_of[dc], layer_base[dy] + x_of[dx])
        plane_peers.append((device, (pair_of[dy] + core_of[dc]) * n_layer + device[1]))
    z_peers = [
        (y_lo * (CORES * n_z) + lax.rem(z_at + step, n_z) * CORES + core, layer)
        for (step,) in far_first((n_z,))
    ]

    def send(src, dst, step, device):
        pltpu.make_async_remote_copy(
            src_ref=src,
            dst_ref=dst,
            send_sem=send_sem.at[step],
            recv_sem=recv_sem.at[step],
            device_id=device,
            device_id_type=MESH,
        ).start()

    barrier = pltpu.get_barrier_semaphore()

    def along_z(step):
        return y_lo * (CORES * n_z) + lax.rem(z_at + step + n_z, n_z) * CORES + core, layer

    def greet(sem, devices):
        for device in devices:
            pl.semaphore_signal(sem, inc=1, device_id=device, device_id_type=MESH)

    greeted = [(phi, peer) for peer in layer_peers] + [
        (phi_base[0] + 1 - core, layer),
        (phi_base[0] + (1 - 2 * y_lo) * (CORES * n_z) + core, layer),
        (phi_base[0] + (1 - 2 * y_lo) * (CORES * n_z) + 1 - core, layer),
        (above, layer),
        (below, layer),
        along_z(1),
        along_z(-1),
    ]
    loads = [
        pltpu.make_async_copy(src, dst, load_sem.at[at])
        for at, (src, dst) in enumerate(
            (
                (feats_in, feats),
                (cot_in, cot),
                (first_in, first),
                (biases_in, biases),
                (second_in, second),
                (node_first_in, node_first),
                (node_second_in, node_second),
                (count_in, count),
                (source_in, source),
                (target_in, target),
                (rim_up_in, rim_up),
                (rim_down_in, rim_down),
                (edges_in, edges0),
            )
        )
    ]
    greet(barrier, greeted)
    for load in loads:
        load.start()

    lane = lax.broadcasted_iota(jnp.int32, (1, LANES), 1)
    low_half = lane < latent
    own_rows = pl.ds(pl.multiple_of(layer * hits, hits), hits)
    swap_rows = pl.ds(pl.multiple_of(layer * half, half), half)

    loads[0].wait()
    loads[1].wait()
    wide_pick = pick(latent, LANES, 0, latent)
    high_pick = pick(latent, LANES, -latent, LANES)
    own_send[...] = (
        nn(feats[...], wide_pick) + nn(cot[...].astype(BF16), high_pick)
    ).astype(BF16)
    pl.semaphore_wait(barrier, len(greeted))
    known = [step for step in (1, 2, 4) if step < n_z // 2]

    def tell(at):
        if at < len(known):
            greet(chain_sem.at[at], [along_z(known[at]), along_z(-known[at])])

    def told(at):
        if at < len(known):
            pl.semaphore_wait(chain_sem.at[at], 2)

    tell(0)
    for peer in layer_peers:
        send(own_send, slab_land.at[own_rows, :], 0, (phi, peer))
    slab_land[own_rows, :] = own_send[...]
    send(rim_up_in, rim_near.at[0], 2, (above, layer))
    send(rim_down_in, rim_near.at[1], 2, (below, layer))

    shard_rows = pl.ds(pl.multiple_of(plane_at * shard, shard), shard)
    stores = [
        pltpu.make_async_copy(src, dst, store_sem.at[at])
        for at, (src, dst) in enumerate(
            (
                (node_out, node_out_to),
                (edge_out, edge_out_to),
                (node_grad, node_grad_to),
                (shard_sum, sums_to.at[shard_rows, :]),
            )
        )
    ]
    swaps = (None, swap_land.at[0], swap_land.at[1])
    x_rows = pl.ds(pl.multiple_of(x_at * hits, hits), hits)
    lower_x_rows = pl.ds(pl.multiple_of(half + x_at * hits, hits), hits)
    pair_rows = pl.ds(pl.multiple_of(x_at * 2 * hits, 2 * hits), 2 * hits)

    def in_order(pairs):
        parts = [
            pairs[(2 * x + side) * hits : (2 * x + side + 1) * hits]
            for side in range(2)
            for x in range(n_x)
        ]
        return jnp.concatenate(parts, axis=0)

    def swap(at, value):
        swaps[at][swap_rows, :] = value.astype(swaps[at].dtype)
        mine = swaps[at].at[swap_rows, :]
        for peer in layer_peers:
            send(mine, mine, 3 + at, (phi, peer))

    def swapped_sum(at):
        wait_bytes(swaps[at].at[pl.ds(0, (n_layer - 1) * half), :], recv_sem.at[3 + at])
        total = swaps[at][0:half, :].astype(F32)
        for turn in range(1, n_layer):
            total = total + swaps[at][turn * half : (turn + 1) * half, :].astype(F32)
        return total

    for load in loads[2:7]:
        load.wait()
    edge_first = first[...]
    source_wide = nn(edge_first, pick(3 * latent, LANES, 0, latent)).astype(BF16)
    target_wide = nn(edge_first, pick(3 * latent, LANES, latent, latent)).astype(BF16)
    source_high = nn(edge_first, pick(3 * latent, LANES, -latent, LANES) * (~low_half).astype(BF16)).astype(BF16)
    target_high = nn(edge_first, pick(3 * latent, LANES, 0, LANES) * (~low_half).astype(BF16)).astype(BF16)
    first_self = edge_first[:, 2 * latent :]
    edge_second = second[...]
    square_eye = pick(latent, latent, 0, latent)
    self_back = nt(square_eye, first_self).astype(BF16)
    second_back = nt(square_eye, edge_second).astype(BF16)
    zero_square = jnp.zeros((latent, latent), BF16)
    gm_pick = jnp.concatenate(
        [
            high_pick,
            nt(square_eye, jnp.concatenate([zero_square, edge_second], axis=0)).astype(BF16),
        ],
        axis=0,
    )
    first_back = jnp.concatenate([source_wide, target_wide], axis=0)
    first_back_high = jnp.concatenate([source_high, target_high], axis=0)
    node_first_wide = jnp.concatenate(
        [node_first[...], jnp.zeros((LANES - latent, 2 * latent), BF16)], axis=0
    )
    gm_back = nt(gm_pick, node_first_wide)
    gm_back = jnp.concatenate([gm_back[0:latent].astype(BF16), two_parts(gm_back[latent:])], axis=0)
    node_second_low = nn(node_second[...], wide_pick).astype(BF16)
    zero_wide = jnp.zeros((LANES - latent, LANES), BF16)
    node_second_wide = jnp.concatenate([node_second_low, zero_wide], axis=0)
    node_second_under = jnp.concatenate([zero_wide, node_second_low], axis=0)
    bias_rows = lax.dot_general(
        biases[...],
        pick(latent, LANES, 0, latent, F32),
        (((1,), (0,)), ((), ())),
        precision=lax.Precision.HIGHEST,
        preferred_element_type=F32,
    )
    bias_cols = nt_exact(pick(latent, latent, 0, latent, F32), biases[...])
    bias_edge = bias_cols[:, 0:1]
    bias_message = bias_cols[:, 1:2]
    bias_node = bias_rows[2:3, :]
    bias_update = bias_rows[3:4, :]
    for load in loads[7:]:
        load.wait()

    def build(cols):
        width = cols.size
        spot = lax.broadcasted_iota(jnp.int32, (1, width), 1) + cols.start
        here = spot < count[...]
        source_at = jnp.where(here, source[:, cols], -1)
        target_at = jnp.where(here, target[:, cols], -1)
        row = lax.broadcasted_iota(jnp.int32, (slab, width), 0)
        onehot[0:slab, cols] = jnp.where(row == source_at, 1.0, 0.0).astype(BF16)
        onehot[slab : 2 * slab, cols] = jnp.where(row == target_at, 1.0, 0.0).astype(BF16)
        rim_row = lax.broadcasted_iota(jnp.int32, (2 * rim, width), 0) + slab
        onehot[2 * slab : 2 * slab + 2 * rim, cols] = jnp.where(
            rim_row == source_at, 1.0, 0.0
        ).astype(BF16)
        z_part[:, cols] = nn(first_self, edges0[:, cols]) + bias_edge

    chunks(slots, build)
    rim_eye = pick(rim, rim, 0, rim)
    for side, index in enumerate((rim_up, rim_down)):
        put = jnp.where(
            lax.broadcasted_iota(jnp.int32, (slab, rim), 0) == index[...], 1.0, 0.0
        ).astype(BF16)
        rim_put[side] = put
        rim_pick[side * rim : (side + 1) * rim, :] = nt(rim_eye, put).astype(BF16)
    grad_own = lax.dot_general(
        cot[...],
        pick(latent, LANES, 0, latent, F32),
        (((1,), (0,)), ((), ())),
        precision=lax.Precision.HIGHEST,
        preferred_element_type=F32,
    )

    wait_bytes(slab_land.at[pl.ds(0, slab - hits), :], recv_sem.at[0])
    told(0)
    tell(1)
    rim_send[...] = nn(rim_pick[...], slab_land[...]).astype(BF16)
    send(rim_send.at[0:rim], rim_land.at[0, 0:rim], 1, (above, layer))
    send(rim_send.at[rim : 2 * rim], rim_land.at[0, rim : 2 * rim], 1, (below, layer))
    table = jnp.where(low_half, slab_land[...].astype(F32), 0.0).astype(BF16)
    table_kept[...] = table
    for k in range(2):
        own_part = two_parts(
            jnp.concatenate([nt(source_wide, table), nt(target_wide, table)], axis=1)
        )

        def own_terms(cols):
            terms = nn(own_part, onehot[0 : 2 * slab, cols])
            z_part[:, cols] = z_part[:, cols] + (terms[0:latent] + terms[latent:])

        chunks(slots, own_terms)
        if k == 0:
            wait_bytes(rim_land.at[0], recv_sem.at[1])
        else:
            wait_bytes(near_land, recv_sem.at[13])
            for side in range(2):
                rim_land[1, side * rim : (side + 1) * rim, :] = nn(
                    near_pick[side * rim : (side + 1) * rim, :], near_land[side]
                ).astype(BF16)
        rim_part = two_parts(nt(source_wide, rim_land[k]))

        def edge_mlp(cols):
            width = cols.size
            terms = nn(rim_part, onehot[2 * slab : 2 * slab + 2 * rim, cols])
            pre = z_part[:, cols] + (terms[0:latent] + terms[latent:])
            gate = logistic(pre)
            hidden = (pre * gate).astype(BF16)
            hidden_in[k, 3 * latent : 4 * latent, cols] = hidden
            slopes[k, :, cols] = gate * (1.0 + pre * (1.0 - gate))
            old = edges0[:, cols] if k == 0 else edge_new[0, 0:latent, cols]
            here = lax.broadcasted_iota(jnp.int32, (1, width), 1) + cols.start < count[...]
            fresh = jnp.where(
                here, old.astype(F32) + nn(edge_second, hidden) + bias_message, 0.0
            ).astype(BF16)
            edge_new[k, 0:latent, cols] = fresh

        chunks(slots, edge_mlp)
        both_halves = nt(onehot[slab : 2 * slab, :], edge_new[k])
        packed = jnp.concatenate([both_halves[0:half], both_halves[half:]], axis=1)
        if k == 0:
            message_send[...] = packed
            for peer in layer_peers:
                spot = pl.ds(pl.multiple_of(lax.rem(peer, n_x) * hits, hits), hits)
                send(message_send.at[spot, :], message_land.at[own_rows, :], 3, (phi, peer))
            message_land[own_rows, :] = message_send[x_rows, :]
            wait_bytes(rim_near, recv_sem.at[2])
            row = lax.broadcasted_iota(jnp.int32, (slab, rim), 0)
            pair_row = lax.rem(row, 2 * hits)
            hit = (
                lax.div(row, 2 * hits) * hits
                + lax.rem(pair_row, hits)
                + lax.div(pair_row, hits) * half
            )
            for side in range(2):
                put = jnp.where(hit == rim_near[side], 1.0, 0.0).astype(BF16)
                near_pick[side * rim : (side + 1) * rim, :] = nt(rim_eye, put).astype(BF16)
        else:
            swap(k, packed)

        raw_own = nt(wide_pick, table).astype(BF16)
        raw_rim = nt(wide_pick, rim_land[k]).astype(BF16)

        def inputs(cols):
            hidden_in[k, 0:latent, cols] = (
                nn(raw_own, onehot[0:slab, cols])
                + nn(raw_rim, onehot[2 * slab : 2 * slab + 2 * rim, cols])
            ).astype(BF16)
            hidden_in[k, latent : 2 * latent, cols] = nn(
                raw_own, onehot[slab : 2 * slab, cols]
            ).astype(BF16)
            if k == 0:
                old = edges0[:, cols]
                z_part[:, cols] = nn(first_self, edge_new[0, 0:latent, cols]) + bias_edge
            else:
                old = edge_new[0, 0:latent, cols]
                edge_out[:, cols] = edge_new[1, 0:latent, cols]
            hidden_in[k, 2 * latent : 3 * latent, cols] = old

        chunks(slots, inputs)
        if k == 0:
            wait_bytes(message_land.at[pl.ds(0, (n_layer - 1) * hits), :], recv_sem.at[3])
            packed = message_land[0:hits, :]
            for turn in range(1, n_layer):
                packed = packed + message_land[turn * hits : (turn + 1) * hits, :]
            upper_old = table_kept[x_rows, :].astype(F32)
            lower_old = table_kept[lower_x_rows, :].astype(F32)
        else:
            packed = swapped_sum(k)
            table_wide = table.astype(F32)
            upper_old, lower_old = table_wide[0:half], table_wide[half:]
        told(1 + k)
        if k == 0:
            tell(2)
        node_old = jnp.concatenate([upper_old, lower_old], axis=0)
        node_in = jnp.concatenate(
            [
                jnp.where(low_half, upper_old, pltpu.roll(packed, latent, 1)),
                jnp.where(low_half, lower_old, packed),
            ],
            axis=0,
        ).astype(BF16)
        node_pre = nt(node_in, node_first_wide) + bias_node
        node_gate = logistic(node_pre)
        node_hidden = (node_pre * node_gate).astype(BF16)
        node_slope = node_gate * (1.0 + node_pre * (1.0 - node_gate))
        table = (node_old + nt(node_hidden, node_second_wide) + bias_update).astype(BF16)
        if k == 0:
            turned = pltpu.roll(node_slope, latent, 1)
            pairs_land[pair_rows, :] = jnp.where(low_half, table.astype(F32), turned).astype(BF16)
            mine = pairs_land.at[pair_rows, :]
            for (step,) in far_first((n_x,)):
                send(mine, mine, 12, (phi, y_hi * n_x + x_of[step]))
            for x in x_of[::-1]:
                for side, slab_at in enumerate((above, below)):
                    send(mine, near_land.at[side, pair_rows, :], 13, (slab_at, y_hi * n_x + x))
            node_kept[0, 0, 0 : 2 * hits] = node_in
            node_kept[0, 1, 0 : 2 * hits] = node_hidden
            if n_x > 1:
                wait_bytes(pairs_land.at[pl.ds(0, (n_x - 1) * 2 * hits), :], recv_sem.at[12])
            gathered = in_order(pairs_land[...].astype(F32))
            table = jnp.where(low_half, gathered, 0.0).astype(BF16)
            first_slope = pltpu.roll(gathered, latent, 1)
        else:
            node_kept[1, 0] = node_in
            node_kept[1, 1] = node_hidden
            stores[1].start()

    for k in (1, 0):
        if k == 1:
            pre_back = nn(slab_land[...], node_second_under) * node_slope
        else:
            grad_low = grad_now.astype(BF16)
            pre_back = nn(grad_low, node_second_wide) * first_slope
        pre_low = pre_back.astype(BF16)
        in_back = nn(pre_low, node_first_wide)
        gm_part = nt(gm_back, pre_low)
        gm_part = jnp.concatenate(
            [
                gm_part[0:latent].astype(BF16),
                two_parts(gm_part[latent : 2 * latent] + gm_part[2 * latent :]),
            ],
            axis=0,
        )

        def column_at(at, sums):
            return jnp.where(lane == latent + at, jnp.sum(sums, axis=1, keepdims=True), 0.0)

        def node_terms():
            kept_rows = (
                pl.ds(pl.multiple_of(y_hi * hits, hits), hits) if k == 0 else own_rows
            )
            grad_kept[0] = pre_back
            grad_kept[1] = in_back
            if k == 0:
                grad_kept[2] = gained
                grad_mine = grad_own + grad_kept[2, own_rows, :]
            else:
                grad_mine = grad_own
            pre_mine = grad_kept[0, own_rows, :]
            pre_turned = nt(wide_pick, pre_mine.astype(BF16))
            grad_turned = nt(wide_pick, grad_mine.astype(BF16))
            return (
                nn(pre_turned.astype(BF16), node_kept[k, 0, kept_rows, :]),
                nn(grad_turned.astype(BF16), node_kept[k, 1, kept_rows, :])
                + column_at(2, pre_turned)
                + column_at(3, grad_turned),
                grad_mine + jnp.where(low_half, grad_kept[1, own_rows, :], 0.0),
            )

        if k == 1:
            bias_sums[...] = jnp.zeros_like(bias_sums)
        else:
            first_terms, second_terms, grad_own = node_terms()
            grads[2 * latent : 3 * latent, :] = grads[2 * latent : 3 * latent, :] + first_terms
            grads[3 * latent : 4 * latent, :] = grads[3 * latent : 4 * latent, :] + second_terms

        def folded(value):
            pieces = [
                value[:, at : at + LANES] for at in range(0, value.shape[1], LANES)
            ]
            return functools.reduce(lambda one, other: one + other, pieces)

        def edge_back(cols):
            both = nn(gm_part, onehot[slab : 2 * slab, cols])
            edge_grad = both[0:latent]
            hidden_grad = both[latent : 2 * latent] + both[2 * latent :]
            if k == 0:
                edge_grad = edge_grad + grad_edge[:, cols]
                hidden_grad = hidden_grad + second_grad_edge[:, cols]
            else:
                grad_edge[:, cols] = edge_grad
            pre_grad = hidden_grad * slopes[k, :, cols]
            bias_sums[0] = bias_sums[0] + folded(pre_grad)
            bias_sums[1] = bias_sums[1] + folded(edge_grad)
            pre_grad = pre_grad.astype(BF16)
            back_stack[0:latent, cols] = pre_grad
            back_stack[latent : 2 * latent, cols] = pre_grad
            back_stack[2 * latent : 3 * latent, cols] = edge_grad.astype(BF16)

        chunks(slots, edge_back)

        def weight_terms():
            outer = nt(back_stack[latent : 3 * latent, :], hidden_in[k])
            upper = outer[0:latent, 0:LANES]
            lower = jnp.where(low_half, outer[0:latent, LANES:], outer[latent:, LANES:])
            return upper, lower

        if k == 0:
            upper, lower = weight_terms()
            grads[0:latent, :] = grads[0:latent, :] + upper
            grads[latent : 2 * latent, :] = grads[latent : 2 * latent, :] + lower

        if k == 0:
            grads[3 * latent : 4 * latent, :] = (
                grads[3 * latent : 4 * latent, :]
                + column_at(0, bias_sums[0])
                + column_at(1, bias_sums[1])
            )
            for at, (device, spot) in enumerate(plane_peers):
                send(
                    grads.at[pl.ds(pl.multiple_of(spot * shard, shard), shard), :],
                    plane_land.at[pl.ds(at * shard, shard), :],
                    6,
                    device,
                )

        back_send[k] = nt(
            onehot[2 * slab : 2 * slab + 2 * rim, :], back_stack[0 : 2 * latent, :]
        ).astype(BF16)
        send(back_send.at[k, 0:rim], back_land.at[k, 0:rim], 7 + k, (below, layer))
        send(
            back_send.at[k, rim : 2 * rim],
            back_land.at[k, rim : 2 * rim],
            7 + k,
            (above, layer),
        )
        from_source = nt(onehot[0:slab, :], back_stack[0 : 2 * latent, :])
        from_target = nt(onehot[slab : 2 * slab, :], back_stack[0 : 2 * latent, :])
        if k == 0:
            wait_bytes(plane_land, recv_sem.at[6])
            total = grads[shard_rows, :]
            for turn in range(n_plane - 1):
                total = total + plane_land[turn * shard : (turn + 1) * shard, :]
            z_rows = pl.ds(pl.multiple_of(z_at * shard, shard), shard)
            z_land[z_rows, :] = total
            for peer in z_peers:
                send(z_land.at[z_rows, :], z_land.at[z_rows, :], 9, peer)
        wait_bytes(back_land.at[k], recv_sem.at[7 + k])
        from_source = (
            from_source
            + nn(rim_put[0], back_land[k, 0:rim])
            + nn(rim_put[1], back_land[k, rim : 2 * rim])
        )
        comb = jnp.where(low_half, from_source, from_target).astype(BF16)
        packed = nn(comb[0:half], first_back) + nn(comb[half:], first_back_high)
        if k == 1:
            swap(2, packed)
            upper, lower = weight_terms()
            first_terms, second_terms, grad_own = node_terms()
            grads[0:latent, :] = upper
            grads[latent : 2 * latent, :] = lower
            grads[2 * latent : 3 * latent, :] = first_terms
            grads[3 * latent : 4 * latent, :] = second_terms
            node_kept[1, 0] = table
            node_out[...] = node_kept[1, 0, own_rows, 0:latent]
            stores[0].start()

            def carried(cols):
                old = grad_edge[:, cols] + nn(self_back, back_stack[0:latent, cols])
                grad_edge[:, cols] = old
                second_grad_edge[:, cols] = nn(second_back, old.astype(BF16))

            chunks(slots, carried)
            cot_slab = pltpu.roll(slab_land[...].astype(F32), latent, 1)
            grad_before = jnp.where(low_half, cot_slab + in_back, 0.0)
            packed = swapped_sum(2)
            gained = jnp.concatenate(
                [
                    jnp.where(low_half, packed, 0.0),
                    jnp.where(low_half, pltpu.roll(packed, latent, 1), 0.0),
                ],
                axis=0,
            )
            grad_now = grad_before + gained
        else:
            comb_send[...] = packed.astype(BF16)

            def rows_of(device):
                return pl.ds(pl.multiple_of(lax.rem(device, n_layer // 2) * hits, hits), hits)

            for at, peer in enumerate(layer_peers):
                send(
                    comb_send.at[rows_of(peer), :],
                    comb_land.at[pl.ds(at * hits, hits), :],
                    10,
                    (phi, peer),
                )
            wait_bytes(z_land.at[pl.ds(0, (n_z - 1) * shard), :], recv_sem.at[9])
            total = z_land[0:shard, :]
            for turn in range(1, n_z):
                total = total + z_land[turn * shard : (turn + 1) * shard, :]
            shard_sum[...] = total
            for device, _ in plane_peers:
                send(shard_sum, sums_to.at[shard_rows, :], 11, device)
            stores[3].start()
            wait_bytes(comb_land, recv_sem.at[10])
            total = comb_send[rows_of(layer), :].astype(F32)
            for turn in range(n_layer - 1):
                total = total + comb_land[turn * hits : (turn + 1) * hits, :].astype(F32)
            total = jnp.where(layer < n_layer // 2, total, pltpu.roll(total, latent, 1))
            node_grad[...] = (grad_own + total)[:, 0:latent]
            stores[2].start()

    wait_bytes(slab_land.at[pl.ds(0, slab - hits), :], send_sem.at[0])
    wait_bytes(rim_send, send_sem.at[1])
    wait_bytes(rim_near, send_sem.at[2])
    wait_bytes(message_land.at[pl.ds(0, (n_layer - 1) * hits), :], send_sem.at[3])
    if n_x > 1:
        wait_bytes(pairs_land.at[pl.ds(0, (n_x - 1) * 2 * hits), :], send_sem.at[12])
    wait_bytes(near_land, send_sem.at[13])
    for k in range(2):
        wait_bytes(back_send.at[k], send_sem.at[7 + k])
    for at in range(1, 3):
        wait_bytes(swaps[at].at[pl.ds(0, (n_layer - 1) * half), :], send_sem.at[3 + at])
    wait_bytes(plane_land, send_sem.at[6])
    wait_bytes(z_land.at[pl.ds(0, (n_z - 1) * shard), :], send_sem.at[9])
    wait_bytes(comb_land, send_sem.at[10])
    wait_bytes(plane_land, send_sem.at[11])
    for store in stores:
        store.wait()
    wait_bytes(sums_to.at[pl.ds(0, (n_plane - 1) * shard), :], recv_sem.at[11])


def deliver(*refs):
    sources, targets, held, sums = refs[:4], refs[4:12], refs[12:20], refs[20]
    in_sem, out_sem = refs[21:]
    first, second, node_first, node_second, biases = held[3:]
    latent = second.shape[0]
    loads = [
        pltpu.make_async_copy(sources[at], dst, in_sem.at[at])
        for at, dst in enumerate((*held[:3], sums))
    ]
    stores = [
        pltpu.make_async_copy(held[at], targets[at], out_sem.at[at]) for at in range(8)
    ]
    for load in loads[::-1]:
        load.start()
    loads[3].wait()
    first[:, 0:LANES] = sums[0:latent, :]
    first[:, LANES:] = sums[latent : 2 * latent, 0:latent]
    second[...] = pltpu.roll(sums[latent : 2 * latent, :], latent, 1)[:, 0:latent]
    node_first[...] = sums[2 * latent : 3 * latent, :]
    node_second[...] = sums[3 * latent : 4 * latent, 0:latent]
    biases[...] = sums[3 * latent : 4 * latent, :].T[latent : latent + 4, :]
    for store in stores[3:]:
        store.start()
    for load, store in zip(loads[:3], stores):
        load.wait()
        store.start()
    for store in stores:
        store.wait()


def body(n_phi, n_layer, *arrays):
    node_feats, edge_feats, edge_source, edge_target, *others, node_cot = arrays
    latent, hits = node_feats.shape
    slots = edge_feats.shape[1]
    slab = hits * n_layer
    rim = others[1].shape[1]
    n_plane = Y_LO * CORES * n_layer
    n_z = n_phi // (Y_LO * CORES)
    grad_rows = 4 * latent
    shard = grad_rows // n_plane
    hbm = pl.BlockSpec(memory_space=pltpu.HBM)
    operands = (
        node_feats.T,
        edge_feats,
        edge_source.reshape(1, slots),
        edge_target.reshape(1, slots),
        *others,
        node_cot.T,
    )
    outs = [
        jax.ShapeDtypeStruct(*out)
        for out in (
            ((hits, latent), BF16),
            ((latent, slots), BF16),
            ((hits, latent), F32),
            ((latent, 3 * latent), F32),
            ((latent, latent), F32),
            ((latent, 2 * latent), F32),
            ((latent, latent), F32),
            ((4, latent), F32),
        )
    ]
    results = pl.pallas_call(
        functools.partial(kernel, n_phi, n_layer),
        out_shape=[*outs[:3], jax.ShapeDtypeStruct((grad_rows, LANES), F32)],
        in_specs=[hbm] * len(operands),
        out_specs=[hbm] * 4,
        scratch_shapes=[pltpu.VMEM(array.shape, array.dtype) for array in (*operands, *outs[:3])]
        + [
            pltpu.VMEM((2 * slab + 2 * rim, slots), BF16),
            pltpu.VMEM((2 * rim, slab), BF16),
            pltpu.VMEM((2, slab, rim), BF16),
            pltpu.VMEM((2, 4 * latent, slots), BF16),
            pltpu.VMEM((2, latent, slots), BF16),
            pltpu.VMEM((latent, slots), F32),
            pltpu.VMEM((2, latent, slots), F32),
            pltpu.VMEM((latent, slots), F32),
            pltpu.VMEM((latent, slots), F32),
            pltpu.VMEM((3 * latent, slots), BF16),
            pltpu.VMEM((2, latent, LANES), F32),
            pltpu.VMEM((2, 2, slab, LANES), BF16),
            pltpu.VMEM((3, slab, LANES), F32),
            pltpu.VMEM((hits, LANES), BF16),
            pltpu.VMEM((slab, LANES), BF16),
            pltpu.VMEM((slab, LANES), BF16),
            pltpu.VMEM((2, 1, rim), jnp.int32),
            pltpu.VMEM((2 * rim, slab), BF16),
            pltpu.VMEM((2, slab, LANES), BF16),
            pltpu.VMEM((slab, LANES), BF16),
            pltpu.VMEM((2 * rim, LANES), BF16),
            pltpu.VMEM((2, 2 * rim, LANES), BF16),
            pltpu.VMEM((slab // 2, LANES), F32),
            pltpu.VMEM((slab, LANES), F32),
            pltpu.VMEM((2, n_layer * slab // 2, LANES), BF16),
            pltpu.VMEM((2, 2 * rim, LANES), BF16),
            pltpu.VMEM((2, 2 * rim, LANES), BF16),
            pltpu.VMEM((slab // 2, LANES), BF16),
            pltpu.VMEM(((n_layer - 1) * hits, LANES), BF16),
            pltpu.VMEM((grad_rows, LANES), F32),
            pltpu.VMEM(((n_plane - 1) * shard, LANES), F32),
            pltpu.VMEM((n_z * shard, LANES), F32),
            pltpu.VMEM((shard, LANES), F32),
            pltpu.SemaphoreType.DMA((len(operands),)),
            pltpu.SemaphoreType.DMA((4,)),
            pltpu.SemaphoreType.REGULAR((3,)),
            pltpu.SemaphoreType.DMA((14,)),
            pltpu.SemaphoreType.DMA((14,)),
        ],
        compiler_params=pltpu.CompilerParams(
            collective_id=0, has_side_effects=True, vmem_limit_bytes=VMEM_BYTES
        ),
    )(*operands)
    node_out, edge_out, node_grad, *totals = pl.pallas_call(
        deliver,
        out_shape=outs,
        in_specs=[hbm] * 4,
        out_specs=[hbm] * len(outs),
        scratch_shapes=[pltpu.VMEM(out.shape, out.dtype) for out in outs]
        + [
            pltpu.VMEM((grad_rows, LANES), F32),
            pltpu.SemaphoreType.DMA((4,)),
            pltpu.SemaphoreType.DMA((len(outs),)),
        ],
        compiler_params=pltpu.CompilerParams(vmem_limit_bytes=VMEM_BYTES),
    )(*results)
    return node_out.T, edge_out, node_grad.T, *totals


def solution(mesh):
    split = P(None, ("phi", "layer"))
    return jax.shard_map(
        functools.partial(body, mesh.shape["phi"], mesh.shape["layer"]),
        mesh=mesh,
        in_specs=(
            split,
            split,
            P(("phi", "layer")),
            P(("phi", "layer")),
            P("phi", "layer"),
            P("phi", None),
            P("phi", None),
            P(),
            P(),
            P(),
            P(),
            P(),
            split,
        ),
        out_specs=(split, split, split, P(), P(), P(), P(), P()),
        check_vma=False,
    )
```

```python
import functools
import itertools

import jax
import jax.numpy as jnp
from jax import lax
from jax.experimental import pallas as pl
from jax.experimental.pallas import tpu as pltpu
from jax.sharding import PartitionSpec as P

MESH = pl.DeviceIdType.MESH
BF16 = jnp.bfloat16
F32 = jnp.float32
LANES = 128
Y_LO = 2
CORES = 2
CHUNK = 2048
VMEM_BYTES = 64 * 1024 * 1024


def nn(left, right):
    return lax.dot_general(left, right, (((1,), (0,)), ((), ())), preferred_element_type=F32)


def nt(left, right):
    return lax.dot_general(left, right, (((1,), (1,)), ((), ())), preferred_element_type=F32)


def nt_exact(left, right):
    return lax.dot_general(
        left,
        right,
        (((1,), (1,)), ((), ())),
        precision=lax.Precision.HIGHEST,
        preferred_element_type=F32,
    )


def pick(rows, cols, row_shift, col_limit, dtype=BF16):
    row = lax.broadcasted_iota(jnp.int32, (rows, cols), 0)
    col = lax.broadcasted_iota(jnp.int32, (rows, cols), 1)
    return jnp.where((row == col + row_shift) & (col < col_limit), 1.0, 0.0).astype(dtype)


def two_parts(value):
    main = value.astype(BF16)
    return jnp.concatenate([main, (value - main.astype(F32)).astype(BF16)], axis=0)


def logistic(value):
    return 0.5 * jnp.tanh(0.5 * value) + 0.5


def chunks(total, step):
    size = min(CHUNK, total)

    def run(turn, carry):
        step(pl.ds(pl.multiple_of(turn * size, size), size))
        return carry

    lax.fori_loop(0, total // size, run, 0, unroll=True)


def wait_bytes(ref, sem):
    pltpu.make_async_copy(ref, ref, sem).wait()


def far_first(sizes):
    steps = list(itertools.product(*(range(size) for size in sizes)))
    hops = lambda step: sum(min(at, size - at) for at, size in zip(step, sizes))
    return sorted(steps[1:], key=hops, reverse=True)


def kernel(
    n_phi,
    n_layer,
    feats_in,
    edges_in,
    source_in,
    target_in,
    count_in,
    rim_up_in,
    rim_down_in,
    first_in,
    second_in,
    node_first_in,
    node_second_in,
    biases_in,
    cot_in,
    node_out_to,
    edge_out_to,
    node_grad_to,
    sums_to,
    feats,
    edges0,
    source,
    target,
    count,
    rim_up,
    rim_down,
    first,
    second,
    node_first,
    node_second,
    biases,
    cot,
    node_out,
    edge_out,
    node_grad,
    onehot,
    rim_pick,
    rim_put,
    hidden_in,
    edge_new,
    z_part,
    slopes,
    grad_edge,
    second_grad_edge,
    back_stack,
    bias_sums,
    node_kept,
    grad_kept,
    own_send,
    slab_land,
    table_kept,
    rim_near,
    near_pick,
    near_land,
    pairs_land,
    rim_send,
    rim_land,
    message_send,
    message_land,
    swap_land,
    back_send,
    back_land,
    comb_send,
    comb_land,
    grads,
    plane_land,
    z_land,
    shard_sum,
    load_sem,
    store_sem,
    chain_sem,
    send_sem,
    recv_sem,
):
    hits, latent = feats.shape
    slots = edges0.shape[1]
    slab = hits * n_layer
    half = slab // 2
    rim = rim_up.shape[1]
    n_z = n_phi // (Y_LO * CORES)
    n_plane = Y_LO * CORES * n_layer
    n_x = n_layer // 2
    n_y = 2 * Y_LO
    shard = grads.shape[0] // n_plane
    phi = lax.axis_index("phi")
    layer = lax.axis_index("layer")
    core = lax.rem(phi, CORES)
    z_at = lax.rem(lax.div(phi, CORES), n_z)
    y_lo = lax.div(phi, CORES * n_z)
    y_hi = lax.div(layer, n_x)
    x_at = lax.rem(layer, n_x)
    y_at = y_hi * Y_LO + y_lo
    plane_at = (y_lo * CORES + core) * n_layer + layer
    above = lax.rem(phi + 1, n_phi)
    below = lax.rem(phi + n_phi - 1, n_phi)

    x_of = [lax.rem(x_at + step, n_x) for step in range(n_x)]
    y_hi_of = [lax.rem(y_hi + step, 2) * n_x for step in range(2)]
    layer_peers = [
        y_hi_of[dy // Y_LO] + x_of[dx]
        for dy, dx in far_first((n_y, n_x))
        if dy % Y_LO == 0
    ]
    y_of = [lax.rem(y_at + step, n_y) for step in range(n_y)]
    pair_of = [lax.rem(y, Y_LO) * CORES for y in y_of]
    phi_base = [lax.rem(y, Y_LO) * (CORES * n_z) + z_at * CORES for y in y_of]
    layer_base = [lax.div(y, Y_LO) * n_x for y in y_of]
    core_of = [core, 1 - core]
    plane_peers = []
    for dy, dx, dc in far_first((n_y, n_x, CORES)):
        device = (phi_base[dy] + core_of[dc], layer_base[dy] + x_of[dx])
        plane_peers.append((device, (pair_of[dy] + core_of[dc]) * n_layer + device[1]))
    z_peers = [
        (y_lo * (CORES * n_z) + lax.rem(z_at + step, n_z) * CORES + core, layer)
        for (step,) in far_first((n_z,))
    ]

    def send(src, dst, step, device):
        pltpu.make_async_remote_copy(
            src_ref=src,
            dst_ref=dst,
            send_sem=send_sem.at[step],
            recv_sem=recv_sem.at[step],
            device_id=device,
            device_id_type=MESH,
        ).start()

    barrier = pltpu.get_barrier_semaphore()

    def along_z(step):
        return y_lo * (CORES * n_z) + lax.rem(z_at + step + n_z, n_z) * CORES + core, layer

    def greet(sem, devices):
        for device in devices:
            pl.semaphore_signal(sem, inc=1, device_id=device, device_id_type=MESH)

    greeted = [(phi, peer) for peer in layer_peers] + [
        (phi_base[0] + 1 - core, layer),
        (phi_base[0] + (1 - 2 * y_lo) * (CORES * n_z) + core, layer),
        (phi_base[0] + (1 - 2 * y_lo) * (CORES * n_z) + 1 - core, layer),
        (above, layer),
        (below, layer),
        along_z(1),
        along_z(-1),
    ]
    loads = [
        pltpu.make_async_copy(src, dst, load_sem.at[at])
        for at, (src, dst) in enumerate(
            (
                (feats_in, feats),
                (cot_in, cot),
                (first_in, first),
                (biases_in, biases),
                (second_in, second),
                (node_first_in, node_first),
                (node_second_in, node_second),
                (count_in, count),
                (source_in, source),
                (target_in, target),
                (rim_up_in, rim_up),
                (rim_down_in, rim_down),
                (edges_in, edges0),
            )
        )
    ]
    greet(barrier, greeted)
    for load in loads:
        load.start()

    lane = lax.broadcasted_iota(jnp.int32, (1, LANES), 1)
    low_half = lane < latent
    own_rows = pl.ds(pl.multiple_of(layer * hits, hits), hits)
    swap_rows = pl.ds(pl.multiple_of(layer * half, half), half)

    loads[0].wait()
    loads[1].wait()
    wide_pick = pick(latent, LANES, 0, latent)
    high_pick = pick(latent, LANES, -latent, LANES)
    own_send[...] = (
        nn(feats[...], wide_pick) + nn(cot[...].astype(BF16), high_pick)
    ).astype(BF16)
    pl.semaphore_wait(barrier, len(greeted))
    known = [step for step in (1, 2, 4) if step < n_z // 2]

    def tell(at):
        if at < len(known):
            greet(chain_sem.at[at], [along_z(known[at]), along_z(-known[at])])

    def told(at):
        if at < len(known):
            pl.semaphore_wait(chain_sem.at[at], 2)

    tell(0)
    for peer in layer_peers:
        send(own_send, slab_land.at[own_rows, :], 0, (phi, peer))
    slab_land[own_rows, :] = own_send[...]
    send(rim_up_in, rim_near.at[0], 2, (above, layer))
    send(rim_down_in, rim_near.at[1], 2, (below, layer))

    shard_rows = pl.ds(pl.multiple_of(plane_at * shard, shard), shard)
    stores = [
        pltpu.make_async_copy(src, dst, store_sem.at[at])
        for at, (src, dst) in enumerate(
            (
                (node_out, node_out_to),
                (edge_out, edge_out_to),
                (node_grad, node_grad_to),
                (shard_sum, sums_to.at[shard_rows, :]),
            )
        )
    ]
    swaps = (None, swap_land.at[0], swap_land.at[1])
    x_rows = pl.ds(pl.multiple_of(x_at * hits, hits), hits)
    lower_x_rows = pl.ds(pl.multiple_of(half + x_at * hits, hits), hits)
    pair_rows = pl.ds(pl.multiple_of(x_at * 2 * hits, 2 * hits), 2 * hits)

    def in_order(pairs):
        parts = [
            pairs[(2 * x + side) * hits : (2 * x + side + 1) * hits]
            for side in range(2)
            for x in range(n_x)
        ]
        return jnp.concatenate(parts, axis=0)

    def swap(at, value):
        swaps[at][swap_rows, :] = value.astype(swaps[at].dtype)
        mine = swaps[at].at[swap_rows, :]
        for peer in layer_peers:
            send(mine, mine, 3 + at, (phi, peer))

    def swapped_sum(at):
        wait_bytes(swaps[at].at[pl.ds(0, (n_layer - 1) * half), :], recv_sem.at[3 + at])
        total = swaps[at][0:half, :].astype(F32)
        for turn in range(1, n_layer):
            total = total + swaps[at][turn * half : (turn + 1) * half, :].astype(F32)
        return total

    for load in loads[2:7]:
        load.wait()
    edge_first = first[...]
    source_wide = nn(edge_first, pick(3 * latent, LANES, 0, latent)).astype(BF16)
    target_wide = nn(edge_first, pick(3 * latent, LANES, latent, latent)).astype(BF16)
    source_high = nn(edge_first, pick(3 * latent, LANES, -latent, LANES) * (~low_half).astype(BF16)).astype(BF16)
    target_high = nn(edge_first, pick(3 * latent, LANES, 0, LANES) * (~low_half).astype(BF16)).astype(BF16)
    first_self = edge_first[:, 2 * latent :]
    edge_second = second[...]
    square_eye = pick(latent, latent, 0, latent)
    self_back = nt(square_eye, first_self).astype(BF16)
    second_back = nt(square_eye, edge_second).astype(BF16)
    zero_square = jnp.zeros((latent, latent), BF16)
    gm_pick = jnp.concatenate(
        [
            high_pick,
            nt(square_eye, jnp.concatenate([zero_square, edge_second], axis=0)).astype(BF16),
        ],
        axis=0,
    )
    first_back = jnp.concatenate([source_wide, target_wide], axis=0)
    first_back_high = jnp.concatenate([source_high, target_high], axis=0)
    node_first_wide = jnp.concatenate(
        [node_first[...], jnp.zeros((LANES - latent, 2 * latent), BF16)], axis=0
    )
    gm_back = nt(gm_pick, node_first_wide)
    gm_back = jnp.concatenate([gm_back[0:latent].astype(BF16), two_parts(gm_back[latent:])], axis=0)
    node_second_low = nn(node_second[...], wide_pick).astype(BF16)
    zero_wide = jnp.zeros((LANES - latent, LANES), BF16)
    node_second_wide = jnp.concatenate([node_second_low, zero_wide], axis=0)
    node_second_under = jnp.concatenate([zero_wide, node_second_low], axis=0)
    bias_rows = lax.dot_general(
        biases[...],
        pick(latent, LANES, 0, latent, F32),
        (((1,), (0,)), ((), ())),
        precision=lax.Precision.HIGHEST,
        preferred_element_type=F32,
    )
    bias_cols = nt_exact(pick(latent, latent, 0, latent, F32), biases[...])
    bias_edge = bias_cols[:, 0:1]
    bias_message = bias_cols[:, 1:2]
    bias_node = bias_rows[2:3, :]
    bias_update = bias_rows[3:4, :]
    for load in loads[7:]:
        load.wait()

    def build(cols):
        width = cols.size
        spot = lax.broadcasted_iota(jnp.int32, (1, width), 1) + cols.start
        here = spot < count[...]
        source_at = jnp.where(here, source[:, cols], -1)
        target_at = jnp.where(here, target[:, cols], -1)
        row = lax.broadcasted_iota(jnp.int32, (slab, width), 0)
        onehot[0:slab, cols] = jnp.where(row == source_at, 1.0, 0.0).astype(BF16)
        onehot[slab : 2 * slab, cols] = jnp.where(row == target_at, 1.0, 0.0).astype(BF16)
        rim_row = lax.broadcasted_iota(jnp.int32, (2 * rim, width), 0) + slab
        onehot[2 * slab : 2 * slab + 2 * rim, cols] = jnp.where(
            rim_row == source_at, 1.0, 0.0
        ).astype(BF16)
        z_part[:, cols] = nn(first_self, edges0[:, cols]) + bias_edge

    chunks(slots, build)
    rim_eye = pick(rim, rim, 0, rim)
    for side, index in enumerate((rim_up, rim_down)):
        put = jnp.where(
            lax.broadcasted_iota(jnp.int32, (slab, rim), 0) == index[...], 1.0, 0.0
        ).astype(BF16)
        rim_put[side] = put
        rim_pick[side * rim : (side + 1) * rim, :] = nt(rim_eye, put).astype(BF16)
    grad_own = lax.dot_general(
        cot[...],
        pick(latent, LANES, 0, latent, F32),
        (((1,), (0,)), ((), ())),
        precision=lax.Precision.HIGHEST,
        preferred_element_type=F32,
    )

    wait_bytes(slab_land.at[pl.ds(0, slab - hits), :], recv_sem.at[0])
    told(0)
    tell(1)
    rim_send[...] = nn(rim_pick[...], slab_land[...]).astype(BF16)
    send(rim_send.at[0:rim], rim_land.at[0, 0:rim], 1, (above, layer))
    send(rim_send.at[rim : 2 * rim], rim_land.at[0, rim : 2 * rim], 1, (below, layer))
    table = jnp.where(low_half, slab_land[...].astype(F32), 0.0).astype(BF16)
    table_kept[...] = table
    for k in range(2):
        own_part = two_parts(
            jnp.concatenate([nt(source_wide, table), nt(target_wide, table)], axis=1)
        )

        def own_terms(cols):
            terms = nn(own_part, onehot[0 : 2 * slab, cols])
            z_part[:, cols] = z_part[:, cols] + (terms[0:latent] + terms[latent:])

        chunks(slots, own_terms)
        if k == 0:
            wait_bytes(rim_land.at[0], recv_sem.at[1])
        else:
            wait_bytes(near_land, recv_sem.at[13])
            for side in range(2):
                rim_land[1, side * rim : (side + 1) * rim, :] = nn(
                    near_pick[side * rim : (side + 1) * rim, :], near_land[side]
                ).astype(BF16)
        rim_part = two_parts(nt(source_wide, rim_land[k]))

        def edge_mlp(cols):
            width = cols.size
            terms = nn(rim_part, onehot[2 * slab : 2 * slab + 2 * rim, cols])
            pre = z_part[:, cols] + (terms[0:latent] + terms[latent:])
            gate = logistic(pre)
            hidden = (pre * gate).astype(BF16)
            hidden_in[k, 3 * latent : 4 * latent, cols] = hidden
            slopes[k, :, cols] = gate * (1.0 + pre * (1.0 - gate))
            old = edges0[:, cols] if k == 0 else edge_new[0, 0:latent, cols]
            here = lax.broadcasted_iota(jnp.int32, (1, width), 1) + cols.start < count[...]
            fresh = jnp.where(
                here, old.astype(F32) + nn(edge_second, hidden) + bias_message, 0.0
            ).astype(BF16)
            edge_new[k, 0:latent, cols] = fresh

        chunks(slots, edge_mlp)
        both_halves = nt(onehot[slab : 2 * slab, :], edge_new[k])
        packed = jnp.concatenate([both_halves[0:half], both_halves[half:]], axis=1)
        if k == 0:
            message_send[...] = packed
            for peer in layer_peers:
                spot = pl.ds(pl.multiple_of(lax.rem(peer, n_x) * hits, hits), hits)
                send(message_send.at[spot, :], message_land.at[own_rows, :], 3, (phi, peer))
            message_land[own_rows, :] = message_send[x_rows, :]
            wait_bytes(rim_near, recv_sem.at[2])
            row = lax.broadcasted_iota(jnp.int32, (slab, rim), 0)
            pair_row = lax.rem(row, 2 * hits)
            hit = (
                lax.div(row, 2 * hits) * hits
                + lax.rem(pair_row, hits)
                + lax.div(pair_row, hits) * half
            )
            for side in range(2):
                put = jnp.where(hit == rim_near[side], 1.0, 0.0).astype(BF16)
                near_pick[side * rim : (side + 1) * rim, :] = nt(rim_eye, put).astype(BF16)
        else:
            swap(k, packed)

        raw_own = nt(wide_pick, table).astype(BF16)
        raw_rim = nt(wide_pick, rim_land[k]).astype(BF16)

        def inputs(cols):
            hidden_in[k, 0:latent, cols] = (
                nn(raw_own, onehot[0:slab, cols])
                + nn(raw_rim, onehot[2 * slab : 2 * slab + 2 * rim, cols])
            ).astype(BF16)
            hidden_in[k, latent : 2 * latent, cols] = nn(
                raw_own, onehot[slab : 2 * slab, cols]
            ).astype(BF16)
            if k == 0:
                old = edges0[:, cols]
                z_part[:, cols] = nn(first_self, edge_new[0, 0:latent, cols]) + bias_edge
            else:
                old = edge_new[0, 0:latent, cols]
                edge_out[:, cols] = edge_new[1, 0:latent, cols]
            hidden_in[k, 2 * latent : 3 * latent, cols] = old

        chunks(slots, inputs)
        if k == 0:
            wait_bytes(message_land.at[pl.ds(0, (n_layer - 1) * hits), :], recv_sem.at[3])
            packed = message_land[0:hits, :]
            for turn in range(1, n_layer):
                packed = packed + message_land[turn * hits : (turn + 1) * hits, :]
            upper_old = table_kept[x_rows, :].astype(F32)
            lower_old = table_kept[lower_x_rows, :].astype(F32)
        else:
            packed = swapped_sum(k)
            table_wide = table.astype(F32)
            upper_old, lower_old = table_wide[0:half], table_wide[half:]
        told(1 + k)
        if k == 0:
            tell(2)
        node_old = jnp.concatenate([upper_old, lower_old], axis=0)
        node_in = jnp.concatenate(
            [
                jnp.where(low_half, upper_old, pltpu.roll(packed, latent, 1)),
                jnp.where(low_half, lower_old, packed),
            ],
            axis=0,
        ).astype(BF16)
        node_pre = nt(node_in, node_first_wide) + bias_node
        node_gate = logistic(node_pre)
        node_hidden = (node_pre * node_gate).astype(BF16)
        node_slope = node_gate * (1.0 + node_pre * (1.0 - node_gate))
        table = (node_old + nt(node_hidden, node_second_wide) + bias_update).astype(BF16)
        if k == 0:
            turned = pltpu.roll(node_slope, latent, 1)
            pairs_land[pair_rows, :] = jnp.where(low_half, table.astype(F32), turned).astype(BF16)
            mine = pairs_land.at[pair_rows, :]
            for (step,) in far_first((n_x,)):
                send(mine, mine, 12, (phi, y_hi * n_x + x_of[step]))
            for x in x_of[::-1]:
                for side, slab_at in enumerate((above, below)):
                    send(mine, near_land.at[side, pair_rows, :], 13, (slab_at, y_hi * n_x + x))
            node_kept[0, 0, 0 : 2 * hits] = node_in
            node_kept[0, 1, 0 : 2 * hits] = node_hidden
            if n_x > 1:
                wait_bytes(pairs_land.at[pl.ds(0, (n_x - 1) * 2 * hits), :], recv_sem.at[12])
            gathered = in_order(pairs_land[...].astype(F32))
            table = jnp.where(low_half, gathered, 0.0).astype(BF16)
            first_slope = pltpu.roll(gathered, latent, 1)
        else:
            node_kept[1, 0] = node_in
            node_kept[1, 1] = node_hidden
            stores[1].start()

    for k in (1, 0):
        if k == 1:
            pre_back = nn(slab_land[...], node_second_under) * node_slope
        else:
            grad_low = grad_now.astype(BF16)
            pre_back = nn(grad_low, node_second_wide) * first_slope
        pre_low = pre_back.astype(BF16)
        in_back = nn(pre_low, node_first_wide)
        gm_part = nt(gm_back, pre_low)
        gm_part = jnp.concatenate(
            [
                gm_part[0:latent].astype(BF16),
                two_parts(gm_part[latent : 2 * latent] + gm_part[2 * latent :]),
            ],
            axis=0,
        )

        def column_at(at, sums):
            return jnp.where(lane == latent + at, jnp.sum(sums, axis=1, keepdims=True), 0.0)

        def node_terms():
            kept_rows = (
                pl.ds(pl.multiple_of(y_hi * hits, hits), hits) if k == 0 else own_rows
            )
            grad_kept[0] = pre_back
            grad_kept[1] = in_back
            if k == 0:
                grad_kept[2] = gained
                grad_mine = grad_own + grad_kept[2, own_rows, :]
            else:
                grad_mine = grad_own
            pre_mine = grad_kept[0, own_rows, :]
            pre_turned = nt(wide_pick, pre_mine.astype(BF16))
            grad_turned = nt(wide_pick, grad_mine.astype(BF16))
            return (
                nn(pre_turned.astype(BF16), node_kept[k, 0, kept_rows, :]),
                nn(grad_turned.astype(BF16), node_kept[k, 1, kept_rows, :])
                + column_at(2, pre_turned)
                + column_at(3, grad_turned),
                grad_mine + jnp.where(low_half, grad_kept[1, own_rows, :], 0.0),
            )

        if k == 1:
            bias_sums[...] = jnp.zeros_like(bias_sums)
        else:
            first_terms, second_terms, grad_own = node_terms()
            grads[2 * latent : 3 * latent, :] = grads[2 * latent : 3 * latent, :] + first_terms
            grads[3 * latent : 4 * latent, :] = grads[3 * latent : 4 * latent, :] + second_terms

        def folded(value):
            pieces = [
                value[:, at : at + LANES] for at in range(0, value.shape[1], LANES)
            ]
            return functools.reduce(lambda one, other: one + other, pieces)

        def edge_back(cols):
            both = nn(gm_part, onehot[slab : 2 * slab, cols])
            edge_grad = both[0:latent]
            hidden_grad = both[latent : 2 * latent] + both[2 * latent :]
            if k == 0:
                edge_grad = edge_grad + grad_edge[:, cols]
                hidden_grad = hidden_grad + second_grad_edge[:, cols]
            else:
                grad_edge[:, cols] = edge_grad
            pre_grad = hidden_grad * slopes[k, :, cols]
            bias_sums[0] = bias_sums[0] + folded(pre_grad)
            bias_sums[1] = bias_sums[1] + folded(edge_grad)
            pre_grad = pre_grad.astype(BF16)
            back_stack[0:latent, cols] = pre_grad
            back_stack[latent : 2 * latent, cols] = pre_grad
            back_stack[2 * latent : 3 * latent, cols] = edge_grad.astype(BF16)

        chunks(slots, edge_back)

        def weight_terms():
            outer = nt(back_stack[latent : 3 * latent, :], hidden_in[k])
            upper = outer[0:latent, 0:LANES]
            lower = jnp.where(low_half, outer[0:latent, LANES:], outer[latent:, LANES:])
            return upper, lower

        if k == 0:
            upper, lower = weight_terms()
            grads[0:latent, :] = grads[0:latent, :] + upper
            grads[latent : 2 * latent, :] = grads[latent : 2 * latent, :] + lower

        if k == 0:
            grads[3 * latent : 4 * latent, :] = (
                grads[3 * latent : 4 * latent, :]
                + column_at(0, bias_sums[0])
                + column_at(1, bias_sums[1])
            )
            for at, (device, spot) in enumerate(plane_peers):
                send(
                    grads.at[pl.ds(pl.multiple_of(spot * shard, shard), shard), :],
                    plane_land.at[pl.ds(at * shard, shard), :],
                    6,
                    device,
                )

        back_send[k] = nt(
            onehot[2 * slab : 2 * slab + 2 * rim, :], back_stack[0 : 2 * latent, :]
        ).astype(BF16)
        send(back_send.at[k, 0:rim], back_land.at[k, 0:rim], 7 + k, (below, layer))
        send(
            back_send.at[k, rim : 2 * rim],
            back_land.at[k, rim : 2 * rim],
            7 + k,
            (above, layer),
        )
        from_source = nt(onehot[0:slab, :], back_stack[0 : 2 * latent, :])
        from_target = nt(onehot[slab : 2 * slab, :], back_stack[0 : 2 * latent, :])
        if k == 0:
            wait_bytes(plane_land, recv_sem.at[6])
            total = grads[shard_rows, :]
            for turn in range(n_plane - 1):
                total = total + plane_land[turn * shard : (turn + 1) * shard, :]
            z_rows = pl.ds(pl.multiple_of(z_at * shard, shard), shard)
            z_land[z_rows, :] = total
            for peer in z_peers:
                send(z_land.at[z_rows, :], z_land.at[z_rows, :], 9, peer)
        wait_bytes(back_land.at[k], recv_sem.at[7 + k])
        from_source = (
            from_source
            + nn(rim_put[0], back_land[k, 0:rim])
            + nn(rim_put[1], back_land[k, rim : 2 * rim])
        )
        comb = jnp.where(low_half, from_source, from_target).astype(BF16)
        packed = nn(comb[0:half], first_back) + nn(comb[half:], first_back_high)
        if k == 1:
            swap(2, packed)
            upper, lower = weight_terms()
            first_terms, second_terms, grad_own = node_terms()
            grads[0:latent, :] = upper
            grads[latent : 2 * latent, :] = lower
            grads[2 * latent : 3 * latent, :] = first_terms
            grads[3 * latent : 4 * latent, :] = second_terms
            node_kept[1, 0] = table
            node_out[...] = node_kept[1, 0, own_rows, 0:latent]
            stores[0].start()

            def carried(cols):
                old = grad_edge[:, cols] + nn(self_back, back_stack[0:latent, cols])
                grad_edge[:, cols] = old
                second_grad_edge[:, cols] = nn(second_back, old.astype(BF16))

            chunks(slots, carried)
            cot_slab = pltpu.roll(slab_land[...].astype(F32), latent, 1)
            grad_before = jnp.where(low_half, cot_slab + in_back, 0.0)
            packed = swapped_sum(2)
            gained = jnp.concatenate(
                [
                    jnp.where(low_half, packed, 0.0),
                    jnp.where(low_half, pltpu.roll(packed, latent, 1), 0.0),
                ],
                axis=0,
            )
            grad_now = grad_before + gained
        else:
            comb_send[...] = packed.astype(BF16)

            def rows_of(device):
                return pl.ds(pl.multiple_of(lax.rem(device, n_layer // 2) * hits, hits), hits)

            for at, peer in enumerate(layer_peers):
                send(
                    comb_send.at[rows_of(peer), :],
                    comb_land.at[pl.ds(at * hits, hits), :],
                    10,
                    (phi, peer),
                )
            wait_bytes(z_land.at[pl.ds(0, (n_z - 1) * shard), :], recv_sem.at[9])
            total = z_land[0:shard, :]
            for turn in range(1, n_z):
                total = total + z_land[turn * shard : (turn + 1) * shard, :]
            shard_sum[...] = total
            for device, _ in plane_peers:
                send(shard_sum, sums_to.at[shard_rows, :], 11, device)
            stores[3].start()
            wait_bytes(comb_land, recv_sem.at[10])
            total = comb_send[rows_of(layer), :].astype(F32)
            for turn in range(n_layer - 1):
                total = total + comb_land[turn * hits : (turn + 1) * hits, :].astype(F32)
            total = jnp.where(layer < n_layer // 2, total, pltpu.roll(total, latent, 1))
            node_grad[...] = (grad_own + total)[:, 0:latent]
            stores[2].start()

    wait_bytes(slab_land.at[pl.ds(0, slab - hits), :], send_sem.at[0])
    wait_bytes(rim_send, send_sem.at[1])
    wait_bytes(rim_near, send_sem.at[2])
    wait_bytes(message_land.at[pl.ds(0, (n_layer - 1) * hits), :], send_sem.at[3])
    if n_x > 1:
        wait_bytes(pairs_land.at[pl.ds(0, (n_x - 1) * 2 * hits), :], send_sem.at[12])
    wait_bytes(near_land, send_sem.at[13])
    for k in range(2):
        wait_bytes(back_send.at[k], send_sem.at[7 + k])
    for at in range(1, 3):
        wait_bytes(swaps[at].at[pl.ds(0, (n_layer - 1) * half), :], send_sem.at[3 + at])
    wait_bytes(plane_land, send_sem.at[6])
    wait_bytes(z_land.at[pl.ds(0, (n_z - 1) * shard), :], send_sem.at[9])
    wait_bytes(comb_land, send_sem.at[10])
    wait_bytes(plane_land, send_sem.at[11])
    for store in stores:
        store.wait()
    wait_bytes(sums_to.at[pl.ds(0, (n_plane - 1) * shard), :], recv_sem.at[11])


def deliver(*refs):
    sources, targets, held, sums = refs[:4], refs[4:12], refs[12:20], refs[20]
    in_sem, out_sem = refs[21:]
    first, second, node_first, node_second, biases = held[3:]
    latent = second.shape[0]
    loads = [
        pltpu.make_async_copy(sources[at], dst, in_sem.at[at])
        for at, dst in enumerate((*held[:3], sums))
    ]
    stores = [
        pltpu.make_async_copy(held[at], targets[at], out_sem.at[at]) for at in range(8)
    ]
    for load in loads[::-1]:
        load.start()
    loads[3].wait()
    first[:, 0:LANES] = sums[0:latent, :]
    first[:, LANES:] = sums[latent : 2 * latent, 0:latent]
    second[...] = pltpu.roll(sums[latent : 2 * latent, :], latent, 1)[:, 0:latent]
    node_first[...] = sums[2 * latent : 3 * latent, :]
    node_second[...] = sums[3 * latent : 4 * latent, 0:latent]
    biases[...] = sums[3 * latent : 4 * latent, :].T[latent : latent + 4, :]
    for store in stores[3:]:
        store.start()
    for load, store in zip(loads[:3], stores):
        load.wait()
        store.start()
    for store in stores:
        store.wait()


def body(n_phi, n_layer, *arrays):
    node_feats, edge_feats, edge_source, edge_target, *others, node_cot = arrays
    latent, hits = node_feats.shape
    slots = edge_feats.shape[1]
    slab = hits * n_layer
    rim = others[1].shape[1]
    n_plane = Y_LO * CORES * n_layer
    n_z = n_phi // (Y_LO * CORES)
    grad_rows = 4 * latent
    shard = grad_rows // n_plane
    hbm = pl.BlockSpec(memory_space=pltpu.HBM)
    operands = (
        node_feats.T,
        edge_feats,
        edge_source.reshape(1, slots),
        edge_target.reshape(1, slots),
        *others,
        node_cot.T,
    )
    outs = [
        jax.ShapeDtypeStruct(*out)
        for out in (
            ((hits, latent), BF16),
            ((latent, slots), BF16),
            ((hits, latent), F32),
            ((latent, 3 * latent), F32),
            ((latent, latent), F32),
            ((latent, 2 * latent), F32),
            ((latent, latent), F32),
            ((4, latent), F32),
        )
    ]
    results = pl.pallas_call(
        functools.partial(kernel, n_phi, n_layer),
        out_shape=[*outs[:3], jax.ShapeDtypeStruct((grad_rows, LANES), F32)],
        in_specs=[hbm] * len(operands),
        out_specs=[hbm] * 4,
        scratch_shapes=[pltpu.VMEM(array.shape, array.dtype) for array in (*operands, *outs[:3])]
        + [
            pltpu.VMEM((2 * slab + 2 * rim, slots), BF16),
            pltpu.VMEM((2 * rim, slab), BF16),
            pltpu.VMEM((2, slab, rim), BF16),
            pltpu.VMEM((2, 4 * latent, slots), BF16),
            pltpu.VMEM((2, latent, slots), BF16),
            pltpu.VMEM((latent, slots), F32),
            pltpu.VMEM((2, latent, slots), F32),
            pltpu.VMEM((latent, slots), F32),
            pltpu.VMEM((latent, slots), F32),
            pltpu.VMEM((3 * latent, slots), BF16),
            pltpu.VMEM((2, latent, LANES), F32),
            pltpu.VMEM((2, 2, slab, LANES), BF16),
            pltpu.VMEM((3, slab, LANES), F32),
            pltpu.VMEM((hits, LANES), BF16),
            pltpu.VMEM((slab, LANES), BF16),
            pltpu.VMEM((slab, LANES), BF16),
            pltpu.VMEM((2, 1, rim), jnp.int32),
            pltpu.VMEM((2 * rim, slab), BF16),
            pltpu.VMEM((2, slab, LANES), BF16),
            pltpu.VMEM((slab, LANES), BF16),
            pltpu.VMEM((2 * rim, LANES), BF16),
            pltpu.VMEM((2, 2 * rim, LANES), BF16),
            pltpu.VMEM((slab // 2, LANES), F32),
            pltpu.VMEM((slab, LANES), F32),
            pltpu.VMEM((2, n_layer * slab // 2, LANES), BF16),
            pltpu.VMEM((2, 2 * rim, LANES), BF16),
            pltpu.VMEM((2, 2 * rim, LANES), BF16),
            pltpu.VMEM((slab // 2, LANES), BF16),
            pltpu.VMEM(((n_layer - 1) * hits, LANES), BF16),
            pltpu.VMEM((grad_rows, LANES), F32),
            pltpu.VMEM(((n_plane - 1) * shard, LANES), F32),
            pltpu.VMEM((n_z * shard, LANES), F32),
            pltpu.VMEM((shard, LANES), F32),
            pltpu.SemaphoreType.DMA((len(operands),)),
            pltpu.SemaphoreType.DMA((4,)),
            pltpu.SemaphoreType.REGULAR((3,)),
            pltpu.SemaphoreType.DMA((14,)),
            pltpu.SemaphoreType.DMA((14,)),
        ],
        compiler_params=pltpu.CompilerParams(
            collective_id=0, has_side_effects=True, vmem_limit_bytes=VMEM_BYTES
        ),
    )(*operands)
    node_out, edge_out, node_grad, *totals = pl.pallas_call(
        deliver,
        out_shape=outs,
        in_specs=[hbm] * 4,
        out_specs=[hbm] * len(outs),
        scratch_shapes=[pltpu.VMEM(out.shape, out.dtype) for out in outs]
        + [
            pltpu.VMEM((grad_rows, LANES), F32),
            pltpu.SemaphoreType.DMA((4,)),
            pltpu.SemaphoreType.DMA((len(outs),)),
        ],
        compiler_params=pltpu.CompilerParams(vmem_limit_bytes=VMEM_BYTES),
    )(*results)
    return node_out.T, edge_out, node_grad.T, *totals


def solution(mesh):
    split = P(None, ("phi", "layer"))
    return jax.shard_map(
        functools.partial(body, mesh.shape["phi"], mesh.shape["layer"]),
        mesh=mesh,
        in_specs=(
            split,
            split,
            P(("phi", "layer")),
            P(("phi", "layer")),
            P("phi", "layer"),
            P("phi", None),
            P("phi", None),
            P(),
            P(),
            P(),
            P(),
            P(),
            split,
        ),
        out_specs=(split, split, split, P(), P(), P(), P(), P()),
        check_vma=False,
    )
```
